32 devices in a mesh: row: 4 (over y, core), col: 8 (over z, x).
Axes of the slice: x: 2, y: 2, z: 4, core: 2. Of those that a mesh axis runs over, the one named last changes fastest.
Arguments:
- marginal: float32 [32768, 128], P(('row', 'col')), may hold values from -6 to 6
- penalty: float32 [128], replicated, may hold values from 0.5 to 8
- ld_diag: float32 [32, 1024, 1024], P(('row', 'col')), may hold values from -0.005 to 1, as said below
- ld_low: float32 [32, 2, 1024, 1024], P(('row', 'col')), may hold values from -0.006 to 0.36
- band: int32 [32], P(('row', 'col')), may hold values from 0 to 2
- genotypes: bfloat16 [1280, 32768], P(None, ('row', 'col')), may hold values from -5 to 5
Outputs:
- effects: float32 [32768, 128], P(('row', 'col'))
- scores: float32 [1280, 128], P(('row', 'col'))
The draws below stay inside these ranges and needn't reach their ends.
Inputs may be any that keep to these rules, and one draw needn't show every extreme that they name: Each block of ld_diag is symmetric with ones on its diagonal.
All inputs are finite; a program needn't handle non-finite values.
Results may differ from the reference program's by a relative error of at most 0.0023.
The reference program's roundings to bfloat16 on the way (of `rounded`) count: a program that leaves them out, or rounds other values in their place, can miss the bound.
Values sent between devices are 32-bit elements; how exact they have to be, the bound alone decides.
No kernel may reach another device: no remote copies, remote signals or barrier semaphores. Data moves between devices by JAX's collectives and lax.ppermute only.
A program may use at most 128 MiB of HBM per device.

```python
import math
import jax
import jax.numpy as jnp
from jax import lax

BS = 1024
K = 128
ITERS = 3
NB = 32
M = 32768
PEOPLE = 1280


def block_shape(key):
    lower_gap = 0.02
    upper_gap = 0.05
    fraction = jax.random.uniform(jax.random.fold_in(key, 11), (NB,), jnp.float32)
    gaps = jnp.exp(jnp.log(lower_gap) + fraction * (jnp.log(upper_gap) - jnp.log(lower_gap)))
    decays = 1.0 - gaps
    corner = jax.random.uniform(jax.random.fold_in(key, 12), (NB,), jnp.float32, 0.1, 0.35)
    return (decays, corner)


def draw_ld_diag(key, part):
    decays, corner = block_shape(key)
    positions = jnp.arange(BS, dtype=jnp.float32)
    distance = jnp.abs(positions[:, None] - positions[None, :])
    smooth = jnp.power(decays[:, None, None], distance[None, :, :])
    spread = jax.random.uniform(jax.random.fold_in(key, 21), (NB, BS, BS), jnp.float32, -1.0, 1.0)
    factor = 0.004
    symmetric = (spread + jnp.swapaxes(spread, 1, 2)) * (0.5 * factor)
    combined = smooth + symmetric
    return jnp.where(distance[None, :, :] < 0.5, jnp.float32(1.0), combined)


def draw_ld_low(key, part):
    decays, corner = block_shape(key)
    previous = jnp.roll(decays, 1)
    positions = jnp.arange(BS, dtype=jnp.float32)
    row_decay = jnp.power(decays[:, None], positions[None, :])
    col_decay = jnp.power(previous[:, None], (BS - positions)[None, :])
    coupled = corner[:, None, None] * row_decay[:, :, None] * col_decay[:, None, :]
    noise_one = jax.random.uniform(jax.random.fold_in(key, 31), (NB, BS, BS), jnp.float32, -0.003, 0.003)
    noise_two = jax.random.uniform(jax.random.fold_in(key, 32), (NB, BS, BS), jnp.float32, -0.006, 0.006)
    return jnp.stack([coupled + noise_one, noise_two], axis=1)


def place_ends(array, own_key, smallest, largest):
    index_at = [jax.random.randint(jax.random.fold_in(own_key, axis), (), 0, length) for axis, length in enumerate(array.shape)]
    main_axis = array.shape.index(max(array.shape))
    beside = index_at[:main_axis] + [(index_at[main_axis] + 1) % array.shape[main_axis]] + index_at[main_axis + 1:]
    return array.at[tuple(index_at)].set(smallest).at[tuple(beside)].set(largest)


def shard_levels(key, dims, shards, low, largest):
    def one(dim, shards_of):
        draws = jax.random.uniform(jax.random.fold_in(jax.random.fold_in(key, 6), dim), (shards_of,), jnp.float32, low / len(shards), largest / len(shards))
        return jnp.repeat(jnp.exp(draws), dims[dim] // shards_of).reshape((-1,) + (1,) * (len(dims) - dim - 1))

    level = one(*shards[0])
    for cut in shards[1:]:
        level = level * one(*cut)
    return level


def gaussian(rng, dims, scale, reach, split=(), kind=jnp.bfloat16):
    result = jax.random.normal(rng, dims, jnp.float32) * scale
    if len(split) > 0:
        result = shard_levels(rng, dims, split, -0.22, 0.18) * result
    return jnp.clip(result, min=-reach, max=reach).astype(kind)


def setup_inputs(seed: int = 0) -> dict:
    key_of = jax.random.split(jax.random.key(seed), 7)
    marginal = gaussian(key_of[0], (M, K), 1.0, 6.0, ((0, 32),), jnp.float32)
    penalty = jnp.clip(jnp.exp(jax.random.uniform(key_of[1], (K,), jnp.float32, math.log(0.5), math.log(8.0))), 0.5, 8.0)
    ld_diag = draw_ld_diag(jax.random.fold_in(key_of[6], 71), 0)
    ld_low = draw_ld_low(jax.random.fold_in(key_of[6], 71), 0)
    band = place_ends(jax.random.randint(key_of[4], (NB,), 0, 3), jax.random.fold_in(key_of[4], 1), 0, 2).astype(jnp.int32)
    genotypes = gaussian(key_of[5], (PEOPLE, M), 1.0, 5.0, ((1, 32),))
    return dict(marginal=marginal, penalty=penalty, ld_diag=ld_diag, ld_low=ld_low, band=band, genotypes=genotypes)


def apply_operator(vec, ld_diag, ld_low, band, penalty):
    hp = lax.Precision.HIGHEST
    out = jnp.einsum("nij,njk->nik", ld_diag, vec, precision=hp) + penalty * vec
    blocks = jnp.arange(NB)
    for dist in (1, 2):
        active = jnp.logical_and(band >= dist, blocks >= dist).astype(jnp.float32)
        tile = ld_low[:, dist - 1] * active[:, None, None]
        below = jnp.concatenate([jnp.zeros((dist, BS, K), jnp.float32), vec[:-dist]], axis=0)
        out = out + jnp.einsum("nij,njk->nik", tile, below, precision=hp)
        upper = jnp.einsum("nji,njk->nik", tile, vec, precision=hp)
        out = out + jnp.concatenate([upper[dist:], jnp.zeros((dist, BS, K), jnp.float32)], axis=0)
    return out


def reference(marginal, penalty, ld_diag, ld_low, band, genotypes):
    residual = marginal.reshape(NB, BS, K)
    direction = residual
    effects = jnp.zeros_like(residual)
    norm_now = jnp.sum(residual * residual, axis=(0, 1))
    for step in range(ITERS):
        image = apply_operator(direction, ld_diag, ld_low, band, penalty)
        alpha = norm_now / jnp.sum(direction * image, axis=(0, 1))
        effects = effects + alpha * direction
        residual = residual - alpha * image
        norm_next = jnp.sum(residual * residual, axis=(0, 1))
        direction = residual + (norm_next / norm_now) * direction
        norm_now = norm_next
    effects = effects.reshape(M, K)
    rounded = effects.astype(jnp.bfloat16)
    scores = jnp.dot(genotypes, rounded, preferred_element_type=jnp.float32)
    return effects, scores
```

```python
import jax
import jax.numpy as jnp
from jax import lax
from jax.experimental import pallas as pl
from jax.experimental.pallas import tpu as pltpu
from jax.sharding import PartitionSpec as P

AXES = ("row", "col")
F32 = jnp.float32
BF16 = jnp.bfloat16
MIB = 1024 * 1024
VMEM = pl.BlockSpec(memory_space=pltpu.VMEM)
SMEM = pl.BlockSpec(memory_space=pltpu.SMEM)


def params():
    return pltpu.CompilerParams(vmem_limit_bytes=40 * MIB)


def cost(flops, num_bytes):
    return pl.CostEstimate(flops=int(flops), bytes_accessed=int(num_bytes), transcendentals=0)


def shifted(block, distance):
    n = lax.axis_size(AXES)
    route = [(i - distance, i) for i in range(n) if 0 <= i - distance < n]
    return lax.ppermute(block, AXES, route)


def first_coupling_kernel(flags, vec, low, narrow, product):
    active = flags[pl.program_id(0)]
    tile = jnp.where(active > 0, low[0], 0.0).astype(BF16)
    narrow[0] = tile
    across = vec[...].T.astype(BF16)
    product[0] = jnp.dot(across, tile, preferred_element_type=F32).T


def first_coupling(flags, vec, low):
    count, size, _ = low.shape
    k = vec.shape[1]
    return pl.pallas_call(
        first_coupling_kernel,
        grid=(count,),
        in_specs=[
            SMEM,
            pl.BlockSpec((size, k), lambda d: (0, 0)),
            pl.BlockSpec((1, size, size), lambda d: (d, 0, 0)),
        ],
        out_specs=[
            pl.BlockSpec((1, size, size), lambda d: (d, 0, 0)),
            pl.BlockSpec((1, size, k), lambda d: (d, 0, 0)),
        ],
        out_shape=[
            jax.ShapeDtypeStruct(low.shape, BF16),
            jax.ShapeDtypeStruct((count, size, k), F32),
        ],
        compiler_params=params(),
        cost_estimate=cost(4 * size * size * k, 12 * size * size),
    )(flags, vec, low)


def coupling_kernel(vec, low, one, two):
    across = vec[...].T.astype(BF16)
    two[...] = jnp.dot(across, low[1], preferred_element_type=F32).T
    one[...] = jnp.dot(across, low[0], preferred_element_type=F32).T


def coupling(vec, low):
    size, k = vec.shape
    return pl.pallas_call(
        coupling_kernel,
        in_specs=[VMEM, VMEM],
        out_specs=[VMEM, VMEM],
        out_shape=[jax.ShapeDtypeStruct(vec.shape, F32)] * 2,
        compiler_params=params(),
        cost_estimate=cost(4 * size * size * k, 4 * size * size),
    )(vec, low)


def first_diag_kernel(vec, diag, narrow, product):
    tile = diag[...].astype(BF16)
    narrow[...] = tile
    product[...] = jnp.dot(tile, vec[...].astype(BF16), preferred_element_type=F32)


def first_diag(vec, diag):
    size, k = vec.shape
    rows = size // 4
    return pl.pallas_call(
        first_diag_kernel,
        grid=(4,),
        in_specs=[pl.BlockSpec((size, k), lambda r: (0, 0)), pl.BlockSpec((rows, size), lambda r: (r, 0))],
        out_specs=[pl.BlockSpec((rows, size), lambda r: (r, 0)), pl.BlockSpec((rows, k), lambda r: (r, 0))],
        out_shape=[jax.ShapeDtypeStruct(diag.shape, BF16), jax.ShapeDtypeStruct(vec.shape, F32)],
        compiler_params=params(),
        cost_estimate=cost(2 * size * size * k, 6 * size * size),
    )(vec, diag)


def diag_kernel(vec, diag, product):
    product[...] = jnp.dot(diag[...], vec[...].astype(BF16), preferred_element_type=F32)


def diag_times(vec, diag):
    size, k = vec.shape
    return pl.pallas_call(
        diag_kernel,
        in_specs=[VMEM, VMEM],
        out_specs=VMEM,
        out_shape=jax.ShapeDtypeStruct(vec.shape, F32),
        compiler_params=params(),
        cost_estimate=cost(2 * size * size * k, 2 * size * size),
    )(vec, diag)


def below_kernel(low, one, two, product):
    acc = jnp.dot(low[0], one[...].astype(BF16), preferred_element_type=F32)
    product[...] = acc + jnp.dot(low[1], two[...].astype(BF16), preferred_element_type=F32)


def below_times(low, one, two):
    size, k = one.shape
    return pl.pallas_call(
        below_kernel,
        in_specs=[VMEM] * 3,
        out_specs=VMEM,
        out_shape=jax.ShapeDtypeStruct(one.shape, F32),
        compiler_params=params(),
        cost_estimate=cost(4 * size * size * k, 4 * size * size),
    )(low, one, two)


def summed(values):
    n = lax.axis_size(AXES)
    spread = jnp.broadcast_to(values[None], (n,) + values.shape)
    return jnp.sum(lax.all_to_all(spread, AXES, 0, 0, tiled=True), axis=0)


def coefficients(moments, penalty):
    def inner(u, v):
        return sum(a * b * moments[i + j] for i, a in enumerate(u) for j, b in enumerate(v))

    n0 = moments[0]
    a0 = n0 / (moments[1] + penalty * n0)
    r1 = [1.0 - a0 * penalty, -a0]
    n1 = inner(r1, r1)
    b0 = n1 / n0
    d1 = [r1[0] + b0, r1[1]]
    ad1 = [penalty * d1[0], d1[0] + penalty * d1[1], d1[1]]
    a1 = n1 / inner(d1, ad1)
    e1 = [a0 + a1 * d1[0], a1 * d1[1]]
    r2 = [r1[0] - a1 * ad1[0], r1[1] - a1 * ad1[1], -a1 * ad1[2]]
    n2 = inner(r2, r2)
    b1 = n2 / n1
    d2 = [r2[0] + b1 * d1[0], r2[1] + b1 * d1[1], r2[2]]
    ad2 = [penalty * d2[0], d2[0] + penalty * d2[1], d2[1] + penalty * d2[2], d2[2]]
    a2 = n2 / inner(d2, ad2)
    return e1[0] + a2 * d2[0], e1[1] + a2 * d2[1], a2 * d2[2]


def body(marginal, penalty, ld_diag, ld_low, band, genotypes):
    position = lax.axis_index(AXES)
    flags = jnp.stack([jnp.logical_and(band[0] >= d, position >= d) for d in (1, 2)]).astype(jnp.int32)

    v0 = marginal
    behind = [shifted(v0, d) for d in (1, 2)]
    low, products = first_coupling(flags, v0, ld_low[0])
    ahead = [shifted(products[d - 1], -d) for d in (1, 2)]
    diag, own = first_diag(v0, ld_diag[0])
    v1 = own + below_times(low, *behind) + ahead[0] + ahead[1]

    behind = [shifted(v1, d) for d in (1, 2)]
    one, two = coupling(v1, low)
    ahead = [shifted(two, -2), shifted(one, -1)]
    own = diag_times(v1, diag)
    v2 = own + below_times(low, *behind) + ahead[0] + ahead[1]

    behind = [shifted(v2, d) for d in (1, 2)]
    half = diag_times(v2, diag) + 2.0 * below_times(low, *behind)
    pairs = [(v0, v0), (v0, v1), (v1, v1), (v1, v2), (v2, v2), (v2, half)]
    moments = summed(jnp.stack([jnp.sum(a * b, axis=0) for a, b in pairs]))
    c0, c1, c2 = coefficients(moments, penalty)
    effects = c0 * v0 + c1 * v1 + c2 * v2
    rounded = effects.astype(BF16)
    partial = jnp.dot(genotypes, rounded, preferred_element_type=F32)
    n = lax.axis_size(AXES)
    pieces = lax.all_to_all(partial.reshape((n, -1) + partial.shape[1:]), AXES, 0, 0, tiled=True)
    return effects, jnp.sum(pieces, axis=0)


def solution(mesh):
    placed = (
        P(AXES, None),
        P(),
        P(AXES, None, None),
        P(AXES, None, None, None),
        P(AXES),
        P(None, AXES),
    )
    return jax.shard_map(
        body,
        mesh=mesh,
        in_specs=placed,
        out_specs=(P(AXES, None), P(AXES, None)),
        check_vma=False,
    )
```

```python
import jax
import jax.numpy as jnp
from jax import lax
from jax.experimental import pallas as pl
from jax.experimental.pallas import tpu as pltpu
from jax.sharding import PartitionSpec as P

AXES = ("row", "col")
F32 = jnp.float32
BF16 = jnp.bfloat16
MIB = 1024 * 1024
VMEM = pl.BlockSpec(memory_space=pltpu.VMEM)
SMEM = pl.BlockSpec(memory_space=pltpu.SMEM)


def params():
    return pltpu.CompilerParams(vmem_limit_bytes=40 * MIB)


def cost(flops, num_bytes):
    return pl.CostEstimate(flops=int(flops), bytes_accessed=int(num_bytes), transcendentals=0)


def shifted(block, distance):
    n = lax.axis_size(AXES)
    route = [(i - distance, i) for i in range(n) if 0 <= i - distance < n]
    return lax.ppermute(block, AXES, route)


def first_coupling_kernel(flags, vec, low, narrow, product):
    active = flags[pl.program_id(0)]
    tile = jnp.where(active > 0, low[0], 0.0).astype(BF16)
    narrow[0] = tile
    across = vec[...].T.astype(BF16)
    product[0] = jnp.dot(across, tile, preferred_element_type=F32).T


def first_coupling(flags, vec, low):
    count, size, _ = low.shape
    k = vec.shape[1]
    return pl.pallas_call(
        first_coupling_kernel,
        grid=(count,),
        in_specs=[
            SMEM,
            pl.BlockSpec((size, k), lambda d: (0, 0)),
            pl.BlockSpec((1, size, size), lambda d: (d, 0, 0)),
        ],
        out_specs=[
            pl.BlockSpec((1, size, size), lambda d: (d, 0, 0)),
            pl.BlockSpec((1, size, k), lambda d: (d, 0, 0)),
        ],
        out_shape=[
            jax.ShapeDtypeStruct(low.shape, BF16),
            jax.ShapeDtypeStruct((count, size, k), F32),
        ],
        compiler_params=params(),
        cost_estimate=cost(4 * size * size * k, 12 * size * size),
    )(flags, vec, low)


def coupling_kernel(vec, low, one, two):
    across = vec[...].T.astype(BF16)
    two[...] = jnp.dot(across, low[1], preferred_element_type=F32).T
    one[...] = jnp.dot(across, low[0], preferred_element_type=F32).T


def coupling(vec, low):
    size, k = vec.shape
    return pl.pallas_call(
        coupling_kernel,
        in_specs=[VMEM, VMEM],
        out_specs=[VMEM, VMEM],
        out_shape=[jax.ShapeDtypeStruct(vec.shape, F32)] * 2,
        compiler_params=params(),
        cost_estimate=cost(4 * size * size * k, 4 * size * size),
    )(vec, low)


def first_diag_kernel(vec, diag, narrow, product):
    tile = diag[...].astype(BF16)
    narrow[...] = tile
    product[...] = jnp.dot(tile, vec[...].astype(BF16), preferred_element_type=F32)


def first_diag(vec, diag):
    size, k = vec.shape
    rows = size // 4
    return pl.pallas_call(
        first_diag_kernel,
        grid=(4,),
        in_specs=[pl.BlockSpec((size, k), lambda r: (0, 0)), pl.BlockSpec((rows, size), lambda r: (r, 0))],
        out_specs=[pl.BlockSpec((rows, size), lambda r: (r, 0)), pl.BlockSpec((rows, k), lambda r: (r, 0))],
        out_shape=[jax.ShapeDtypeStruct(diag.shape, BF16), jax.ShapeDtypeStruct(vec.shape, F32)],
        compiler_params=params(),
        cost_estimate=cost(2 * size * size * k, 6 * size * size),
    )(vec, diag)


def diag_kernel(vec, diag, product):
    product[...] = jnp.dot(diag[...], vec[...].astype(BF16), preferred_element_type=F32)


def diag_times(vec, diag):
    size, k = vec.shape
    return pl.pallas_call(
        diag_kernel,
        in_specs=[VMEM, VMEM],
        out_specs=VMEM,
        out_shape=jax.ShapeDtypeStruct(vec.shape, F32),
        compiler_params=params(),
        cost_estimate=cost(2 * size * size * k, 2 * size * size),
    )(vec, diag)


def middle_kernel(vec, diag, low, two, product):
    acc = jnp.dot(diag[...], vec[...].astype(BF16), preferred_element_type=F32)
    product[...] = acc + jnp.dot(low[1], two[...].astype(BF16), preferred_element_type=F32)


def middle(vec, diag, low, two):
    size, k = vec.shape
    return pl.pallas_call(
        middle_kernel,
        in_specs=[VMEM] * 4,
        out_specs=VMEM,
        out_shape=jax.ShapeDtypeStruct(vec.shape, F32),
        compiler_params=params(),
        cost_estimate=cost(4 * size * size * k, 4 * size * size),
    )(vec, diag, low, two)


def finish_kernel(odd, part, low, from_even, from_odd, ahead, ahead_pair, out):
    one = jnp.where(odd[0] > 0, from_even[...], from_odd[...])
    acc = jnp.dot(low[0], one.astype(BF16), preferred_element_type=F32)
    out[...] = acc + part[...] + ahead[...] + jnp.where(odd[0] > 0, 0.0, ahead_pair[...])


def finish(odd, part, low, from_even, from_odd, ahead, ahead_pair):
    size, k = part.shape
    return pl.pallas_call(
        finish_kernel,
        in_specs=[SMEM] + [VMEM] * 6,
        out_specs=VMEM,
        out_shape=jax.ShapeDtypeStruct(part.shape, F32),
        compiler_params=params(),
        cost_estimate=cost(2 * size * size * k, 2 * size * size),
    )(odd, part, low, from_even, from_odd, ahead, ahead_pair)


def last_kernel(odd, part, low, from_even, from_odd, v0, v1, v2, own, moments):
    one = jnp.where(odd[0] > 0, from_even[...], from_odd[...])
    half = own[...] + 2.0 * (part[...] + jnp.dot(low[0], one.astype(BF16), preferred_element_type=F32))
    pairs = [(v0, v0), (v0, v1), (v1, v1), (v1, v2), (v2, v2)]
    for row, (a, b) in enumerate(pairs):
        moments[row : row + 1] = jnp.sum(a[...] * b[...], axis=0, keepdims=True)
    moments[5:6] = jnp.sum(v2[...] * half, axis=0, keepdims=True)
    moments[6:8] = jnp.zeros_like(moments[6:8])


def last(odd, part, low, from_even, from_odd, v0, v1, v2, own):
    size, k = part.shape
    return pl.pallas_call(
        last_kernel,
        in_specs=[SMEM] + [VMEM] * 8,
        out_specs=VMEM,
        out_shape=jax.ShapeDtypeStruct((8, k), F32),
        compiler_params=params(),
        cost_estimate=cost(2 * size * size * k, 2 * size * size),
    )(odd, part, low, from_even, from_odd, v0, v1, v2, own)


def two_kernel(low, two, product):
    product[...] = jnp.dot(low[1], two[...].astype(BF16), preferred_element_type=F32)


def two_times(low, two):
    size, k = two.shape
    return pl.pallas_call(
        two_kernel,
        in_specs=[VMEM, VMEM],
        out_specs=VMEM,
        out_shape=jax.ShapeDtypeStruct(two.shape, F32),
        compiler_params=params(),
        cost_estimate=cost(2 * size * size * k, 2 * size * size),
    )(low, two)


def tail_kernel(pieces, penalty, v0, v1, v2, genotypes, effects, partial):
    sums = pieces[0]
    for piece in range(1, pieces.shape[0]):
        sums = sums + pieces[piece]
    moments = [sums[row : row + 1] for row in range(6)]
    c0, c1, c2 = coefficients(moments, penalty[...])
    value = c0 * v0[...] + c1 * v1[...] + c2 * v2[...]
    effects[...] = value
    partial[...] = jnp.dot(genotypes[...], value.astype(BF16), preferred_element_type=F32)


def tail(pieces, penalty, v0, v1, v2, genotypes):
    people, size = genotypes.shape
    k = v0.shape[1]
    return pl.pallas_call(
        tail_kernel,
        in_specs=[VMEM] * 6,
        out_specs=[VMEM, VMEM],
        out_shape=[jax.ShapeDtypeStruct(v0.shape, F32), jax.ShapeDtypeStruct((people, k), F32)],
        compiler_params=params(),
        cost_estimate=cost(2 * people * size * k, 2 * people * size),
    )(pieces, penalty, v0, v1, v2, genotypes)


def spread_over(values, axis):
    n = lax.axis_size(axis)
    return lax.all_to_all(jnp.broadcast_to(values[None], (n,) + values.shape), axis, 0, 0, tiled=True)


def scattered_over(values, axis):
    n = lax.axis_size(axis)
    pieces = values.reshape((n, values.shape[0] // n) + values.shape[1:])
    return jnp.sum(lax.all_to_all(pieces, axis, 0, 0, tiled=True), axis=0)


def routed(block, pairs):
    return lax.ppermute(block, AXES, pairs)


def coefficients(moments, penalty):
    def inner(u, v):
        return sum(a * b * moments[i + j] for i, a in enumerate(u) for j, b in enumerate(v))

    n0 = moments[0]
    a0 = n0 / (moments[1] + penalty * n0)
    r1 = [1.0 - a0 * penalty, -a0]
    n1 = inner(r1, r1)
    b0 = n1 / n0
    d1 = [r1[0] + b0, r1[1]]
    ad1 = [penalty * d1[0], d1[0] + penalty * d1[1], d1[1]]
    a1 = n1 / inner(d1, ad1)
    e1 = [a0 + a1 * d1[0], a1 * d1[1]]
    r2 = [r1[0] - a1 * ad1[0], r1[1] - a1 * ad1[1], -a1 * ad1[2]]
    n2 = inner(r2, r2)
    b1 = n2 / n1
    d2 = [r2[0] + b1 * d1[0], r2[1] + b1 * d1[1], r2[2]]
    ad2 = [penalty * d2[0], d2[0] + penalty * d2[1], d2[1] + penalty * d2[2], d2[2]]
    a2 = n2 / inner(d2, ad2)
    return e1[0] + a2 * d2[0], e1[1] + a2 * d2[1], a2 * d2[2]


def body(marginal, penalty, ld_diag, ld_low, band, genotypes):
    n = lax.axis_size(AXES)
    position = lax.axis_index(AXES)
    flags = jnp.stack([jnp.logical_and(band[0] >= d, position >= d) for d in (1, 2)]).astype(jnp.int32)
    odd = (position % 2).astype(jnp.int32)[None]
    even_to_odd = [(i, i + 1) for i in range(0, n, 2)]
    odd_to_even = [(i + 1, i) for i in range(0, n, 2)]

    def behind(vec):
        two = shifted(vec, 2)
        return two, routed(vec, even_to_odd), routed(two, odd_to_even)

    def ahead(one, two):
        pair = routed(one, even_to_odd + odd_to_even)
        return shifted(two + jnp.where(odd[0] > 0, pair, 0.0), -2), pair

    v0 = marginal
    low, products = first_coupling(flags, v0, ld_low[0])
    v0, products = lax.optimization_barrier((v0, products))
    up, up_pair = ahead(products[0], products[1])
    two, from_even, from_odd = behind(v0)
    diag, own = first_diag(v0, ld_diag[0])
    part = own + two_times(low, two)
    v1 = finish(odd, part, low, from_even, from_odd, up, up_pair)

    two, from_even, from_odd = behind(v1)
    up, up_pair = ahead(*coupling(v1, low))
    part = middle(v1, diag, low, two)
    v2 = finish(odd, part, low, from_even, from_odd, up, up_pair)

    two, from_even, from_odd = behind(v2)
    own = diag_times(v2, diag)
    moments = last(odd, two_times(low, two), low, from_even, from_odd, v0, v1, v2, own)
    moments = jnp.sum(spread_over(moments, "row"), axis=0)
    pieces = spread_over(moments, "col")
    effects, partial = tail(pieces, penalty[None], v0, v1, v2, genotypes)
    return effects, scattered_over(scattered_over(partial, "row"), "col")


def solution(mesh):
    placed = (
        P(AXES, None),
        P(),
        P(AXES, None, None),
        P(AXES, None, None, None),
        P(AXES),
        P(None, AXES),
    )
    return jax.shard_map(
        body,
        mesh=mesh,
        in_specs=placed,
        out_specs=(P(AXES, None), P(AXES, None)),
        check_vma=False,
    )
```

```python
import functools

import jax
import jax.numpy as jnp
from jax import lax
from jax.experimental import pallas as pl
from jax.experimental.pallas import tpu as pltpu
from jax.sharding import PartitionSpec as P

AXES = ("row", "col")
F32 = jnp.float32
BF16 = jnp.bfloat16
MIB = 1024 * 1024
VMEM = pl.BlockSpec(memory_space=pltpu.VMEM)
SMEM = pl.BlockSpec(memory_space=pltpu.SMEM)


def params(mib=32):
    return pltpu.CompilerParams(vmem_limit_bytes=mib * MIB)


def cost(flops, num_bytes):
    return pl.CostEstimate(flops=int(flops), bytes_accessed=int(num_bytes), transcendentals=0)


def shifted(block, distance):
    n = lax.axis_size(AXES)
    route = [(i - distance, i) for i in range(n) if 0 <= i - distance < n]
    return lax.ppermute(block, AXES, route)


def first_coupling_kernel(flags, vec, low, narrow, product):
    active = flags[pl.program_id(1)]
    tile = jnp.where(active > 0, low[0], 0.0).astype(BF16)
    narrow[0] = tile
    across = vec[...].T.astype(BF16)
    product[0] = jnp.dot(across, tile, preferred_element_type=F32).T


def first_coupling(flags, vec, low):
    count, size, _ = low.shape
    k = vec.shape[1]
    parts = 4
    wide = size // parts
    return pl.pallas_call(
        first_coupling_kernel,
        grid=(parts, count),
        in_specs=[
            SMEM,
            pl.BlockSpec((size, k), lambda c, d: (0, 0)),
            pl.BlockSpec((1, size, wide), lambda c, d: (d, 0, c)),
        ],
        out_specs=[
            pl.BlockSpec((1, size, wide), lambda c, d: (d, 0, c)),
            pl.BlockSpec((1, wide, k), lambda c, d: (d, c, 0)),
        ],
        out_shape=[
            jax.ShapeDtypeStruct(low.shape, BF16),
            jax.ShapeDtypeStruct((count, size, k), F32),
        ],
        compiler_params=params(56),
        cost_estimate=cost(4 * size * size * k, 12 * size * size),
    )(flags, vec, low)


def coupling_kernel(vec, low, product):
    across = vec[...].T.astype(BF16)
    for d in range(2):
        product[d] = jnp.dot(across, low[d], preferred_element_type=F32).T


def coupling(vec, low):
    size, k = vec.shape
    return pl.pallas_call(
        coupling_kernel,
        in_specs=[VMEM, VMEM],
        out_specs=VMEM,
        out_shape=jax.ShapeDtypeStruct((2, size, k), F32),
        compiler_params=params(),
        cost_estimate=cost(4 * size * size * k, 4 * size * size),
    )(vec, low)


def first_diag_kernel(vec, diag, narrow, product):
    tile = diag[...].astype(BF16)
    narrow[...] = tile
    product[...] = jnp.dot(tile, vec[...].astype(BF16), preferred_element_type=F32)


def first_diag(vec, diag):
    size, k = vec.shape
    rows = size // 4
    return pl.pallas_call(
        first_diag_kernel,
        grid=(4,),
        in_specs=[pl.BlockSpec((size, k), lambda r: (0, 0)), pl.BlockSpec((rows, size), lambda r: (r, 0))],
        out_specs=[pl.BlockSpec((rows, size), lambda r: (r, 0)), pl.BlockSpec((rows, k), lambda r: (r, 0))],
        out_shape=[jax.ShapeDtypeStruct(diag.shape, BF16), jax.ShapeDtypeStruct(vec.shape, F32)],
        compiler_params=params(),
        cost_estimate=cost(2 * size * size * k, 6 * size * size),
    )(vec, diag)


def diag_kernel(vec, diag, product):
    product[...] = jnp.dot(diag[...], vec[...].astype(BF16), preferred_element_type=F32)


def diag_times(vec, diag):
    size, k = vec.shape
    return pl.pallas_call(
        diag_kernel,
        in_specs=[VMEM, VMEM],
        out_specs=VMEM,
        out_shape=jax.ShapeDtypeStruct(vec.shape, F32),
        compiler_params=params(),
        cost_estimate=cost(2 * size * size * k, 2 * size * size),
    )(vec, diag)


def finish_kernel(odd, own, part, low, from_even, from_odd, ahead_a, ahead_b, pair_a, pair_b, out):
    one = jnp.where(odd[0] > 0, from_even[...], from_odd[...])
    acc = jnp.dot(low[0], one.astype(BF16), preferred_element_type=F32) + own[...] + part[...]
    half = ahead_a.shape[0]
    for place, (straight, pair) in enumerate(((ahead_a, pair_a), (ahead_b, pair_b))):
        rows = slice(place * half, (place + 1) * half)
        out[rows] = acc[rows] + straight[...] + jnp.where(odd[0] > 0, 0.0, pair[...])


def finish(odd, own, part, low, from_even, from_odd, ahead_a, ahead_b, pair_a, pair_b):
    size, k = part.shape
    return pl.pallas_call(
        finish_kernel,
        in_specs=[SMEM] + [VMEM] * 9,
        out_specs=VMEM,
        out_shape=jax.ShapeDtypeStruct(part.shape, F32),
        compiler_params=params(),
        cost_estimate=cost(2 * size * size * k, 2 * size * size),
    )(odd, own, part, low, from_even, from_odd, ahead_a, ahead_b, pair_a, pair_b)


def last_kernel(low, one, two, v0, v1, v2, own, moments):
    below = jnp.dot(low[0], one[...].astype(BF16), preferred_element_type=F32)
    below = below + jnp.dot(low[1], two[...].astype(BF16), preferred_element_type=F32)
    pairs = [(v0, v0), (v0, v1), (v1, v1), (v1, v2), (v2, v2)]
    for row, (a, b) in enumerate(pairs):
        moments[row : row + 1] = jnp.sum(a[...] * b[...], axis=0, keepdims=True)
    moments[5:6] = jnp.sum(v2[...] * (own[...] + 2.0 * below), axis=0, keepdims=True)
    moments[6:8] = jnp.zeros_like(moments[6:8])


def last(low, one, two, v0, v1, v2, own):
    size, k = v0.shape
    return pl.pallas_call(
        last_kernel,
        in_specs=[VMEM] * 7,
        out_specs=VMEM,
        out_shape=jax.ShapeDtypeStruct((8, k), F32),
        compiler_params=params(),
        cost_estimate=cost(4 * size * size * k, 4 * size * size),
    )(low, one, two, v0, v1, v2, own)


def two_kernel(low, two, product):
    product[...] = jnp.dot(low[1], two[...].astype(BF16), preferred_element_type=F32)


def two_times(low, two):
    size, k = two.shape
    return pl.pallas_call(
        two_kernel,
        in_specs=[VMEM, VMEM],
        out_specs=VMEM,
        out_shape=jax.ShapeDtypeStruct(two.shape, F32),
        compiler_params=params(),
        cost_estimate=cost(2 * size * size * k, 2 * size * size),
    )(low, two)


def group_rows(genotypes, groups, group):
    rows = genotypes.shape[0] // groups
    return genotypes[pl.ds(pl.multiple_of(group * rows, rows), rows)]


def send_kernel(groups, row, sums, penalty, v0, v1, v2, genotypes, effects, rounded, send):
    moments = [sums[m : m + 1] for m in range(6)]
    c0, c1, c2 = coefficients(moments, penalty[...])
    value = c0 * v0[...] + c1 * v1[...] + c2 * v2[...]
    effects[...] = value
    narrow = value.astype(BF16)
    rounded[...] = narrow
    other = 1 - row[0] % 2
    for g in range(groups // 2):
        send[g] = jnp.dot(group_rows(genotypes, groups, 2 * g + other), narrow, preferred_element_type=F32)


def keep_kernel(groups, row, rounded, genotypes, keep):
    mine = row[0] % 2
    for g in range(groups // 2):
        keep[g] = jnp.dot(group_rows(genotypes, groups, 2 * g + mine), rounded[...], preferred_element_type=F32)


def partial_scores(row, groups, sums, penalty, v0, v1, v2, genotypes):
    people, size = genotypes.shape
    k = v0.shape[1]
    half = jax.ShapeDtypeStruct((groups // 2, people // groups, k), F32)
    effects, rounded, send = pl.pallas_call(
        functools.partial(send_kernel, groups),
        in_specs=[SMEM] + [VMEM] * 6,
        out_specs=[VMEM] * 3,
        out_shape=[jax.ShapeDtypeStruct(v0.shape, F32), jax.ShapeDtypeStruct(v0.shape, BF16), half],
        compiler_params=params(),
        cost_estimate=cost(people * size * k, 2 * people * size),
    )(row, sums, penalty, v0, v1, v2, genotypes)
    keep = pl.pallas_call(
        functools.partial(keep_kernel, groups),
        in_specs=[SMEM, VMEM, VMEM],
        out_specs=VMEM,
        out_shape=half,
        compiler_params=params(),
        cost_estimate=cost(people * size * k, 2 * people * size),
    )(row, rounded, genotypes)
    return effects, send, keep


def scattered_over(values, axis):
    n = lax.axis_size(axis)
    pieces = values.reshape((n, values.shape[0] // n) + values.shape[1:])
    return jnp.sum(lax.all_to_all(pieces, axis, 0, 0, tiled=True), axis=0)


def routed(block, pairs):
    return lax.ppermute(block, AXES, pairs)


def coefficients(moments, penalty):
    def inner(u, v):
        return sum(a * b * moments[i + j] for i, a in enumerate(u) for j, b in enumerate(v))

    n0 = moments[0]
    a0 = n0 / (moments[1] + penalty * n0)
    r1 = [1.0 - a0 * penalty, -a0]
    n1 = inner(r1, r1)
    b0 = n1 / n0
    d1 = [r1[0] + b0, r1[1]]
    ad1 = [penalty * d1[0], d1[0] + penalty * d1[1], d1[1]]
    a1 = n1 / inner(d1, ad1)
    e1 = [a0 + a1 * d1[0], a1 * d1[1]]
    r2 = [r1[0] - a1 * ad1[0], r1[1] - a1 * ad1[1], -a1 * ad1[2]]
    n2 = inner(r2, r2)
    b1 = n2 / n1
    d2 = [r2[0] + b1 * d1[0], r2[1] + b1 * d1[1], r2[2]]
    ad2 = [penalty * d2[0], d2[0] + penalty * d2[1], d2[1] + penalty * d2[2], d2[2]]
    a2 = n2 / inner(d2, ad2)
    return e1[0] + a2 * d2[0], e1[1] + a2 * d2[1], a2 * d2[2]


def swapped(block, bit):
    return routed(block, [(i, i ^ bit) for i in range(lax.axis_size(AXES))])


def body(marginal, penalty, ld_diag, ld_low, band, genotypes):
    n = lax.axis_size(AXES)
    rows, cols = lax.axis_size("row"), lax.axis_size("col")
    position = lax.axis_index(AXES)
    row = lax.axis_index("row")
    flags = jnp.stack([jnp.logical_and(band[0] >= d, position >= d) for d in (1, 2)]).astype(jnp.int32)
    odd = (position % 2).astype(jnp.int32)[None]
    even_to_odd = [(i, i + 1) for i in range(0, n, 2)]
    odd_to_even = [(i + 1, i) for i in range(0, n, 2)]
    half = marginal.shape[0] // 2

    def halos(vec, two, products):
        pairs, ups = [], []
        for part in range(2):
            one = products[0, part * half : (part + 1) * half]
            pairs.append(routed(one, even_to_odd + odd_to_even))
        for part in range(2):
            far = products[1, part * half : (part + 1) * half]
            ups.append(shifted(far + jnp.where(odd[0] > 0, pairs[part], 0.0), -2))
        vec, pairs[0] = lax.optimization_barrier((vec, pairs[0]))
        from_even = routed(vec, even_to_odd)
        from_odd = routed(two, odd_to_even)
        return from_even, from_odd, *ups, *pairs

    v0 = marginal
    two = shifted(v0, 2)
    low, products = first_coupling(flags, v0, ld_low[0])
    parts = halos(v0, two, products)
    diag, own = first_diag(v0, ld_diag[0])
    v1 = finish(odd, own, two_times(low, two), low, *parts)

    two = shifted(v1, 2)
    parts = halos(v1, two, coupling(v1, low))
    v2 = finish(odd, diag_times(v1, diag), two_times(low, two), low, *parts)

    one, two = shifted(v2, 1), shifted(v2, 2)
    sums = last(low, one, two, v0, v1, v2, diag_times(v2, diag))
    bit = 1
    while bit < n:
        sums = sums + swapped(sums, bit)
        bit *= 2

    effects, send, keep = partial_scores(row.astype(jnp.int32)[None], rows, sums, penalty[None], v0, v1, v2, genotypes)
    total = keep + swapped(send, cols)
    bit = rows // 4
    while bit:
        mine = (row // (2 * bit)) % 2
        total = total.reshape((2, -1) + total.shape[1:])
        send = lax.dynamic_index_in_dim(total, 1 - mine, 0, keepdims=False)
        total = lax.dynamic_index_in_dim(total, mine, 0, keepdims=False) + swapped(send, 2 * bit * cols)
        bit //= 2
    return effects, scattered_over(total[0], "col")


def solution(mesh):
    placed = (
        P(AXES, None),
        P(),
        P(AXES, None, None),
        P(AXES, None, None, None),
        P(AXES),
        P(None, AXES),
    )
    return jax.shard_map(
        body,
        mesh=mesh,
        in_specs=placed,
        out_specs=(P(AXES, None), P(AXES, None)),
        check_vma=False,
    )
```

```python
import functools

import jax
import jax.numpy as jnp
from jax import lax
from jax.experimental import pallas as pl
from jax.experimental.pallas import tpu as pltpu
from jax.sharding import PartitionSpec as P

AXES = ("row", "col")
F32 = jnp.float32
BF16 = jnp.bfloat16
MIB = 1024 * 1024
VMEM = pl.BlockSpec(memory_space=pltpu.VMEM)
SMEM = pl.BlockSpec(memory_space=pltpu.SMEM)


def params(mib=32):
    return pltpu.CompilerParams(vmem_limit_bytes=mib * MIB)


def cost(flops, num_bytes):
    return pl.CostEstimate(flops=int(flops), bytes_accessed=int(num_bytes), transcendentals=0)


def shifted(block, distance):
    n = lax.axis_size(AXES)
    route = [(i - distance, i) for i in range(n) if 0 <= i - distance < n]
    return lax.ppermute(block, AXES, route)


def split_store(value, first, second):
    half = first.shape[0]
    first[...] = value[:half]
    second[...] = value[half:]


def first_coupling_kernel(flags, vec, low, narrow, one_a, one_b, far_a, far_b, tiles, arrived):
    count, size = narrow.shape[0], narrow.shape[1]
    chunks = tiles.shape[0] // count
    rows = size // chunks
    copies = []
    for d in range(count):
        for c in range(chunks):
            place = d * chunks + c
            copies.append(pltpu.make_async_copy(low.at[d, pl.ds(c * rows, rows)], tiles.at[place], arrived.at[place]))
            copies[-1].start()
    across = vec[...].T.astype(BF16)
    for d, (first, second) in enumerate(((one_a, one_b), (far_a, far_b))):
        acc = None
        for c in range(chunks):
            place = d * chunks + c
            copies[place].wait()
            tile = jnp.where(flags[d] > 0, tiles[place], 0.0).astype(BF16)
            narrow[d, c * rows : (c + 1) * rows] = tile
            term = jnp.dot(across[:, c * rows : (c + 1) * rows], tile, preferred_element_type=F32)
            acc = term if acc is None else acc + term
        split_store(acc.T, first, second)


def first_coupling(flags, vec, low):
    count, size, _ = low.shape
    k = vec.shape[1]
    chunks = 4
    return pl.pallas_call(
        first_coupling_kernel,
        in_specs=[SMEM, VMEM, pl.BlockSpec(memory_space=pltpu.HBM)],
        out_specs=[VMEM] * 5,
        out_shape=[jax.ShapeDtypeStruct(low.shape, BF16)] + [jax.ShapeDtypeStruct((size // 2, k), F32)] * 4,
        scratch_shapes=[
            pltpu.VMEM((count * chunks, size // chunks, size), F32),
            pltpu.SemaphoreType.DMA((count * chunks,)),
        ],
        compiler_params=params(46),
        cost_estimate=cost(4 * size * size * k, 12 * size * size),
    )(flags, vec, low)


def coupling_kernel(vec, low, one_a, one_b, far_a, far_b):
    across = vec[...].T.astype(BF16)
    split_store(jnp.dot(across, low[0], preferred_element_type=F32).T, one_a, one_b)
    split_store(jnp.dot(across, low[1], preferred_element_type=F32).T, far_a, far_b)


def coupling(vec, low):
    size, k = vec.shape
    return pl.pallas_call(
        coupling_kernel,
        in_specs=[VMEM, VMEM],
        out_specs=[VMEM] * 4,
        out_shape=[jax.ShapeDtypeStruct((size // 2, k), F32)] * 4,
        compiler_params=params(),
        cost_estimate=cost(4 * size * size * k, 4 * size * size),
    )(vec, low)


def relay_kernel(odd, far, pair, after, out):
    out[...] = far[...] + jnp.where(odd[0] > 0, pair[...], 0.0)


def choose_kernel(odd, vec, two, after, out):
    out[...] = jnp.where(odd[0] > 0, two[...], vec[...])


def small(kernel, odd, left, right, after):
    return pl.pallas_call(
        kernel,
        in_specs=[SMEM, VMEM, VMEM, pl.BlockSpec(memory_space=pl.ANY)],
        out_specs=VMEM,
        out_shape=jax.ShapeDtypeStruct(left.shape, F32),
        compiler_params=params(),
        cost_estimate=cost(left.size, 12 * left.size),
    )(odd, left, right, after)


def first_diag_kernel(vec, diag, narrow, product):
    tile = diag[...].astype(BF16)
    narrow[...] = tile
    product[...] = jnp.dot(tile, vec[...].astype(BF16), preferred_element_type=F32)


def first_diag(vec, diag):
    size, k = vec.shape
    rows = size // 4
    return pl.pallas_call(
        first_diag_kernel,
        grid=(4,),
        in_specs=[pl.BlockSpec((size, k), lambda r: (0, 0)), pl.BlockSpec((rows, size), lambda r: (r, 0))],
        out_specs=[pl.BlockSpec((rows, size), lambda r: (r, 0)), pl.BlockSpec((rows, k), lambda r: (r, 0))],
        out_shape=[jax.ShapeDtypeStruct(diag.shape, BF16), jax.ShapeDtypeStruct(vec.shape, F32)],
        compiler_params=params(),
        cost_estimate=cost(2 * size * size * k, 6 * size * size),
    )(vec, diag)


def diag_kernel(vec, diag, product):
    product[...] = jnp.dot(diag[...], vec[...].astype(BF16), preferred_element_type=F32)


def diag_times(vec, diag):
    size, k = vec.shape
    return pl.pallas_call(
        diag_kernel,
        in_specs=[VMEM, VMEM],
        out_specs=VMEM,
        out_shape=jax.ShapeDtypeStruct(vec.shape, F32),
        compiler_params=params(),
        cost_estimate=cost(2 * size * size * k, 2 * size * size),
    )(vec, diag)


def finish_kernel(odd, part, low, one, ahead_a, ahead_b, pair_a, pair_b, out):
    acc = jnp.dot(low[0], one[...].astype(BF16), preferred_element_type=F32) + part[...]
    half = ahead_a.shape[0]
    for place, (straight, pair) in enumerate(((ahead_a, pair_a), (ahead_b, pair_b))):
        rows = slice(place * half, (place + 1) * half)
        out[rows] = acc[rows] + straight[...] + jnp.where(odd[0] > 0, 0.0, pair[...])


def finish(odd, part, low, one, ahead_a, ahead_b, pair_a, pair_b):
    size, k = part.shape
    return pl.pallas_call(
        finish_kernel,
        in_specs=[SMEM] + [VMEM] * 7,
        out_specs=VMEM,
        out_shape=jax.ShapeDtypeStruct(part.shape, F32),
        compiler_params=params(),
        cost_estimate=cost(2 * size * size * k, 2 * size * size),
    )(odd, part, low, one, ahead_a, ahead_b, pair_a, pair_b)


def two_kernel(own, low, two, product):
    product[...] = own[...] + jnp.dot(low[1], two[...].astype(BF16), preferred_element_type=F32)


def add_two(own, low, two):
    size, k = two.shape
    return pl.pallas_call(
        two_kernel,
        in_specs=[VMEM] * 3,
        out_specs=VMEM,
        out_shape=jax.ShapeDtypeStruct(two.shape, F32),
        compiler_params=params(),
        cost_estimate=cost(2 * size * size * k, 2 * size * size),
    )(own, low, two)


def most_kernel(low, one_a, two_a, two_b, v0, v1, v2, own, part, moments):
    half = one_a.shape[0]
    below = jnp.dot(low[0, :, :half], one_a[...].astype(BF16), preferred_element_type=F32)
    below = below + jnp.dot(low[1, :, :half], two_a[...].astype(BF16), preferred_element_type=F32)
    below = below + jnp.dot(low[1, :, half:], two_b[...].astype(BF16), preferred_element_type=F32)
    part[...] = own[...] + 2.0 * below
    pairs = [(v0, v0), (v0, v1), (v1, v1), (v1, v2), (v2, v2)]
    for row, (a, b) in enumerate(pairs):
        moments[row : row + 1] = jnp.sum(a[...] * b[...], axis=0, keepdims=True)
    moments[5:8] = jnp.zeros_like(moments[5:8])


def last_kernel(low, one_b, v2, part, moments, out):
    half = one_b.shape[0]
    image = part[...] + 2.0 * jnp.dot(low[0, :, half:], one_b[...].astype(BF16), preferred_element_type=F32)
    out[...] = moments[...]
    out[5:6] = jnp.sum(v2[...] * image, axis=0, keepdims=True)


def most(low, one_a, two_a, two_b, v0, v1, v2, own):
    size, k = v0.shape
    return pl.pallas_call(
        most_kernel,
        in_specs=[VMEM] * 8,
        out_specs=[VMEM] * 2,
        out_shape=[jax.ShapeDtypeStruct(v0.shape, F32), jax.ShapeDtypeStruct((8, k), F32)],
        compiler_params=params(),
        cost_estimate=cost(3 * size * size * k, 3 * size * size),
    )(low, one_a, two_a, two_b, v0, v1, v2, own)


def last(low, one_b, v2, part, moments):
    size, k = v2.shape
    return pl.pallas_call(
        last_kernel,
        in_specs=[VMEM] * 5,
        out_specs=VMEM,
        out_shape=jax.ShapeDtypeStruct((8, k), F32),
        compiler_params=params(),
        cost_estimate=cost(size * size * k, size * size),
    )(low, one_b, v2, part, moments)


def group_rows(genotypes, groups, group):
    rows = genotypes.shape[0] // groups
    return genotypes[pl.ds(pl.multiple_of(group * rows, rows), rows)]


def send_kernel(groups, row, pieces, penalty, v0, v1, v2, genotypes, effects, rounded, send):
    sums = pieces[0]
    for piece in range(1, pieces.shape[0]):
        sums = sums + pieces[piece]
    moments = [sums[m : m + 1] for m in range(6)]
    c0, c1, c2 = coefficients(moments, penalty[...])
    value = c0 * v0[...] + c1 * v1[...] + c2 * v2[...]
    effects[...] = value
    narrow = value.astype(BF16)
    rounded[...] = narrow
    other = 1 - row[0] % 2
    for g in range(groups // 2):
        send[g] = jnp.dot(group_rows(genotypes, groups, 2 * g + other), narrow, preferred_element_type=F32)


def keep_kernel(groups, row, rounded, genotypes, keep):
    mine = row[0] % 2
    for g in range(groups // 2):
        keep[g] = jnp.dot(group_rows(genotypes, groups, 2 * g + mine), rounded[...], preferred_element_type=F32)


def partial_scores(row, groups, pieces, penalty, v0, v1, v2, genotypes):
    people, size = genotypes.shape
    k = v0.shape[1]
    half = jax.ShapeDtypeStruct((groups // 2, people // groups, k), F32)
    effects, rounded, send = pl.pallas_call(
        functools.partial(send_kernel, groups),
        in_specs=[SMEM] + [VMEM] * 6,
        out_specs=[VMEM] * 3,
        out_shape=[jax.ShapeDtypeStruct(v0.shape, F32), jax.ShapeDtypeStruct(v0.shape, BF16), half],
        compiler_params=params(),
        cost_estimate=cost(people * size * k, 2 * people * size),
    )(row, pieces, penalty, v0, v1, v2, genotypes)
    keep = pl.pallas_call(
        functools.partial(keep_kernel, groups),
        in_specs=[SMEM, VMEM, VMEM],
        out_specs=VMEM,
        out_shape=half,
        compiler_params=params(),
        cost_estimate=cost(people * size * k, 2 * people * size),
    )(row, rounded, genotypes)
    return effects, send, keep


def scattered_over(values, axis):
    n = lax.axis_size(axis)
    pieces = values.reshape((n, values.shape[0] // n) + values.shape[1:])
    return jnp.sum(lax.all_to_all(pieces, axis, 0, 0, tiled=True), axis=0)


def routed(block, pairs):
    return lax.ppermute(block, AXES, pairs)


def coefficients(moments, penalty):
    def inner(u, v):
        return sum(a * b * moments[i + j] for i, a in enumerate(u) for j, b in enumerate(v))

    n0 = moments[0]
    a0 = n0 / (moments[1] + penalty * n0)
    r1 = [1.0 - a0 * penalty, -a0]
    n1 = inner(r1, r1)
    b0 = n1 / n0
    d1 = [r1[0] + b0, r1[1]]
    ad1 = [penalty * d1[0], d1[0] + penalty * d1[1], d1[1]]
    a1 = n1 / inner(d1, ad1)
    e1 = [a0 + a1 * d1[0], a1 * d1[1]]
    r2 = [r1[0] - a1 * ad1[0], r1[1] - a1 * ad1[1], -a1 * ad1[2]]
    n2 = inner(r2, r2)
    b1 = n2 / n1
    d2 = [r2[0] + b1 * d1[0], r2[1] + b1 * d1[1], r2[2]]
    ad2 = [penalty * d2[0], d2[0] + penalty * d2[1], d2[1] + penalty * d2[2], d2[2]]
    a2 = n2 / inner(d2, ad2)
    return e1[0] + a2 * d2[0], e1[1] + a2 * d2[1], a2 * d2[2]


def swapped(block, bit):
    return routed(block, [(i, i ^ bit) for i in range(lax.axis_size(AXES))])


def body(marginal, penalty, ld_diag, ld_low, band, genotypes):
    n = lax.axis_size(AXES)
    rows, cols = lax.axis_size("row"), lax.axis_size("col")
    position = lax.axis_index(AXES)
    row = lax.axis_index("row")
    flags = jnp.stack([jnp.logical_and(band[0] >= d, position >= d) for d in (1, 2)]).astype(jnp.int32)
    odd = (position % 2).astype(jnp.int32)[None]
    half = marginal.shape[0] // 2

    def halos(vec, two, products):
        one_a, one_b, far_a, far_b = products
        pair_a, pair_b = swapped(one_a, 1), swapped(one_b, 1)
        sum_a = small(relay_kernel, odd, far_a, pair_a, far_b)
        up_a = shifted(sum_a, -2)
        chosen = small(choose_kernel, odd, vec, two, sum_a)
        one = swapped(chosen, 1)
        up_b = shifted(small(relay_kernel, odd, far_b, pair_b, chosen), -2)
        return one, up_a, up_b, pair_a, pair_b

    v0 = marginal
    two = shifted(v0, 2)
    low, *products = first_coupling(flags, v0, ld_low[0])
    parts = halos(v0, two, products)
    diag, own = first_diag(v0, ld_diag[0])
    v1 = finish(odd, add_two(own, low, two), low, *parts)

    two = shifted(v1, 2)
    parts = halos(v1, two, coupling(v1, low))
    v2 = finish(odd, add_two(diag_times(v1, diag), low, two), low, *parts)

    ones, twos = [], []
    for part in (v2[:half], v2[half:]):
        twos.append(shifted(part, 2))
        ones.append(swapped(small(choose_kernel, odd, part, twos[-1], part), 1))
    part, moments = most(low, ones[0], *twos, v0, v1, v2, diag_times(v2, diag))
    moments = last(low, ones[1], v2, part, moments)
    pieces = lax.all_to_all(jnp.broadcast_to(moments[None], (n,) + moments.shape), AXES, 0, 0, tiled=True)

    effects, send, keep = partial_scores(row.astype(jnp.int32)[None], rows, pieces, penalty[None], v0, v1, v2, genotypes)
    received = swapped(send, cols)
    bit = rows // 4
    while bit:
        mine = (row // (2 * bit)) % 2
        keep = keep.reshape((2, -1) + keep.shape[1:])
        received = received.reshape((2, -1) + received.shape[1:])

        def chosen(index):
            return lax.dynamic_index_in_dim(keep, index, 0, False) + lax.dynamic_index_in_dim(received, index, 0, False)

        keep, received = chosen(mine), swapped(chosen(1 - mine), 2 * bit * cols)
        bit //= 2
    return effects, scattered_over((keep + received)[0], "col")


def solution(mesh):
    placed = (
        P(AXES, None),
        P(),
        P(AXES, None, None),
        P(AXES, None, None, None),
        P(AXES),
        P(None, AXES),
    )
    return jax.shard_map(
        body,
        mesh=mesh,
        in_specs=placed,
        out_specs=(P(AXES, None), P(AXES, None)),
        check_vma=False,
    )
```

```python
import functools

import jax
import jax.numpy as jnp
from jax import lax
from jax.experimental import pallas as pl
from jax.experimental.pallas import tpu as pltpu
from jax.sharding import PartitionSpec as P

AXES = ("row", "col")
F32 = jnp.float32
BF16 = jnp.bfloat16
MIB = 1024 * 1024
VMEM = pl.BlockSpec(memory_space=pltpu.VMEM)
SMEM = pl.BlockSpec(memory_space=pltpu.SMEM)


def params(mib=20):
    return pltpu.CompilerParams(vmem_limit_bytes=mib * MIB)


def cost(flops, num_bytes):
    return pl.CostEstimate(flops=int(flops), bytes_accessed=int(num_bytes), transcendentals=0)


def shifted(block, distance):
    n = lax.axis_size(AXES)
    route = [(i - distance, i) for i in range(n) if 0 <= i - distance < n]
    return lax.ppermute(block, AXES, route)


def split_store(value, first, second):
    half = first.shape[0]
    first[...] = value[:half]
    second[...] = value[half:]


def first_coupling_kernel(d, flags, vec, low, narrow, first, second, tiles, own, arrived):
    size = narrow.shape[0]
    chunks = tiles.shape[0]
    rows = size // chunks
    fetch = pltpu.make_async_copy(vec, own, arrived.at[chunks])
    fetch.start()
    copies = []
    for c in range(chunks):
        copies.append(pltpu.make_async_copy(low.at[d, pl.ds(c * rows, rows)], tiles.at[c], arrived.at[c]))
        copies[-1].start()
    fetch.wait()
    across = own[...].T.astype(BF16)
    acc = None
    for c in range(chunks):
        copies[c].wait()
        tile = jnp.where(flags[d] > 0, tiles[c], 0.0).astype(BF16)
        narrow[c * rows : (c + 1) * rows] = tile
        term = jnp.dot(across[:, c * rows : (c + 1) * rows], tile, preferred_element_type=F32)
        acc = term if acc is None else acc + term
    split_store(acc.T, first, second)


def first_coupling(d, flags, vec, low):
    size, k = vec.shape
    chunks = 4
    return pl.pallas_call(
        functools.partial(first_coupling_kernel, d),
        in_specs=[SMEM] + [pl.BlockSpec(memory_space=pltpu.HBM)] * 2,
        out_specs=[VMEM] * 3,
        out_shape=[jax.ShapeDtypeStruct((size, size), BF16)] + [jax.ShapeDtypeStruct((size // 2, k), F32)] * 2,
        scratch_shapes=[
            pltpu.VMEM((chunks, size // chunks, size), F32),
            pltpu.VMEM((size, k), F32),
            pltpu.SemaphoreType.DMA((chunks + 1,)),
        ],
        compiler_params=params(48),
        cost_estimate=cost(2 * size * size * k, 6 * size * size),
    )(flags, vec, low)


def coupling_kernel(vec, low, first, second):
    across = vec[...].T.astype(BF16)
    split_store(jnp.dot(across, low[...], preferred_element_type=F32).T, first, second)


def coupling(vec, low):
    size, k = vec.shape
    return pl.pallas_call(
        coupling_kernel,
        in_specs=[VMEM, VMEM],
        out_specs=[VMEM] * 2,
        out_shape=[jax.ShapeDtypeStruct((size // 2, k), F32)] * 2,
        compiler_params=params(),
        cost_estimate=cost(2 * size * size * k, 2 * size * size),
    )(vec, low)


def relay_kernel(odd, far, pair, after, out):
    out[...] = far[...] + jnp.where(odd[0] > 0, pair[...], 0.0)


def choose_kernel(odd, vec, two, after, first, second):
    split_store(jnp.where(odd[0] > 0, two[...], vec[...]), first, second)


def choose(odd, vec, two, after):
    size, k = vec.shape
    return pl.pallas_call(
        choose_kernel,
        in_specs=[SMEM, VMEM, VMEM, pl.BlockSpec(memory_space=pl.ANY)],
        out_specs=[VMEM] * 2,
        out_shape=[jax.ShapeDtypeStruct((size // 2, k), F32)] * 2,
        compiler_params=params(),
        cost_estimate=cost(vec.size, 12 * vec.size),
    )(odd, vec, two, after)


def choose_part_kernel(odd, vec, two, after, out):
    out[...] = jnp.where(odd[0] > 0, two[...], vec[...])


def small(kernel, odd, left, right, after):
    return pl.pallas_call(
        kernel,
        in_specs=[SMEM, VMEM, VMEM, pl.BlockSpec(memory_space=pl.ANY)],
        out_specs=VMEM,
        out_shape=jax.ShapeDtypeStruct(left.shape, F32),
        compiler_params=params(),
        cost_estimate=cost(left.size, 12 * left.size),
    )(odd, left, right, after)


def first_diag_kernel(vec, diag, narrow, product):
    tile = diag[...].astype(BF16)
    narrow[...] = tile
    product[...] = jnp.dot(tile, vec[...].astype(BF16), preferred_element_type=F32)


def first_diag(vec, diag):
    size, k = vec.shape
    rows = size // 4
    return pl.pallas_call(
        first_diag_kernel,
        grid=(4,),
        in_specs=[pl.BlockSpec((size, k), lambda r: (0, 0)), pl.BlockSpec((rows, size), lambda r: (r, 0))],
        out_specs=[pl.BlockSpec((rows, size), lambda r: (r, 0)), pl.BlockSpec((rows, k), lambda r: (r, 0))],
        out_shape=[jax.ShapeDtypeStruct(diag.shape, BF16), jax.ShapeDtypeStruct(vec.shape, F32)],
        compiler_params=params(),
        cost_estimate=cost(2 * size * size * k, 6 * size * size),
    )(vec, diag)


def diag_kernel(vec, diag, product):
    product[...] = jnp.dot(diag[...], vec[...].astype(BF16), preferred_element_type=F32)


def diag_times(vec, diag):
    size, k = vec.shape
    return pl.pallas_call(
        diag_kernel,
        in_specs=[VMEM, VMEM],
        out_specs=VMEM,
        out_shape=jax.ShapeDtypeStruct(vec.shape, F32),
        compiler_params=params(),
        cost_estimate=cost(2 * size * size * k, 2 * size * size),
    )(vec, diag)


def finish_kernel(odd, part, low, one_a, one_b, ahead_a, ahead_b, pair_a, pair_b, out):
    half = ahead_a.shape[0]
    acc = jnp.dot(low[:, :half], one_a[...].astype(BF16), preferred_element_type=F32) + part[...]
    acc = acc + jnp.dot(low[:, half:], one_b[...].astype(BF16), preferred_element_type=F32)
    for place, (straight, pair) in enumerate(((ahead_a, pair_a), (ahead_b, pair_b))):
        rows = slice(place * half, (place + 1) * half)
        out[rows] = acc[rows] + straight[...] + jnp.where(odd[0] > 0, 0.0, pair[...])


def finish(odd, part, low, one_a, one_b, ahead_a, ahead_b, pair_a, pair_b):
    size, k = part.shape
    return pl.pallas_call(
        finish_kernel,
        in_specs=[SMEM] + [VMEM] * 8,
        out_specs=VMEM,
        out_shape=jax.ShapeDtypeStruct(part.shape, F32),
        compiler_params=params(),
        cost_estimate=cost(2 * size * size * k, 2 * size * size),
    )(odd, part, low, one_a, one_b, ahead_a, ahead_b, pair_a, pair_b)


def two_kernel(own, low, two, product):
    product[...] = own[...] + jnp.dot(low[...], two[...].astype(BF16), preferred_element_type=F32)


def add_two(own, low, two):
    size, k = two.shape
    return pl.pallas_call(
        two_kernel,
        in_specs=[VMEM] * 3,
        out_specs=VMEM,
        out_shape=jax.ShapeDtypeStruct(two.shape, F32),
        compiler_params=params(),
        cost_estimate=cost(2 * size * size * k, 2 * size * size),
    )(own, low, two)


def most_kernel(low_one, low_two, one_a, two_a, two_b, v0, v1, v2, own, part, moments):
    half = one_a.shape[0]
    below = jnp.dot(low_one[:, :half], one_a[...].astype(BF16), preferred_element_type=F32)
    below = below + jnp.dot(low_two[:, :half], two_a[...].astype(BF16), preferred_element_type=F32)
    below = below + jnp.dot(low_two[:, half:], two_b[...].astype(BF16), preferred_element_type=F32)
    part[...] = own[...] + 2.0 * below
    pairs = [(v0, v0), (v0, v1), (v1, v1), (v1, v2), (v2, v2)]
    for row, (a, b) in enumerate(pairs):
        moments[row : row + 1] = jnp.sum(a[...] * b[...], axis=0, keepdims=True)
    moments[5:8] = jnp.zeros_like(moments[5:8])


def last_kernel(low, one_b, v2, part, moments, out):
    half = one_b.shape[0]
    image = part[...] + 2.0 * jnp.dot(low[:, half:], one_b[...].astype(BF16), preferred_element_type=F32)
    out[...] = moments[...]
    out[5:6] = jnp.sum(v2[...] * image, axis=0, keepdims=True)


def most(low_one, low_two, one_a, two_a, two_b, v0, v1, v2, own):
    size, k = v0.shape
    return pl.pallas_call(
        most_kernel,
        in_specs=[VMEM] * 9,
        out_specs=[VMEM] * 2,
        out_shape=[jax.ShapeDtypeStruct(v0.shape, F32), jax.ShapeDtypeStruct((8, k), F32)],
        compiler_params=params(),
        cost_estimate=cost(3 * size * size * k, 3 * size * size),
    )(low_one, low_two, one_a, two_a, two_b, v0, v1, v2, own)


def last(low, one_b, v2, part, moments):
    size, k = v2.shape
    return pl.pallas_call(
        last_kernel,
        in_specs=[VMEM] * 5,
        out_specs=VMEM,
        out_shape=jax.ShapeDtypeStruct((8, k), F32),
        compiler_params=params(),
        cost_estimate=cost(size * size * k, size * size),
    )(low, one_b, v2, part, moments)


def group_rows(genotypes, groups, group):
    rows = genotypes.shape[0] // groups
    return genotypes[pl.ds(pl.multiple_of(group * rows, rows), rows)]


def send_kernel(groups, row, pieces, penalty, v0, v1, v2, genotypes, effects, rounded, send):
    sums = pieces[0]
    for piece in range(1, pieces.shape[0]):
        sums = sums + pieces[piece]
    moments = [sums[m : m + 1] for m in range(6)]
    c0, c1, c2 = coefficients(moments, penalty[...])
    value = c0 * v0[...] + c1 * v1[...] + c2 * v2[...]
    effects[...] = value
    narrow = value.astype(BF16)
    rounded[...] = narrow
    other = 1 - row[0] % 2
    for g in range(groups // 2):
        send[g] = jnp.dot(group_rows(genotypes, groups, 2 * g + other), narrow, preferred_element_type=F32)


def keep_kernel(groups, row, rounded, genotypes, keep):
    mine = row[0] % 2
    for g in range(groups // 2):
        keep[g] = jnp.dot(group_rows(genotypes, groups, 2 * g + mine), rounded[...], preferred_element_type=F32)


def partial_scores(row, groups, pieces, penalty, v0, v1, v2, genotypes):
    people, size = genotypes.shape
    k = v0.shape[1]
    half = jax.ShapeDtypeStruct((groups // 2, people // groups, k), F32)
    effects, rounded, send = pl.pallas_call(
        functools.partial(send_kernel, groups),
        in_specs=[SMEM] + [VMEM] * 6,
        out_specs=[VMEM] * 3,
        out_shape=[jax.ShapeDtypeStruct(v0.shape, F32), jax.ShapeDtypeStruct(v0.shape, BF16), half],
        compiler_params=params(),
        cost_estimate=cost(people * size * k, 2 * people * size),
    )(row, pieces, penalty, v0, v1, v2, genotypes)
    keep = pl.pallas_call(
        functools.partial(keep_kernel, groups),
        in_specs=[SMEM, VMEM, VMEM],
        out_specs=VMEM,
        out_shape=half,
        compiler_params=params(),
        cost_estimate=cost(people * size * k, 2 * people * size),
    )(row, rounded, genotypes)
    return effects, send, keep


def pick_kernel(index, keep, received, mine, other):
    mine[...] = keep[index[0]] + received[index[0]]
    other[...] = keep[1 - index[0]] + received[1 - index[0]]


def pick(index, keep, received):
    half = jax.ShapeDtypeStruct(keep.shape[1:], F32)
    return pl.pallas_call(
        pick_kernel,
        in_specs=[SMEM, VMEM, VMEM],
        out_specs=[VMEM] * 2,
        out_shape=[half] * 2,
        compiler_params=params(),
        cost_estimate=cost(keep.size, 12 * keep.size),
    )(index, keep, received)


def scattered_over(values, axis):
    n = lax.axis_size(axis)
    pieces = values.reshape((n, values.shape[0] // n) + values.shape[1:])
    return jnp.sum(lax.all_to_all(pieces, axis, 0, 0, tiled=True), axis=0)


def routed(block, pairs):
    return lax.ppermute(block, AXES, pairs)


def coefficients(moments, penalty):
    def inner(u, v):
        return sum(a * b * moments[i + j] for i, a in enumerate(u) for j, b in enumerate(v))

    n0 = moments[0]
    a0 = n0 / (moments[1] + penalty * n0)
    r1 = [1.0 - a0 * penalty, -a0]
    n1 = inner(r1, r1)
    b0 = n1 / n0
    d1 = [r1[0] + b0, r1[1]]
    ad1 = [penalty * d1[0], d1[0] + penalty * d1[1], d1[1]]
    a1 = n1 / inner(d1, ad1)
    e1 = [a0 + a1 * d1[0], a1 * d1[1]]
    r2 = [r1[0] - a1 * ad1[0], r1[1] - a1 * ad1[1], -a1 * ad1[2]]
    n2 = inner(r2, r2)
    b1 = n2 / n1
    d2 = [r2[0] + b1 * d1[0], r2[1] + b1 * d1[1], r2[2]]
    ad2 = [penalty * d2[0], d2[0] + penalty * d2[1], d2[1] + penalty * d2[2], d2[2]]
    a2 = n2 / inner(d2, ad2)
    return e1[0] + a2 * d2[0], e1[1] + a2 * d2[1], a2 * d2[2]


def swapped(block, bit):
    return routed(block, [(i, i ^ bit) for i in range(lax.axis_size(AXES))])


def body(marginal, penalty, ld_diag, ld_low, band, genotypes):
    n = lax.axis_size(AXES)
    rows, cols = lax.axis_size("row"), lax.axis_size("col")
    position = lax.axis_index(AXES)
    row = lax.axis_index("row")
    flags = jnp.stack([jnp.logical_and(band[0] >= d, position >= d) for d in (1, 2)]).astype(jnp.int32)
    odd = (position % 2).astype(jnp.int32)[None]
    half = marginal.shape[0] // 2

    def halos(vec, first, second):
        one_a, one_b = first(vec)
        pair_a, pair_b = swapped(one_a, 1), swapped(one_b, 1)
        vec, one_b = lax.optimization_barrier((vec, one_b))
        two = shifted(vec, 2)
        far_a, far_b = second(vec)
        sum_a = small(relay_kernel, odd, far_a, pair_a, far_b)
        up_a = shifted(sum_a, -2)
        sum_b = small(relay_kernel, odd, far_b, pair_b, sum_a)
        up_b = shifted(sum_b, -2)
        chosen_a, chosen_b = choose(odd, vec, two, sum_b)
        return two, (swapped(chosen_a, 1), swapped(chosen_b, 1), up_a, up_b, pair_a, pair_b)

    v0 = marginal
    lows = [None, None]

    def from_start(d):
        def run(vec):
            lows[d], first, second = first_coupling(d, flags, vec, ld_low[0])
            return first, second

        return run

    two, parts = halos(v0, from_start(0), from_start(1))
    low_one, low_two = lows
    diag, own = first_diag(v0, ld_diag[0])
    v1 = finish(odd, add_two(own, low_two, two), low_one, *parts)

    two, parts = halos(v1, lambda vec: coupling(vec, low_one), lambda vec: coupling(vec, low_two))
    v2 = finish(odd, add_two(diag_times(v1, diag), low_two, two), low_one, *parts)

    ones, twos = [], []
    for part in (v2[:half], v2[half:]):
        twos.append(shifted(part, 2))
        ones.append(swapped(small(choose_part_kernel, odd, part, twos[-1], part), 1))
    part, moments = most(low_one, low_two, ones[0], *twos, v0, v1, v2, diag_times(v2, diag))
    moments = last(low_one, ones[1], v2, part, moments)
    pieces = lax.all_to_all(jnp.broadcast_to(moments[None], (n,) + moments.shape), AXES, 0, 0, tiled=True)

    effects, send, keep = partial_scores(row.astype(jnp.int32)[None], rows, pieces, penalty[None], v0, v1, v2, genotypes)
    received = swapped(send, cols)
    bit = rows // 4
    while bit:
        mine = (row // (2 * bit)) % 2
        keep = keep.reshape((2, -1) + keep.shape[1:])
        received = received.reshape((2, -1) + received.shape[1:])

        keep, send = pick(mine.astype(jnp.int32)[None], keep, received)
        received = swapped(send, 2 * bit * cols)
        bit //= 2
    return effects, scattered_over((keep + received)[0], "col")


def solution(mesh):
    placed = (
        P(AXES, None),
        P(),
        P(AXES, None, None),
        P(AXES, None, None, None),
        P(AXES),
        P(None, AXES),
    )
    return jax.shard_map(
        body,
        mesh=mesh,
        in_specs=placed,
        out_specs=(P(AXES, None), P(AXES, None)),
        check_vma=False,
    )
```

```python
import functools

import jax
import jax.numpy as jnp
from jax import lax
from jax.experimental import pallas as pl
from jax.experimental.pallas import tpu as pltpu
from jax.sharding import PartitionSpec as P

AXES = ("row", "col")
F32 = jnp.float32
BF16 = jnp.bfloat16
MIB = 1024 * 1024
VMEM = pl.BlockSpec(memory_space=pltpu.VMEM)
SMEM = pl.BlockSpec(memory_space=pltpu.SMEM)


def params(mib=20):
    return pltpu.CompilerParams(vmem_limit_bytes=mib * MIB)


def cost(flops, num_bytes):
    return pl.CostEstimate(flops=int(flops), bytes_accessed=int(num_bytes), transcendentals=0)


def shifted(block, distance):
    n = lax.axis_size(AXES)
    route = [(i - distance, i) for i in range(n) if 0 <= i - distance < n]
    return lax.ppermute(block, AXES, route)


def split_store(value, first, second):
    half = first.shape[0]
    first[...] = value[:half]
    second[...] = value[half:]


def first_coupling_kernel(flags, vec, low, own, low_one, low_two, one, one_a, one_b, far, tiles, arrived):
    size = own.shape[0]
    chunks = tiles.shape[0] // 2
    rows = size // chunks
    fetch = pltpu.make_async_copy(vec, own, arrived.at[2 * chunks])
    fetch.start()
    copies = []
    for place in range(2 * chunks):
        d, c = place // chunks, place % chunks
        copies.append(pltpu.make_async_copy(low.at[d, pl.ds(c * rows, rows)], tiles.at[place], arrived.at[place]))
        copies[-1].start()
    fetch.wait()
    across = own[...].T.astype(BF16)
    for d, narrow in enumerate((low_one, low_two)):
        acc = None
        for c in range(chunks):
            place = d * chunks + c
            copies[place].wait()
            tile = jnp.where(flags[d] > 0, tiles[place], 0.0).astype(BF16)
            narrow[c * rows : (c + 1) * rows] = tile
            term = jnp.dot(across[:, c * rows : (c + 1) * rows], tile, preferred_element_type=F32)
            acc = term if acc is None else acc + term
        if d == 0:
            one[...] = acc.T
            split_store(one[...], one_a, one_b)
        else:
            far[...] = acc.T


def first_coupling(flags, vec, low):
    size, k = vec.shape
    chunks = 4
    whole, half = jax.ShapeDtypeStruct((size, k), F32), jax.ShapeDtypeStruct((size // 2, k), F32)
    tile = jax.ShapeDtypeStruct((size, size), BF16)
    return pl.pallas_call(
        first_coupling_kernel,
        in_specs=[SMEM] + [pl.BlockSpec(memory_space=pltpu.HBM)] * 2,
        out_specs=[VMEM] * 7,
        out_shape=[whole, tile, tile, whole, half, half, whole],
        scratch_shapes=[
            pltpu.VMEM((2 * chunks, size // chunks, size), F32),
            pltpu.SemaphoreType.DMA((2 * chunks + 1,)),
        ],
        compiler_params=params(46),
        cost_estimate=cost(4 * size * size * k, 12 * size * size),
    )(flags, vec, low)


def coupling_kernel(vec, low_one, low_two, one, one_a, one_b, far):
    across = vec[...].T.astype(BF16)
    one[...] = jnp.dot(across, low_one[...], preferred_element_type=F32).T
    split_store(one[...], one_a, one_b)
    far[...] = jnp.dot(across, low_two[...], preferred_element_type=F32).T


def coupling(vec, low_one, low_two):
    size, k = vec.shape
    whole, half = jax.ShapeDtypeStruct((size, k), F32), jax.ShapeDtypeStruct((size // 2, k), F32)
    return pl.pallas_call(
        coupling_kernel,
        in_specs=[VMEM] * 3,
        out_specs=[VMEM] * 4,
        out_shape=[whole, half, half, whole],
        compiler_params=params(),
        cost_estimate=cost(4 * size * size * k, 4 * size * size),
    )(vec, low_one, low_two)


def relay_kernel(part, place, far, pair, after, out):
    half = pair.shape[0]
    out[...] = far[part * half : (part + 1) * half] + jnp.where(place[0] > 0, pair[...], 0.0)


def choose_kernel(place, vec, two, after, out):
    out[...] = jnp.where(place[0] > 0, two[...], vec[...])


def small(kernel, place, left, right, after):
    return pl.pallas_call(
        kernel,
        in_specs=[SMEM, VMEM, VMEM, pl.BlockSpec(memory_space=pl.ANY)],
        out_specs=VMEM,
        out_shape=jax.ShapeDtypeStruct(right.shape, F32),
        compiler_params=params(),
        cost_estimate=cost(right.size, 12 * right.size),
    )(place, left, right, after)


def first_diag_kernel(vec, diag, narrow, product):
    tile = diag[...].astype(BF16)
    narrow[...] = tile
    product[...] = jnp.dot(tile, vec[...].astype(BF16), preferred_element_type=F32)


def first_diag(vec, diag):
    size, k = vec.shape
    rows = size // 4
    return pl.pallas_call(
        first_diag_kernel,
        grid=(4,),
        in_specs=[pl.BlockSpec((size, k), lambda r: (0, 0)), pl.BlockSpec((rows, size), lambda r: (r, 0))],
        out_specs=[pl.BlockSpec((rows, size), lambda r: (r, 0)), pl.BlockSpec((rows, k), lambda r: (r, 0))],
        out_shape=[jax.ShapeDtypeStruct(diag.shape, BF16), jax.ShapeDtypeStruct(vec.shape, F32)],
        compiler_params=params(),
        cost_estimate=cost(2 * size * size * k, 6 * size * size),
    )(vec, diag)


def diag_kernel(vec, diag, product):
    product[...] = jnp.dot(diag[...], vec[...].astype(BF16), preferred_element_type=F32)


def diag_times(vec, diag):
    size, k = vec.shape
    return pl.pallas_call(
        diag_kernel,
        in_specs=[VMEM, VMEM],
        out_specs=VMEM,
        out_shape=jax.ShapeDtypeStruct(vec.shape, F32),
        compiler_params=params(),
        cost_estimate=cost(2 * size * size * k, 2 * size * size),
    )(vec, diag)


def finish_kernel(place, part, low, one, ahead_a, ahead_b, pair_a, pair_b, wrap_one, wrap_two, out):
    acc = jnp.dot(low[...], one[...].astype(BF16), preferred_element_type=F32) + part[...]
    half = ahead_a.shape[0]
    for number, (straight, pair) in enumerate(((ahead_a, pair_a), (ahead_b, pair_b))):
        rows = slice(number * half, (number + 1) * half)
        far = jnp.where(place[1] > 0, wrap_one[rows] + wrap_two[rows], straight[...])
        out[rows] = acc[rows] + far + jnp.where(place[0] > 0, 0.0, pair[...])


def finish(place, part, low, *arrived):
    size, k = part.shape
    return pl.pallas_call(
        finish_kernel,
        in_specs=[SMEM] + [VMEM] * 9,
        out_specs=VMEM,
        out_shape=jax.ShapeDtypeStruct(part.shape, F32),
        compiler_params=params(),
        cost_estimate=cost(2 * size * size * k, 2 * size * size),
    )(place, part, low, *arrived)


def two_kernel(own, low, two, product):
    product[...] = own[...] + jnp.dot(low[...], two[...].astype(BF16), preferred_element_type=F32)


def add_two(own, low, two):
    size, k = two.shape
    return pl.pallas_call(
        two_kernel,
        in_specs=[VMEM] * 3,
        out_specs=VMEM,
        out_shape=jax.ShapeDtypeStruct(two.shape, F32),
        compiler_params=params(),
        cost_estimate=cost(2 * size * size * k, 2 * size * size),
    )(own, low, two)


def most_kernel(low_one, low_two, one_a, two_a, two_b, v0, v1, v2, own, part, moments):
    half = one_a.shape[0]
    below = jnp.dot(low_one[:, :half], one_a[...].astype(BF16), preferred_element_type=F32)
    below = below + jnp.dot(low_two[:, :half], two_a[...].astype(BF16), preferred_element_type=F32)
    below = below + jnp.dot(low_two[:, half:], two_b[...].astype(BF16), preferred_element_type=F32)
    part[...] = own[...] + 2.0 * below
    pairs = [(v0, v0), (v0, v1), (v1, v1), (v1, v2), (v2, v2)]
    for row, (a, b) in enumerate(pairs):
        moments[row : row + 1] = jnp.sum(a[...] * b[...], axis=0, keepdims=True)
    moments[5:8] = jnp.zeros_like(moments[5:8])


def last_kernel(low, one_b, v2, part, moments, out):
    half = one_b.shape[0]
    image = part[...] + 2.0 * jnp.dot(low[:, half:], one_b[...].astype(BF16), preferred_element_type=F32)
    out[...] = moments[...]
    out[5:6] = jnp.sum(v2[...] * image, axis=0, keepdims=True)


def most(low_one, low_two, one_a, two_a, two_b, v0, v1, v2, own):
    size, k = v0.shape
    return pl.pallas_call(
        most_kernel,
        in_specs=[VMEM] * 9,
        out_specs=[VMEM] * 2,
        out_shape=[jax.ShapeDtypeStruct(v0.shape, F32), jax.ShapeDtypeStruct((8, k), F32)],
        compiler_params=params(),
        cost_estimate=cost(3 * size * size * k, 3 * size * size),
    )(low_one, low_two, one_a, two_a, two_b, v0, v1, v2, own)


def last(low, one_b, v2, part, moments):
    size, k = v2.shape
    return pl.pallas_call(
        last_kernel,
        in_specs=[VMEM] * 5,
        out_specs=VMEM,
        out_shape=jax.ShapeDtypeStruct((8, k), F32),
        compiler_params=params(),
        cost_estimate=cost(size * size * k, size * size),
    )(low, one_b, v2, part, moments)


def group_rows(genotypes, groups, group):
    rows = genotypes.shape[0] // groups
    return genotypes[pl.ds(pl.multiple_of(group * rows, rows), rows)]


def send_kernel(groups, row, pieces, penalty, v0, v1, v2, genotypes, effects, rounded, send):
    sums = pieces[0]
    for piece in range(1, pieces.shape[0]):
        sums = sums + pieces[piece]
    moments = [sums[m : m + 1] for m in range(6)]
    c0, c1, c2 = coefficients(moments, penalty[...])
    value = c0 * v0[...] + c1 * v1[...] + c2 * v2[...]
    effects[...] = value
    narrow = value.astype(BF16)
    rounded[...] = narrow
    other = 1 - row[0] % 2
    for g in range(groups // 2):
        send[g] = jnp.dot(group_rows(genotypes, groups, 2 * g + other), narrow, preferred_element_type=F32)


def keep_kernel(groups, row, rounded, genotypes, keep):
    mine = row[0] % 2
    for g in range(groups // 2):
        keep[g] = jnp.dot(group_rows(genotypes, groups, 2 * g + mine), rounded[...], preferred_element_type=F32)


def partial_scores(row, groups, pieces, penalty, v0, v1, v2, genotypes):
    people, size = genotypes.shape
    k = v0.shape[1]
    half = jax.ShapeDtypeStruct((groups // 2, people // groups, k), F32)
    effects, rounded, send = pl.pallas_call(
        functools.partial(send_kernel, groups),
        in_specs=[SMEM] + [VMEM] * 6,
        out_specs=[VMEM] * 3,
        out_shape=[jax.ShapeDtypeStruct(v0.shape, F32), jax.ShapeDtypeStruct(v0.shape, BF16), half],
        compiler_params=params(),
        cost_estimate=cost(people * size * k, 2 * people * size),
    )(row, pieces, penalty, v0, v1, v2, genotypes)
    keep = pl.pallas_call(
        functools.partial(keep_kernel, groups),
        in_specs=[SMEM, VMEM, VMEM],
        out_specs=VMEM,
        out_shape=half,
        compiler_params=params(),
        cost_estimate=cost(people * size * k, 2 * people * size),
    )(row, rounded, genotypes)
    return effects, send, keep


def pick_kernel(index, keep, received, mine, other):
    mine[...] = keep[index[0]] + received[index[0]]
    other[...] = keep[1 - index[0]] + received[1 - index[0]]


def pick(index, keep, received):
    half = jax.ShapeDtypeStruct(keep.shape[1:], F32)
    return pl.pallas_call(
        pick_kernel,
        in_specs=[SMEM, VMEM, VMEM],
        out_specs=[VMEM] * 2,
        out_shape=[half] * 2,
        compiler_params=params(),
        cost_estimate=cost(keep.size, 12 * keep.size),
    )(index, keep, received)


def scattered_over(values, axis):
    n = lax.axis_size(axis)
    pieces = values.reshape((n, values.shape[0] // n) + values.shape[1:])
    return jnp.sum(lax.all_to_all(pieces, axis, 0, 0, tiled=True), axis=0)


def routed(block, pairs):
    return lax.ppermute(block, AXES, pairs)


def coefficients(moments, penalty):
    def inner(u, v):
        return sum(a * b * moments[i + j] for i, a in enumerate(u) for j, b in enumerate(v))

    n0 = moments[0]
    a0 = n0 / (moments[1] + penalty * n0)
    r1 = [1.0 - a0 * penalty, -a0]
    n1 = inner(r1, r1)
    b0 = n1 / n0
    d1 = [r1[0] + b0, r1[1]]
    ad1 = [penalty * d1[0], d1[0] + penalty * d1[1], d1[1]]
    a1 = n1 / inner(d1, ad1)
    e1 = [a0 + a1 * d1[0], a1 * d1[1]]
    r2 = [r1[0] - a1 * ad1[0], r1[1] - a1 * ad1[1], -a1 * ad1[2]]
    n2 = inner(r2, r2)
    b1 = n2 / n1
    d2 = [r2[0] + b1 * d1[0], r2[1] + b1 * d1[1], r2[2]]
    ad2 = [penalty * d2[0], d2[0] + penalty * d2[1], d2[1] + penalty * d2[2], d2[2]]
    a2 = n2 / inner(d2, ad2)
    return e1[0] + a2 * d2[0], e1[1] + a2 * d2[1], a2 * d2[2]


def swapped(block, bit):
    return routed(block, [(i, i ^ bit) for i in range(lax.axis_size(AXES))])


def body(marginal, penalty, ld_diag, ld_low, band, genotypes):
    n = lax.axis_size(AXES)
    rows, cols = lax.axis_size("row"), lax.axis_size("col")
    position = lax.axis_index(AXES)
    row = lax.axis_index("row")
    flags = jnp.stack([jnp.logical_and(band[0] >= d, position >= d) for d in (1, 2)]).astype(jnp.int32)
    place = jnp.stack([position % 2 == 1, position % cols >= cols - 2]).astype(jnp.int32)
    half = marginal.shape[0] // 2
    near_back = [(i, i - 2) for i in range(2, n) if i % cols >= 2]
    wrap_two_back = [(i, i - 2) for i in range(2, n) if i % cols < 2]
    wrap_one_back = [(i, i - 1) for i in range(cols, n, cols)]

    def halos(vec, two, one, one_a, one_b, far):
        pair_a, pair_b = swapped(one_a, 1), swapped(one_b, 1)
        wrap_two = routed(far, wrap_two_back)
        wrap_one = routed(one, wrap_one_back)
        sum_a = small(functools.partial(relay_kernel, 0), place, far, pair_a, far)
        up_a = routed(sum_a, near_back)
        chosen = small(choose_kernel, place, vec, two, sum_a)
        one = swapped(chosen, 1)
        up_b = routed(small(functools.partial(relay_kernel, 1), place, far, pair_b, chosen), near_back)
        return one, up_a, up_b, pair_a, pair_b, wrap_one, wrap_two

    two = shifted(marginal, 2)
    v0, low_one, low_two, *products = first_coupling(flags, marginal, ld_low[0])
    arrived = halos(v0, two, *products)
    diag, own = first_diag(v0, ld_diag[0])
    v1 = finish(place, add_two(own, low_two, two), low_one, *arrived)

    two = shifted(v1, 2)
    arrived = halos(v1, two, *coupling(v1, low_one, low_two))
    v2 = finish(place, add_two(diag_times(v1, diag), low_two, two), low_one, *arrived)

    ones, twos = [], []
    for part in (v2[:half], v2[half:]):
        twos.append(shifted(part, 2))
        ones.append(swapped(small(choose_kernel, place, part, twos[-1], part), 1))
    part, moments = most(low_one, low_two, ones[0], *twos, v0, v1, v2, diag_times(v2, diag))
    moments = last(low_one, ones[1], v2, part, moments)
    pieces = lax.all_to_all(jnp.broadcast_to(moments[None], (n,) + moments.shape), AXES, 0, 0, tiled=True)

    effects, send, keep = partial_scores(row.astype(jnp.int32)[None], rows, pieces, penalty[None], v0, v1, v2, genotypes)
    received = swapped(send, cols)
    bit = rows // 4
    while bit:
        mine = (row // (2 * bit)) % 2
        keep = keep.reshape((2, -1) + keep.shape[1:])
        received = received.reshape((2, -1) + received.shape[1:])

        keep, send = pick(mine.astype(jnp.int32)[None], keep, received)
        received = swapped(send, 2 * bit * cols)
        bit //= 2
    return effects, scattered_over((keep + received)[0], "col")


def solution(mesh):
    placed = (
        P(AXES, None),
        P(),
        P(AXES, None, None),
        P(AXES, None, None, None),
        P(AXES),
        P(None, AXES),
    )
    return jax.shard_map(
        body,
        mesh=mesh,
        in_specs=placed,
        out_specs=(P(AXES, None), P(AXES, None)),
        check_vma=False,
    )
```

```python
import functools

import jax
import jax.numpy as jnp
from jax import lax
from jax.experimental import pallas as pl
from jax.experimental.pallas import tpu as pltpu
from jax.sharding import PartitionSpec as P

AXES = ("row", "col")
F32 = jnp.float32
BF16 = jnp.bfloat16
MIB = 1024 * 1024
VMEM = pl.BlockSpec(memory_space=pltpu.VMEM)
SMEM = pl.BlockSpec(memory_space=pltpu.SMEM)


def params(mib=20):
    return pltpu.CompilerParams(vmem_limit_bytes=mib * MIB)


def cost(flops, num_bytes):
    return pl.CostEstimate(flops=int(flops), bytes_accessed=int(num_bytes), transcendentals=0)


def shifted(block, distance):
    n = lax.axis_size(AXES)
    route = [(i - distance, i) for i in range(n) if 0 <= i - distance < n]
    return lax.ppermute(block, AXES, route)


def split_store(value, first, second):
    half = first.shape[0]
    first[...] = value[:half]
    second[...] = value[half:]


def first_coupling_kernel(flags, vec, low, narrow, one_a, one_b, far_a, far_b, tiles, arrived):
    count, size = narrow.shape[0], narrow.shape[1]
    chunks = tiles.shape[0] // count
    rows = size // chunks
    copies = []
    for d in range(count):
        for c in range(chunks):
            place = d * chunks + c
            copies.append(pltpu.make_async_copy(low.at[d, pl.ds(c * rows, rows)], tiles.at[place], arrived.at[place]))
            copies[-1].start()
    across = vec[...].T.astype(BF16)
    for d, (first, second) in enumerate(((one_a, one_b), (far_a, far_b))):
        acc = None
        for c in range(chunks):
            place = d * chunks + c
            copies[place].wait()
            tile = jnp.where(flags[d] > 0, tiles[place], 0.0).astype(BF16)
            narrow[d, c * rows : (c + 1) * rows] = tile
            term = jnp.dot(across[:, c * rows : (c + 1) * rows], tile, preferred_element_type=F32)
            acc = term if acc is None else acc + term
        split_store(acc.T, first, second)


def first_coupling(flags, vec, low):
    count, size, _ = low.shape
    k = vec.shape[1]
    chunks = 4
    return pl.pallas_call(
        first_coupling_kernel,
        in_specs=[SMEM, VMEM, pl.BlockSpec(memory_space=pltpu.HBM)],
        out_specs=[VMEM] * 5,
        out_shape=[jax.ShapeDtypeStruct(low.shape, BF16)] + [jax.ShapeDtypeStruct((size // 2, k), F32)] * 4,
        scratch_shapes=[
            pltpu.VMEM((count * chunks, size // chunks, size), F32),
            pltpu.SemaphoreType.DMA((count * chunks,)),
        ],
        compiler_params=params(46),
        cost_estimate=cost(4 * size * size * k, 12 * size * size),
    )(flags, vec, low)


def coupling_kernel(vec, low, one_a, one_b, far_a, far_b):
    across = vec[...].T.astype(BF16)
    split_store(jnp.dot(across, low[0], preferred_element_type=F32).T, one_a, one_b)
    split_store(jnp.dot(across, low[1], preferred_element_type=F32).T, far_a, far_b)


def coupling(vec, low):
    size, k = vec.shape
    return pl.pallas_call(
        coupling_kernel,
        in_specs=[VMEM, VMEM],
        out_specs=[VMEM] * 4,
        out_shape=[jax.ShapeDtypeStruct((size // 2, k), F32)] * 4,
        compiler_params=params(),
        cost_estimate=cost(4 * size * size * k, 4 * size * size),
    )(vec, low)


def relay_kernel(odd, far, pair, after, out):
    out[...] = far[...] + jnp.where(odd[0] > 0, pair[...], 0.0)


def choose_kernel(odd, vec, two, after, out):
    out[...] = jnp.where(odd[0] > 0, two[...], vec[...])


def small(kernel, odd, left, right, after):
    return pl.pallas_call(
        kernel,
        in_specs=[SMEM, VMEM, VMEM, pl.BlockSpec(memory_space=pl.ANY)],
        out_specs=VMEM,
        out_shape=jax.ShapeDtypeStruct(left.shape, F32),
        compiler_params=params(),
        cost_estimate=cost(left.size, 12 * left.size),
    )(odd, left, right, after)


def first_diag_kernel(vec, diag, narrow, product):
    tile = diag[...].astype(BF16)
    narrow[...] = tile
    product[...] = jnp.dot(tile, vec[...].astype(BF16), preferred_element_type=F32)


def first_diag(vec, diag):
    size, k = vec.shape
    rows = size // 4
    return pl.pallas_call(
        first_diag_kernel,
        grid=(4,),
        in_specs=[pl.BlockSpec((size, k), lambda r: (0, 0)), pl.BlockSpec((rows, size), lambda r: (r, 0))],
        out_specs=[pl.BlockSpec((rows, size), lambda r: (r, 0)), pl.BlockSpec((rows, k), lambda r: (r, 0))],
        out_shape=[jax.ShapeDtypeStruct(diag.shape, BF16), jax.ShapeDtypeStruct(vec.shape, F32)],
        compiler_params=params(),
        cost_estimate=cost(2 * size * size * k, 6 * size * size),
    )(vec, diag)


def diag_kernel(vec, diag, product):
    product[...] = jnp.dot(diag[...], vec[...].astype(BF16), preferred_element_type=F32)


def diag_times(vec, diag):
    size, k = vec.shape
    return pl.pallas_call(
        diag_kernel,
        in_specs=[VMEM, VMEM],
        out_specs=VMEM,
        out_shape=jax.ShapeDtypeStruct(vec.shape, F32),
        compiler_params=params(),
        cost_estimate=cost(2 * size * size * k, 2 * size * size),
    )(vec, diag)


def finish_kernel(odd, part, low, one, ahead_a, ahead_b, pair_a, pair_b, out, upper):
    acc = jnp.dot(low[0], one[...].astype(BF16), preferred_element_type=F32) + part[...]
    half = ahead_a.shape[0]
    for place, (straight, pair) in enumerate(((ahead_a, pair_a), (ahead_b, pair_b))):
        rows = slice(place * half, (place + 1) * half)
        out[rows] = acc[rows] + straight[...] + jnp.where(odd[0] > 0, 0.0, pair[...])
    upper[...] = out[:half]


def finish(odd, part, low, one, ahead_a, ahead_b, pair_a, pair_b):
    size, k = part.shape
    return pl.pallas_call(
        finish_kernel,
        in_specs=[SMEM] + [VMEM] * 7,
        out_specs=[VMEM] * 2,
        out_shape=[jax.ShapeDtypeStruct(part.shape, F32), jax.ShapeDtypeStruct((size // 2, k), F32)],
        compiler_params=params(),
        cost_estimate=cost(2 * size * size * k, 2 * size * size),
    )(odd, part, low, one, ahead_a, ahead_b, pair_a, pair_b)


def two_kernel(own, low, two, product):
    product[...] = own[...] + jnp.dot(low[1], two[...].astype(BF16), preferred_element_type=F32)


def add_two(own, low, two):
    size, k = two.shape
    return pl.pallas_call(
        two_kernel,
        in_specs=[VMEM] * 3,
        out_specs=VMEM,
        out_shape=jax.ShapeDtypeStruct(two.shape, F32),
        compiler_params=params(),
        cost_estimate=cost(2 * size * size * k, 2 * size * size),
    )(own, low, two)


def lower_kernel(vec, low, one, far):
    across = vec[...].T.astype(BF16)
    half = one.shape[0]
    one[...] = jnp.dot(across, low[0, :, half:], preferred_element_type=F32).T
    far[...] = jnp.dot(across, low[1, :, half:], preferred_element_type=F32).T


def lower_coupling(vec, low):
    size, k = vec.shape
    return pl.pallas_call(
        lower_kernel,
        in_specs=[VMEM, VMEM],
        out_specs=[VMEM] * 2,
        out_shape=[jax.ShapeDtypeStruct((size // 2, k), F32)] * 2,
        compiler_params=params(),
        cost_estimate=cost(2 * size * size * k, 2 * size * size),
    )(vec, low)


def own_kernel(v0, v1, v2, diag, moments):
    image = jnp.dot(diag[...], v2[...].astype(BF16), preferred_element_type=F32)
    pairs = [(v0, v0), (v0, v1), (v1, v1), (v1, v2), (v2, v2)]
    for row, (a, b) in enumerate(pairs):
        moments[row : row + 1] = jnp.sum(a[...] * b[...], axis=0, keepdims=True)
    moments[5:6] = jnp.sum(v2[...] * image, axis=0, keepdims=True)
    moments[6:8] = jnp.zeros_like(moments[6:8])


def own_moments(v0, v1, v2, diag):
    size, k = v0.shape
    return pl.pallas_call(
        own_kernel,
        in_specs=[VMEM] * 4,
        out_specs=VMEM,
        out_shape=jax.ShapeDtypeStruct((8, k), F32),
        compiler_params=params(),
        cost_estimate=cost(2 * size * size * k, 2 * size * size),
    )(v0, v1, v2, diag)


def last_kernel(odd, low, one, two, v2, up, pair, moments, out):
    half = one.shape[0]
    below = jnp.dot(low[1, :, :half], two[...].astype(BF16), preferred_element_type=F32)
    below = below + jnp.dot(low[0, :, :half], one[...].astype(BF16), preferred_element_type=F32)
    above = up[...] + jnp.where(odd[0] > 0, 0.0, pair[...])
    coupled = jnp.sum(v2[...] * below, axis=0, keepdims=True) + jnp.sum(v2[half:] * above, axis=0, keepdims=True)
    out[...] = moments[...]
    out[5:6] = moments[5:6] + 2.0 * coupled


def last(odd, low, one, two, v2, up, pair, moments):
    size, k = v2.shape
    return pl.pallas_call(
        last_kernel,
        in_specs=[SMEM] + [VMEM] * 7,
        out_specs=VMEM,
        out_shape=jax.ShapeDtypeStruct((8, k), F32),
        compiler_params=params(),
        cost_estimate=cost(2 * size * size * k, 2 * size * size),
    )(odd, low, one, two, v2, up, pair, moments)


def group_rows(genotypes, groups, group):
    rows = genotypes.shape[0] // groups
    return genotypes[pl.ds(pl.multiple_of(group * rows, rows), rows)]


def send_kernel(groups, row, pieces, penalty, v0, v1, v2, genotypes, effects, rounded, send):
    sums = pieces[0]
    for piece in range(1, pieces.shape[0]):
        sums = sums + pieces[piece]
    moments = [sums[m : m + 1] for m in range(6)]
    c0, c1, c2 = coefficients(moments, penalty[...])
    value = c0 * v0[...] + c1 * v1[...] + c2 * v2[...]
    effects[...] = value
    narrow = value.astype(BF16)
    rounded[...] = narrow
    other = 1 - row[0] % 2
    for g in range(groups // 2):
        send[g] = jnp.dot(group_rows(genotypes, groups, 2 * g + other), narrow, preferred_element_type=F32)


def keep_kernel(groups, row, rounded, genotypes, keep):
    mine = row[0] % 2
    for g in range(groups // 2):
        keep[g] = jnp.dot(group_rows(genotypes, groups, 2 * g + mine), rounded[...], preferred_element_type=F32)


def partial_scores(row, groups, pieces, penalty, v0, v1, v2, genotypes):
    people, size = genotypes.shape
    k = v0.shape[1]
    half = jax.ShapeDtypeStruct((groups // 2, people // groups, k), F32)
    effects, rounded, send = pl.pallas_call(
        functools.partial(send_kernel, groups),
        in_specs=[SMEM] + [VMEM] * 6,
        out_specs=[VMEM] * 3,
        out_shape=[jax.ShapeDtypeStruct(v0.shape, F32), jax.ShapeDtypeStruct(v0.shape, BF16), half],
        compiler_params=params(),
        cost_estimate=cost(people * size * k, 2 * people * size),
    )(row, pieces, penalty, v0, v1, v2, genotypes)
    keep = pl.pallas_call(
        functools.partial(keep_kernel, groups),
        in_specs=[SMEM, VMEM, VMEM],
        out_specs=VMEM,
        out_shape=half,
        compiler_params=params(),
        cost_estimate=cost(people * size * k, 2 * people * size),
    )(row, rounded, genotypes)
    return effects, send, keep


def pick_kernel(index, keep, received, mine, other):
    mine[...] = keep[index[0]] + received[index[0]]
    other[...] = keep[1 - index[0]] + received[1 - index[0]]


def pick(index, keep, received):
    half = jax.ShapeDtypeStruct(keep.shape[1:], F32)
    return pl.pallas_call(
        pick_kernel,
        in_specs=[SMEM, VMEM, VMEM],
        out_specs=[VMEM] * 2,
        out_shape=[half] * 2,
        compiler_params=params(),
        cost_estimate=cost(keep.size, 12 * keep.size),
    )(index, keep, received)


def scattered_over(values, axis):
    n = lax.axis_size(axis)
    pieces = values.reshape((n, values.shape[0] // n) + values.shape[1:])
    return jnp.sum(lax.all_to_all(pieces, axis, 0, 0, tiled=True), axis=0)


def routed(block, pairs):
    return lax.ppermute(block, AXES, pairs)


def coefficients(moments, penalty):
    def inner(u, v):
        return sum(a * b * moments[i + j] for i, a in enumerate(u) for j, b in enumerate(v))

    n0 = moments[0]
    a0 = n0 / (moments[1] + penalty * n0)
    r1 = [1.0 - a0 * penalty, -a0]
    n1 = inner(r1, r1)
    b0 = n1 / n0
    d1 = [r1[0] + b0, r1[1]]
    ad1 = [penalty * d1[0], d1[0] + penalty * d1[1], d1[1]]
    a1 = n1 / inner(d1, ad1)
    e1 = [a0 + a1 * d1[0], a1 * d1[1]]
    r2 = [r1[0] - a1 * ad1[0], r1[1] - a1 * ad1[1], -a1 * ad1[2]]
    n2 = inner(r2, r2)
    b1 = n2 / n1
    d2 = [r2[0] + b1 * d1[0], r2[1] + b1 * d1[1], r2[2]]
    ad2 = [penalty * d2[0], d2[0] + penalty * d2[1], d2[1] + penalty * d2[2], d2[2]]
    a2 = n2 / inner(d2, ad2)
    return e1[0] + a2 * d2[0], e1[1] + a2 * d2[1], a2 * d2[2]


def swapped(block, bit):
    return routed(block, [(i, i ^ bit) for i in range(lax.axis_size(AXES))])


def body(marginal, penalty, ld_diag, ld_low, band, genotypes):
    n = lax.axis_size(AXES)
    rows, cols = lax.axis_size("row"), lax.axis_size("col")
    position = lax.axis_index(AXES)
    row = lax.axis_index("row")
    flags = jnp.stack([jnp.logical_and(band[0] >= d, position >= d) for d in (1, 2)]).astype(jnp.int32)
    odd = (position % 2).astype(jnp.int32)[None]
    half = marginal.shape[0] // 2

    def halos(vec, two, products):
        one_a, one_b, far_a, far_b = products
        pair_a, pair_b = swapped(one_a, 1), swapped(one_b, 1)
        sum_a = small(relay_kernel, odd, far_a, pair_a, far_b)
        up_a = shifted(sum_a, -2)
        chosen = small(choose_kernel, odd, vec, two, sum_a)
        one = swapped(chosen, 1)
        up_b = shifted(small(relay_kernel, odd, far_b, pair_b, chosen), -2)
        return one, up_a, up_b, pair_a, pair_b

    v0 = marginal
    two = shifted(v0, 2)
    low, *products = first_coupling(flags, v0, ld_low[0])
    parts = halos(v0, two, products)
    diag, own = first_diag(v0, ld_diag[0])
    v1, _ = finish(odd, add_two(own, low, two), low, *parts)

    two = shifted(v1, 2)
    parts = halos(v1, two, coupling(v1, low))
    v2, upper = finish(odd, add_two(diag_times(v1, diag), low, two), low, *parts)

    two = shifted(upper, 2)
    one, far = lower_coupling(v2, low)
    pair = swapped(one, 1)
    moments = own_moments(v0, v1, v2, diag)
    above = small(relay_kernel, odd, far, pair, far)
    up = shifted(above, -2)
    one = swapped(small(choose_kernel, odd, upper, two, above), 1)
    moments = last(odd, low, one, two, v2, up, pair, moments)
    pieces = lax.all_to_all(jnp.broadcast_to(moments[None], (n,) + moments.shape), AXES, 0, 0, tiled=True)

    effects, send, keep = partial_scores(row.astype(jnp.int32)[None], rows, pieces, penalty[None], v0, v1, v2, genotypes)
    received = swapped(send, cols)
    bit = rows // 4
    while bit:
        mine = (row // (2 * bit)) % 2
        keep = keep.reshape((2, -1) + keep.shape[1:])
        received = received.reshape((2, -1) + received.shape[1:])

        keep, send = pick(mine.astype(jnp.int32)[None], keep, received)
        received = swapped(send, 2 * bit * cols)
        bit //= 2
    return effects, scattered_over((keep + received)[0], "col")


def solution(mesh):
    placed = (
        P(AXES, None),
        P(),
        P(AXES, None, None),
        P(AXES, None, None, None),
        P(AXES),
        P(None, AXES),
    )
    return jax.shard_map(
        body,
        mesh=mesh,
        in_specs=placed,
        out_specs=(P(AXES, None), P(AXES, None)),
        check_vma=False,
    )
```

```python
import functools

import jax
import jax.numpy as jnp
from jax import lax
from jax.experimental import pallas as pl
from jax.experimental.pallas import tpu as pltpu
from jax.sharding import PartitionSpec as P

AXES = ("row", "col")
F32 = jnp.float32
BF16 = jnp.bfloat16
MIB = 1024 * 1024
VMEM = pl.BlockSpec(memory_space=pltpu.VMEM)
SMEM = pl.BlockSpec(memory_space=pltpu.SMEM)
ANY = pl.BlockSpec(memory_space=pl.ANY)


def params(mib=20):
    return pltpu.CompilerParams(vmem_limit_bytes=mib * MIB)


def cost(flops, num_bytes):
    return pl.CostEstimate(flops=int(flops), bytes_accessed=int(num_bytes), transcendentals=0)


def shifted(block, distance):
    n = lax.axis_size(AXES)
    route = [(i - distance, i) for i in range(n) if 0 <= i - distance < n]
    return lax.ppermute(block, AXES, route)


def split(size):
    return size * 5 // 8, size - size * 5 // 8


def split_store(value, first, second):
    rows = first.shape[0]
    first[...] = value[:rows]
    second[...] = value[rows:]


def first_coupling_kernel(flags, vec, low, one_a, one_b, far_a, far_b, own, tiles, arrived):
    size = own.shape[0]
    chunks = tiles.shape[0] // 2
    rows = size // chunks
    fetch = pltpu.make_async_copy(vec, own, arrived.at[2 * chunks])
    fetch.start()
    copies = []
    for place in range(2 * chunks):
        d, c = place // chunks, place % chunks
        copies.append(pltpu.make_async_copy(low.at[d, pl.ds(c * rows, rows)], tiles.at[place], arrived.at[place]))
        copies[-1].start()
    fetch.wait()
    across = own[...].T.astype(BF16)
    for d, (first, second) in enumerate(((one_a, one_b), (far_a, far_b))):
        acc = None
        for c in range(chunks):
            place = d * chunks + c
            copies[place].wait()
            tile = jnp.where(flags[d] > 0, tiles[place], 0.0).astype(BF16)
            term = jnp.dot(across[:, c * rows : (c + 1) * rows], tile, preferred_element_type=F32)
            acc = term if acc is None else acc + term
        split_store(acc.T, first, second)


def first_coupling(flags, vec, low):
    size, k = vec.shape
    chunks = 4
    return pl.pallas_call(
        first_coupling_kernel,
        in_specs=[SMEM] + [pl.BlockSpec(memory_space=pltpu.HBM)] * 2,
        out_specs=[VMEM] * 4,
        out_shape=[jax.ShapeDtypeStruct((rows, k), F32) for rows in split(size) * 2],
        scratch_shapes=[
            pltpu.VMEM((size, k), F32),
            pltpu.VMEM((2 * chunks, size // chunks, size), F32),
            pltpu.SemaphoreType.DMA((2 * chunks + 1,)),
        ],
        compiler_params=params(58),
        cost_estimate=cost(4 * size * size * k, 8 * size * size),
    )(flags, vec, low)


def narrow_kernel(flags, low, after, out):
    out[0] = jnp.where(flags[pl.program_id(0)] > 0, low[0], 0.0).astype(BF16)


def narrowed(flags, low, after):
    count, size, _ = low.shape
    rows = size // 2
    block = pl.BlockSpec((1, rows, size), lambda d, r: (d, r, 0))
    return pl.pallas_call(
        narrow_kernel,
        grid=(count, size // rows),
        in_specs=[SMEM, block, ANY],
        out_specs=block,
        out_shape=jax.ShapeDtypeStruct(low.shape, BF16),
        compiler_params=params(),
        cost_estimate=cost(2 * size * size, 12 * size * size),
    )(flags, low, after)


def coupling_kernel(vec, low, one_a, one_b, far_a, far_b):
    across = vec[...].T.astype(BF16)
    split_store(jnp.dot(across, low[0], preferred_element_type=F32).T, one_a, one_b)
    split_store(jnp.dot(across, low[1], preferred_element_type=F32).T, far_a, far_b)


def coupling(vec, low):
    size, k = vec.shape
    return pl.pallas_call(
        coupling_kernel,
        in_specs=[VMEM, VMEM],
        out_specs=[VMEM] * 4,
        out_shape=[jax.ShapeDtypeStruct((rows, k), F32) for rows in split(size) * 2],
        compiler_params=params(),
        cost_estimate=cost(4 * size * size * k, 4 * size * size),
    )(vec, low)


def relay_kernel(odd, far, pair, after, out):
    out[...] = far[...] + jnp.where(odd[0] > 0, pair[...], 0.0)


def choose_kernel(odd, vec, two, after, first, second):
    split_store(jnp.where(odd[0] > 0, two[...], vec[...]), first, second)


def choose(odd, vec, two, after):
    rows, k = vec.shape
    return pl.pallas_call(
        choose_kernel,
        in_specs=[SMEM, VMEM, VMEM, ANY],
        out_specs=[VMEM] * 2,
        out_shape=[jax.ShapeDtypeStruct((rows // 2, k), F32)] * 2,
        compiler_params=params(),
        cost_estimate=cost(vec.size, 12 * vec.size),
    )(odd, vec, two, after)


def relay(odd, far, pair, after):
    return pl.pallas_call(
        relay_kernel,
        in_specs=[SMEM, VMEM, VMEM, ANY],
        out_specs=VMEM,
        out_shape=jax.ShapeDtypeStruct(far.shape, F32),
        compiler_params=params(),
        cost_estimate=cost(far.size, 12 * far.size),
    )(odd, far, pair, after)


def first_diag_kernel(vec, diag, after, narrow, product):
    tile = diag[...].astype(BF16)
    narrow[...] = tile
    product[...] = jnp.dot(tile, vec[...].astype(BF16), preferred_element_type=F32)


def first_diag(vec, diag, after):
    size, k = vec.shape
    rows = size // 4
    return pl.pallas_call(
        first_diag_kernel,
        grid=(4,),
        in_specs=[pl.BlockSpec((size, k), lambda r: (0, 0)), pl.BlockSpec((rows, size), lambda r: (r, 0)), ANY],
        out_specs=[pl.BlockSpec((rows, size), lambda r: (r, 0)), pl.BlockSpec((rows, k), lambda r: (r, 0))],
        out_shape=[jax.ShapeDtypeStruct(diag.shape, BF16), jax.ShapeDtypeStruct(vec.shape, F32)],
        compiler_params=params(),
        cost_estimate=cost(2 * size * size * k, 6 * size * size),
    )(vec, diag, after)


def diag_kernel(vec, diag, after, product):
    product[...] = jnp.dot(diag[...], vec[...].astype(BF16), preferred_element_type=F32)


def diag_times(vec, diag, after):
    size, k = vec.shape
    return pl.pallas_call(
        diag_kernel,
        in_specs=[VMEM, VMEM, ANY],
        out_specs=VMEM,
        out_shape=jax.ShapeDtypeStruct(vec.shape, F32),
        compiler_params=params(),
        cost_estimate=cost(2 * size * size * k, 6 * size * size),
    )(vec, diag, after)


def finish_kernel(odd, part, low, one_a, one_b, ahead_a, ahead_b, pair_a, pair_b, out, upper):
    half = one_a.shape[0]
    acc = jnp.dot(low[0, :, :half], one_a[...].astype(BF16), preferred_element_type=F32) + part[...]
    acc = acc + jnp.dot(low[0, :, half:], one_b[...].astype(BF16), preferred_element_type=F32)
    start = 0
    for straight, pair in ((ahead_a, pair_a), (ahead_b, pair_b)):
        rows = slice(start, start + pair.shape[0])
        out[rows] = acc[rows] + straight[...] + jnp.where(odd[0] > 0, 0.0, pair[...])
        start += pair.shape[0]
    upper[...] = out[:half]


def finish(odd, part, low, *arrived):
    size, k = part.shape
    return pl.pallas_call(
        finish_kernel,
        in_specs=[SMEM] + [VMEM] * 8,
        out_specs=[VMEM] * 2,
        out_shape=[jax.ShapeDtypeStruct(part.shape, F32), jax.ShapeDtypeStruct((size // 2, k), F32)],
        compiler_params=params(),
        cost_estimate=cost(2 * size * size * k, 2 * size * size),
    )(odd, part, low, *arrived)


def two_kernel(own, low, two, product):
    product[...] = own[...] + jnp.dot(low[1], two[...].astype(BF16), preferred_element_type=F32)


def add_two(own, low, two):
    size, k = two.shape
    return pl.pallas_call(
        two_kernel,
        in_specs=[VMEM] * 3,
        out_specs=VMEM,
        out_shape=jax.ShapeDtypeStruct(two.shape, F32),
        compiler_params=params(),
        cost_estimate=cost(2 * size * size * k, 2 * size * size),
    )(own, low, two)


def lower_kernel(vec, low, one, far):
    across = vec[...].T.astype(BF16)
    half = one.shape[0]
    one[...] = jnp.dot(across, low[0, :, half:], preferred_element_type=F32).T
    far[...] = jnp.dot(across, low[1, :, half:], preferred_element_type=F32).T


def lower_coupling(vec, low):
    size, k = vec.shape
    return pl.pallas_call(
        lower_kernel,
        in_specs=[VMEM, VMEM],
        out_specs=[VMEM] * 2,
        out_shape=[jax.ShapeDtypeStruct((size // 2, k), F32)] * 2,
        compiler_params=params(),
        cost_estimate=cost(2 * size * size * k, 2 * size * size),
    )(vec, low)


def own_kernel(v0, v1, v2, diag, after, moments):
    image = jnp.dot(diag[...], v2[...].astype(BF16), preferred_element_type=F32)
    pairs = [(v0, v0), (v0, v1), (v1, v1), (v1, v2), (v2, v2)]
    for row, (a, b) in enumerate(pairs):
        moments[row : row + 1] = jnp.sum(a[...] * b[...], axis=0, keepdims=True)
    moments[5:6] = jnp.sum(v2[...] * image, axis=0, keepdims=True)
    moments[6:8] = jnp.zeros_like(moments[6:8])


def own_moments(v0, v1, v2, diag, after):
    size, k = v0.shape
    return pl.pallas_call(
        own_kernel,
        in_specs=[VMEM] * 4 + [ANY],
        out_specs=VMEM,
        out_shape=jax.ShapeDtypeStruct((8, k), F32),
        compiler_params=params(),
        cost_estimate=cost(2 * size * size * k, 6 * size * size),
    )(v0, v1, v2, diag, after)


def last_kernel(odd, low, one_a, one_b, two, v2, up, pair, moments, out):
    quarter, half = one_a.shape[0], two.shape[0]
    below = jnp.dot(low[1, :, :half], two[...].astype(BF16), preferred_element_type=F32)
    below = below + jnp.dot(low[0, :, :quarter], one_a[...].astype(BF16), preferred_element_type=F32)
    below = below + jnp.dot(low[0, :, quarter:half], one_b[...].astype(BF16), preferred_element_type=F32)
    above = up[...] + jnp.where(odd[0] > 0, 0.0, pair[...])
    coupled = jnp.sum(v2[...] * below, axis=0, keepdims=True) + jnp.sum(v2[half:] * above, axis=0, keepdims=True)
    out[...] = moments[...]
    out[5:6] = moments[5:6] + 2.0 * coupled


def last(odd, low, one_a, one_b, two, v2, up, pair, moments):
    size, k = v2.shape
    return pl.pallas_call(
        last_kernel,
        in_specs=[SMEM] + [VMEM] * 8,
        out_specs=VMEM,
        out_shape=jax.ShapeDtypeStruct((8, k), F32),
        compiler_params=params(),
        cost_estimate=cost(2 * size * size * k, 2 * size * size),
    )(odd, low, one_a, one_b, two, v2, up, pair, moments)


def group_rows(genotypes, groups, group):
    rows = genotypes.shape[0] // groups
    return genotypes[pl.ds(pl.multiple_of(group * rows, rows), rows)]


def send_kernel(groups, row, pieces, penalty, v0, v1, v2, genotypes, effects, rounded, send):
    sums = pieces[0]
    for piece in range(1, pieces.shape[0]):
        sums = sums + pieces[piece]
    moments = [sums[m : m + 1] for m in range(6)]
    c0, c1, c2 = coefficients(moments, penalty[...])
    value = c0 * v0[...] + c1 * v1[...] + c2 * v2[...]
    effects[...] = value
    narrow = value.astype(BF16)
    rounded[...] = narrow
    other = 1 - row[0] % 2
    for g in range(groups // 2):
        send[g] = jnp.dot(group_rows(genotypes, groups, 2 * g + other), narrow, preferred_element_type=F32)


def keep_kernel(groups, row, rounded, genotypes, keep):
    mine = row[0] % 2
    for g in range(groups // 2):
        keep[g] = jnp.dot(group_rows(genotypes, groups, 2 * g + mine), rounded[...], preferred_element_type=F32)


def partial_scores(row, groups, pieces, penalty, v0, v1, v2, genotypes):
    people, size = genotypes.shape
    k = v0.shape[1]
    half = jax.ShapeDtypeStruct((groups // 2, people // groups, k), F32)
    effects, rounded, send = pl.pallas_call(
        functools.partial(send_kernel, groups),
        in_specs=[SMEM] + [VMEM] * 6,
        out_specs=[VMEM] * 3,
        out_shape=[jax.ShapeDtypeStruct(v0.shape, F32), jax.ShapeDtypeStruct(v0.shape, BF16), half],
        compiler_params=params(),
        cost_estimate=cost(people * size * k, 2 * people * size),
    )(row, pieces, penalty, v0, v1, v2, genotypes)
    keep = pl.pallas_call(
        functools.partial(keep_kernel, groups),
        in_specs=[SMEM, VMEM, VMEM],
        out_specs=VMEM,
        out_shape=half,
        compiler_params=params(),
        cost_estimate=cost(people * size * k, 2 * people * size),
    )(row, rounded, genotypes)
    return effects, send, keep


def pick_kernel(index, keep, received, mine, other):
    mine[...] = keep[index[0]] + received[index[0]]
    other[...] = keep[1 - index[0]] + received[1 - index[0]]


def pick(index, keep, received):
    half = jax.ShapeDtypeStruct(keep.shape[1:], F32)
    return pl.pallas_call(
        pick_kernel,
        in_specs=[SMEM, VMEM, VMEM],
        out_specs=[VMEM] * 2,
        out_shape=[half] * 2,
        compiler_params=params(),
        cost_estimate=cost(keep.size, 12 * keep.size),
    )(index, keep, received)


def scattered_over(values, axis):
    n = lax.axis_size(axis)
    pieces = values.reshape((n, values.shape[0] // n) + values.shape[1:])
    return jnp.sum(lax.all_to_all(pieces, axis, 0, 0, tiled=True), axis=0)


def routed(block, pairs):
    return lax.ppermute(block, AXES, pairs)


def coefficients(moments, penalty):
    def inner(u, v):
        return sum(a * b * moments[i + j] for i, a in enumerate(u) for j, b in enumerate(v))

    n0 = moments[0]
    a0 = n0 / (moments[1] + penalty * n0)
    r1 = [1.0 - a0 * penalty, -a0]
    n1 = inner(r1, r1)
    b0 = n1 / n0
    d1 = [r1[0] + b0, r1[1]]
    ad1 = [penalty * d1[0], d1[0] + penalty * d1[1], d1[1]]
    a1 = n1 / inner(d1, ad1)
    e1 = [a0 + a1 * d1[0], a1 * d1[1]]
    r2 = [r1[0] - a1 * ad1[0], r1[1] - a1 * ad1[1], -a1 * ad1[2]]
    n2 = inner(r2, r2)
    b1 = n2 / n1
    d2 = [r2[0] + b1 * d1[0], r2[1] + b1 * d1[1], r2[2]]
    ad2 = [penalty * d2[0], d2[0] + penalty * d2[1], d2[1] + penalty * d2[2], d2[2]]
    a2 = n2 / inner(d2, ad2)
    return e1[0] + a2 * d2[0], e1[1] + a2 * d2[1], a2 * d2[2]


def swapped(block, bit):
    return routed(block, [(i, i ^ bit) for i in range(lax.axis_size(AXES))])


def body(marginal, penalty, ld_diag, ld_low, band, genotypes):
    n = lax.axis_size(AXES)
    rows, cols = lax.axis_size("row"), lax.axis_size("col")
    position = lax.axis_index(AXES)
    row = lax.axis_index("row")
    flags = jnp.stack([jnp.logical_and(band[0] >= d, position >= d) for d in (1, 2)]).astype(jnp.int32)
    odd = (position % 2).astype(jnp.int32)[None]
    half = marginal.shape[0] // 2

    def halos(vec, two, products, own_product):
        one_a, one_b, far_a, far_b, after = products
        pair_a, pair_b = swapped(one_a, 1), swapped(one_b, 1)
        sum_a = relay(odd, far_a, pair_a, after)
        up_a = shifted(sum_a, -2)
        chosen_a, chosen_b = choose(odd, vec, two, sum_a)
        one_a, one_b = swapped(chosen_a, 1), swapped(chosen_b, 1)
        sum_b = relay(odd, far_b, pair_b, chosen_b)
        up_b = shifted(sum_b, -2)
        return own_product(sum_b), (one_a, one_b, up_a, up_b, pair_a, pair_b)

    v0 = marginal
    two = shifted(v0, 2)
    products = first_coupling(flags, v0, ld_low[0])
    low = narrowed(flags, ld_low[0], products[0])
    diag = []

    def first_own(after):
        narrow, product = first_diag(v0, ld_diag[0], after)
        diag.append(narrow)
        return product

    own, arrived = halos(v0, two, (*products, low), first_own)
    diag = diag[0]
    v1, _ = finish(odd, add_two(own, low, two), low, *arrived)

    two = shifted(v1, 2)
    products = coupling(v1, low)
    own, arrived = halos(v1, two, (*products, products[3]), lambda after: diag_times(v1, diag, after))
    v2, upper = finish(odd, add_two(own, low, two), low, *arrived)

    two = shifted(upper, 2)
    one, far = lower_coupling(v2, low)
    pair = swapped(one, 1)
    above = relay(odd, far, pair, far)
    up = shifted(above, -2)
    chosen_a, chosen_b = choose(odd, upper, two, above)
    moments = own_moments(v0, v1, v2, diag, chosen_b)
    one_a, one_b = swapped(chosen_a, 1), swapped(chosen_b, 1)
    moments = last(odd, low, one_a, one_b, two, v2, up, pair, moments)
    pieces = lax.all_to_all(jnp.broadcast_to(moments[None], (n,) + moments.shape), AXES, 0, 0, tiled=True)

    effects, send, keep = partial_scores(row.astype(jnp.int32)[None], rows, pieces, penalty[None], v0, v1, v2, genotypes)
    received = swapped(send, cols)
    bit = rows // 4
    while bit:
        mine = (row // (2 * bit)) % 2
        keep = keep.reshape((2, -1) + keep.shape[1:])
        received = received.reshape((2, -1) + received.shape[1:])

        keep, send = pick(mine.astype(jnp.int32)[None], keep, received)
        received = swapped(send, 2 * bit * cols)
        bit //= 2
    return effects, scattered_over((keep + received)[0], "col")


def solution(mesh):
    placed = (
        P(AXES, None),
        P(),
        P(AXES, None, None),
        P(AXES, None, None, None),
        P(AXES),
        P(None, AXES),
    )
    return jax.shard_map(
        body,
        mesh=mesh,
        in_specs=placed,
        out_specs=(P(AXES, None), P(AXES, None)),
        check_vma=False,
    )
```

```python
import functools

import jax
import jax.numpy as jnp
from jax import lax
from jax.experimental import pallas as pl
from jax.experimental.pallas import tpu as pltpu
from jax.sharding import PartitionSpec as P

AXES = ("row", "col")
F32 = jnp.float32
BF16 = jnp.bfloat16
MIB = 1024 * 1024
VMEM = pl.BlockSpec(memory_space=pltpu.VMEM)
SMEM = pl.BlockSpec(memory_space=pltpu.SMEM)
ANY = pl.BlockSpec(memory_space=pl.ANY)


def params(mib=20):
    return pltpu.CompilerParams(vmem_limit_bytes=mib * MIB)


def cost(flops, num_bytes):
    return pl.CostEstimate(flops=int(flops), bytes_accessed=int(num_bytes), transcendentals=0)


def shifted(block, distance):
    n = lax.axis_size(AXES)
    route = [(i - distance, i) for i in range(n) if 0 <= i - distance < n]
    return lax.ppermute(block, AXES, route)


def active(d, site):
    return jnp.logical_and(site[0] >= d + 1, site[1] >= d + 1)


def first_coupling_kernel(d, site, vec, low, product, own, tiles, arrived):
    size = own.shape[0]
    chunks = tiles.shape[0]
    rows = size // chunks
    fetch = pltpu.make_async_copy(vec, own, arrived.at[chunks])
    fetch.start()
    copies = []
    for c in range(chunks):
        copies.append(pltpu.make_async_copy(low.at[d, pl.ds(c * rows, rows)], tiles.at[c], arrived.at[c]))
        copies[-1].start()
    fetch.wait()
    across = own[...].T.astype(BF16)
    acc = None
    for c in range(chunks):
        copies[c].wait()
        tile = jnp.where(active(d, site), tiles[c], 0.0).astype(BF16)
        term = jnp.dot(across[:, c * rows : (c + 1) * rows], tile, preferred_element_type=F32)
        acc = term if acc is None else acc + term
    product[...] = acc.T


def first_coupling(d, site, vec, low):
    size, k = vec.shape
    chunks = 4
    return pl.pallas_call(
        functools.partial(first_coupling_kernel, d),
        in_specs=[SMEM] + [pl.BlockSpec(memory_space=pltpu.HBM)] * 2,
        out_specs=VMEM,
        out_shape=jax.ShapeDtypeStruct((size, k), F32),
        scratch_shapes=[
            pltpu.VMEM((size, k), F32),
            pltpu.VMEM((chunks, size // chunks, size), F32),
            pltpu.SemaphoreType.DMA((chunks + 1,)),
        ],
        compiler_params=params(58),
        cost_estimate=cost(2 * size * size * k, 4 * size * size),
    )(site, vec, low)


def narrow_kernel(site, low, after, out):
    out[0] = jnp.where(active(pl.program_id(0), site), low[0], 0.0).astype(BF16)


def narrowed(site, low, after):
    count, size, _ = low.shape
    rows = size // 2
    block = pl.BlockSpec((1, rows, size), lambda d, r: (d, r, 0))
    return pl.pallas_call(
        narrow_kernel,
        grid=(count, size // rows),
        in_specs=[SMEM, block, ANY],
        out_specs=block,
        out_shape=jax.ShapeDtypeStruct(low.shape, BF16),
        compiler_params=params(),
        cost_estimate=cost(2 * size * size, 12 * size * size),
    )(site, low, after)


def coupling_kernel(vec, low, one, far):
    across = vec[...].T.astype(BF16)
    one[...] = jnp.dot(across, low[0], preferred_element_type=F32).T
    far[...] = jnp.dot(across, low[1], preferred_element_type=F32).T


def coupling(vec, low):
    size, k = vec.shape
    return pl.pallas_call(
        coupling_kernel,
        in_specs=[VMEM, VMEM],
        out_specs=[VMEM] * 2,
        out_shape=[jax.ShapeDtypeStruct((size, k), F32)] * 2,
        compiler_params=params(),
        cost_estimate=cost(4 * size * size * k, 4 * size * size),
    )(vec, low)


def relay_kernel(odd, far, pair, after, out):
    out[...] = far[...] + jnp.where(odd[0] > 0, pair[...], 0.0)


def choose_kernel(odd, vec, two, after, *parts):
    rows = parts[0].shape[0]
    for place, part in enumerate(parts):
        here = slice(place * rows, (place + 1) * rows)
        part[...] = jnp.where(odd[0] > 0, two[here], vec[here])


def choose(odd, vec, two, after, parts):
    rows, k = vec.shape
    return pl.pallas_call(
        choose_kernel,
        in_specs=[SMEM, VMEM, VMEM, ANY],
        out_specs=[VMEM] * parts,
        out_shape=[jax.ShapeDtypeStruct((rows // parts, k), F32)] * parts,
        compiler_params=params(),
        cost_estimate=cost(vec.size, 12 * vec.size),
    )(odd, vec, two, after)


def relay(odd, far, pair, after):
    return pl.pallas_call(
        relay_kernel,
        in_specs=[SMEM, VMEM, VMEM, ANY],
        out_specs=VMEM,
        out_shape=jax.ShapeDtypeStruct(far.shape, F32),
        compiler_params=params(),
        cost_estimate=cost(far.size, 12 * far.size),
    )(odd, far, pair, after)


def first_diag_kernel(vec, diag, after, narrow, product):
    tile = diag[...].astype(BF16)
    narrow[...] = tile
    product[...] = jnp.dot(tile, vec[...].astype(BF16), preferred_element_type=F32)


def first_diag(vec, diag, after):
    size, k = vec.shape
    rows = size // 4
    return pl.pallas_call(
        first_diag_kernel,
        grid=(4,),
        in_specs=[pl.BlockSpec((size, k), lambda r: (0, 0)), pl.BlockSpec((rows, size), lambda r: (r, 0)), ANY],
        out_specs=[pl.BlockSpec((rows, size), lambda r: (r, 0)), pl.BlockSpec((rows, k), lambda r: (r, 0))],
        out_shape=[jax.ShapeDtypeStruct(diag.shape, BF16), jax.ShapeDtypeStruct(vec.shape, F32)],
        compiler_params=params(),
        cost_estimate=cost(2 * size * size * k, 6 * size * size),
    )(vec, diag, after)


def diag_kernel(vec, diag, after, product):
    product[...] = jnp.dot(diag[...], vec[...].astype(BF16), preferred_element_type=F32)


def diag_times(vec, diag, after):
    size, k = vec.shape
    return pl.pallas_call(
        diag_kernel,
        in_specs=[VMEM, VMEM, ANY],
        out_specs=VMEM,
        out_shape=jax.ShapeDtypeStruct(vec.shape, F32),
        compiler_params=params(),
        cost_estimate=cost(2 * size * size * k, 6 * size * size),
    )(vec, diag, after)


def finish_kernel(odd, part, low, one, ahead, pair, out, upper):
    acc = jnp.dot(low[0], one[...].astype(BF16), preferred_element_type=F32) + part[...]
    out[...] = acc + ahead[...] + jnp.where(odd[0] > 0, 0.0, pair[...])
    upper[...] = out[: upper.shape[0]]


def finish(odd, part, low, one, ahead, pair):
    size, k = part.shape
    return pl.pallas_call(
        finish_kernel,
        in_specs=[SMEM] + [VMEM] * 5,
        out_specs=[VMEM] * 2,
        out_shape=[jax.ShapeDtypeStruct(part.shape, F32), jax.ShapeDtypeStruct((size // 2, k), F32)],
        compiler_params=params(),
        cost_estimate=cost(2 * size * size * k, 2 * size * size),
    )(odd, part, low, one, ahead, pair)


def two_kernel(own, low, two, product):
    product[...] = own[...] + jnp.dot(low[1], two[...].astype(BF16), preferred_element_type=F32)


def add_two(own, low, two):
    size, k = two.shape
    return pl.pallas_call(
        two_kernel,
        in_specs=[VMEM] * 3,
        out_specs=VMEM,
        out_shape=jax.ShapeDtypeStruct(two.shape, F32),
        compiler_params=params(),
        cost_estimate=cost(2 * size * size * k, 2 * size * size),
    )(own, low, two)


def lower_kernel(vec, low, one, far):
    across = vec[...].T.astype(BF16)
    half = one.shape[0]
    one[...] = jnp.dot(across, low[0, :, half:], preferred_element_type=F32).T
    far[...] = jnp.dot(across, low[1, :, half:], preferred_element_type=F32).T


def lower_coupling(vec, low):
    size, k = vec.shape
    return pl.pallas_call(
        lower_kernel,
        in_specs=[VMEM, VMEM],
        out_specs=[VMEM] * 2,
        out_shape=[jax.ShapeDtypeStruct((size // 2, k), F32)] * 2,
        compiler_params=params(),
        cost_estimate=cost(2 * size * size * k, 2 * size * size),
    )(vec, low)


def own_kernel(v0, v1, v2, diag, after, moments):
    image = jnp.dot(diag[...], v2[...].astype(BF16), preferred_element_type=F32)
    pairs = [(v0, v0), (v0, v1), (v1, v1), (v1, v2), (v2, v2)]
    for row, (a, b) in enumerate(pairs):
        moments[row : row + 1] = jnp.sum(a[...] * b[...], axis=0, keepdims=True)
    moments[5:6] = jnp.sum(v2[...] * image, axis=0, keepdims=True)
    moments[6:8] = jnp.zeros_like(moments[6:8])


def own_moments(v0, v1, v2, diag, after):
    size, k = v0.shape
    return pl.pallas_call(
        own_kernel,
        in_specs=[VMEM] * 4 + [ANY],
        out_specs=VMEM,
        out_shape=jax.ShapeDtypeStruct((8, k), F32),
        compiler_params=params(),
        cost_estimate=cost(2 * size * size * k, 6 * size * size),
    )(v0, v1, v2, diag, after)


def last_kernel(odd, low, one_a, one_b, two, v2, up, pair, moments, out):
    quarter, half = one_a.shape[0], two.shape[0]
    below = jnp.dot(low[1, :, :half], two[...].astype(BF16), preferred_element_type=F32)
    below = below + jnp.dot(low[0, :, :quarter], one_a[...].astype(BF16), preferred_element_type=F32)
    below = below + jnp.dot(low[0, :, quarter:half], one_b[...].astype(BF16), preferred_element_type=F32)
    above = up[...] + jnp.where(odd[0] > 0, 0.0, pair[...])
    coupled = jnp.sum(v2[...] * below, axis=0, keepdims=True) + jnp.sum(v2[half:] * above, axis=0, keepdims=True)
    out[...] = moments[...]
    out[5:6] = moments[5:6] + 2.0 * coupled


def last(odd, low, one_a, one_b, two, v2, up, pair, moments):
    size, k = v2.shape
    return pl.pallas_call(
        last_kernel,
        in_specs=[SMEM] + [VMEM] * 8,
        out_specs=VMEM,
        out_shape=jax.ShapeDtypeStruct((8, k), F32),
        compiler_params=params(),
        cost_estimate=cost(2 * size * size * k, 2 * size * size),
    )(odd, low, one_a, one_b, two, v2, up, pair, moments)


def group_rows(genotypes, groups, group):
    rows = genotypes.shape[0] // groups
    return genotypes[pl.ds(pl.multiple_of(group * rows, rows), rows)]


def send_kernel(groups, row, pieces, penalty, v0, v1, v2, genotypes, effects, rounded, send):
    sums = pieces[0]
    for piece in range(1, pieces.shape[0]):
        sums = sums + pieces[piece]
    moments = [sums[m : m + 1] for m in range(6)]
    c0, c1, c2 = coefficients(moments, penalty[...])
    value = c0 * v0[...] + c1 * v1[...] + c2 * v2[...]
    effects[...] = value
    narrow = value.astype(BF16)
    rounded[...] = narrow
    other = 1 - row[0] % 2
    for g in range(groups // 2):
        send[g] = jnp.dot(group_rows(genotypes, groups, 2 * g + other), narrow, preferred_element_type=F32)


def keep_kernel(groups, row, rounded, genotypes, keep):
    mine = row[0] % 2
    for g in range(groups // 2):
        keep[g] = jnp.dot(group_rows(genotypes, groups, 2 * g + mine), rounded[...], preferred_element_type=F32)


def partial_scores(row, groups, pieces, penalty, v0, v1, v2, genotypes):
    people, size = genotypes.shape
    k = v0.shape[1]
    half = jax.ShapeDtypeStruct((groups // 2, people // groups, k), F32)
    effects, rounded, send = pl.pallas_call(
        functools.partial(send_kernel, groups),
        in_specs=[SMEM] + [VMEM] * 6,
        out_specs=[VMEM] * 3,
        out_shape=[jax.ShapeDtypeStruct(v0.shape, F32), jax.ShapeDtypeStruct(v0.shape, BF16), half],
        compiler_params=params(),
        cost_estimate=cost(people * size * k, 2 * people * size),
    )(row, pieces, penalty, v0, v1, v2, genotypes)
    keep = pl.pallas_call(
        functools.partial(keep_kernel, groups),
        in_specs=[SMEM, VMEM, VMEM],
        out_specs=VMEM,
        out_shape=half,
        compiler_params=params(),
        cost_estimate=cost(people * size * k, 2 * people * size),
    )(row, rounded, genotypes)
    return effects, send, keep


def pick_kernel(index, keep, received, mine, other):
    mine[...] = keep[index[0]] + received[index[0]]
    other[...] = keep[1 - index[0]] + received[1 - index[0]]


def pick(index, keep, received):
    half = jax.ShapeDtypeStruct(keep.shape[1:], F32)
    return pl.pallas_call(
        pick_kernel,
        in_specs=[SMEM, VMEM, VMEM],
        out_specs=[VMEM] * 2,
        out_shape=[half] * 2,
        compiler_params=params(),
        cost_estimate=cost(keep.size, 12 * keep.size),
    )(index, keep, received)


def scattered_over(values, axis):
    n = lax.axis_size(axis)
    pieces = values.reshape((n, values.shape[0] // n) + values.shape[1:])
    return jnp.sum(lax.all_to_all(pieces, axis, 0, 0, tiled=True), axis=0)


def routed(block, pairs):
    return lax.ppermute(block, AXES, pairs)


def coefficients(moments, penalty):
    def inner(u, v):
        return sum(a * b * moments[i + j] for i, a in enumerate(u) for j, b in enumerate(v))

    n0 = moments[0]
    a0 = n0 / (moments[1] + penalty * n0)
    r1 = [1.0 - a0 * penalty, -a0]
    n1 = inner(r1, r1)
    b0 = n1 / n0
    d1 = [r1[0] + b0, r1[1]]
    ad1 = [penalty * d1[0], d1[0] + penalty * d1[1], d1[1]]
    a1 = n1 / inner(d1, ad1)
    e1 = [a0 + a1 * d1[0], a1 * d1[1]]
    r2 = [r1[0] - a1 * ad1[0], r1[1] - a1 * ad1[1], -a1 * ad1[2]]
    n2 = inner(r2, r2)
    b1 = n2 / n1
    d2 = [r2[0] + b1 * d1[0], r2[1] + b1 * d1[1], r2[2]]
    ad2 = [penalty * d2[0], d2[0] + penalty * d2[1], d2[1] + penalty * d2[2], d2[2]]
    a2 = n2 / inner(d2, ad2)
    return e1[0] + a2 * d2[0], e1[1] + a2 * d2[1], a2 * d2[2]


def swapped(block, bit):
    return routed(block, [(i, i ^ bit) for i in range(lax.axis_size(AXES))])


def body(marginal, penalty, ld_diag, ld_low, band, genotypes):
    n = lax.axis_size(AXES)
    rows, cols = lax.axis_size("row"), lax.axis_size("col")
    position = lax.axis_index(AXES)
    row = lax.axis_index("row")
    site = jnp.stack([band[0], position.astype(jnp.int32)])
    odd = (position % 2).astype(jnp.int32)[None]
    half = marginal.shape[0] // 2

    def halos(vec, two, first, second):
        one = first()
        pair = swapped(one, 1)
        far = second(one)
        [chosen] = choose(odd, vec, two, far, 1)
        total = relay(odd, far, pair, chosen)
        return total, (swapped(chosen, 1), shifted(total, -2), pair)

    v0 = marginal
    two = shifted(v0, 2)

    def second_tile(after):
        vec, _ = lax.optimization_barrier((v0, after))
        return first_coupling(1, site, vec, ld_low[0])

    total, arrived = halos(v0, two, lambda: first_coupling(0, site, v0, ld_low[0]), second_tile)
    low = narrowed(site, ld_low[0], total)
    diag, own = first_diag(v0, ld_diag[0], low)
    v1, _ = finish(odd, add_two(own, low, two), low, *arrived)

    two = shifted(v1, 2)
    one, far = coupling(v1, low)
    total, arrived = halos(v1, two, lambda: one, lambda after: far)
    own = diag_times(v1, diag, total)
    v2, upper = finish(odd, add_two(own, low, two), low, *arrived)

    two = shifted(upper, 2)
    one, far = lower_coupling(v2, low)
    pair = swapped(one, 1)
    above = relay(odd, far, pair, far)
    up = shifted(above, -2)
    chosen_a, chosen_b = choose(odd, upper, two, above, 2)
    moments = own_moments(v0, v1, v2, diag, chosen_b)
    one_a, one_b = swapped(chosen_a, 1), swapped(chosen_b, 1)
    moments = last(odd, low, one_a, one_b, two, v2, up, pair, moments)
    pieces = lax.all_to_all(jnp.broadcast_to(moments[None], (n,) + moments.shape), AXES, 0, 0, tiled=True)

    effects, send, keep = partial_scores(row.astype(jnp.int32)[None], rows, pieces, penalty[None], v0, v1, v2, genotypes)
    received = swapped(send, cols)
    bit = rows // 4
    while bit:
        mine = (row // (2 * bit)) % 2
        keep = keep.reshape((2, -1) + keep.shape[1:])
        received = received.reshape((2, -1) + received.shape[1:])

        keep, send = pick(mine.astype(jnp.int32)[None], keep, received)
        received = swapped(send, 2 * bit * cols)
        bit //= 2
    return effects, scattered_over((keep + received)[0], "col")


def solution(mesh):
    placed = (
        P(AXES, None),
        P(),
        P(AXES, None, None),
        P(AXES, None, None, None),
        P(AXES),
        P(None, AXES),
    )
    return jax.shard_map(
        body,
        mesh=mesh,
        in_specs=placed,
        out_specs=(P(AXES, None), P(AXES, None)),
        check_vma=False,
    )
```

```python
import functools

import jax
import jax.numpy as jnp
from jax import lax
from jax.experimental import pallas as pl
from jax.experimental.pallas import tpu as pltpu
from jax.sharding import PartitionSpec as P

AXES = ("row", "col")
F32 = jnp.float32
BF16 = jnp.bfloat16
MIB = 1024 * 1024
VMEM = pl.BlockSpec(memory_space=pltpu.VMEM)
SMEM = pl.BlockSpec(memory_space=pltpu.SMEM)
ANY = pl.BlockSpec(memory_space=pl.ANY)


def params(mib=20):
    return pltpu.CompilerParams(vmem_limit_bytes=mib * MIB)


def cost(flops, num_bytes):
    return pl.CostEstimate(flops=int(flops), bytes_accessed=int(num_bytes), transcendentals=0)


def shifted(block, distance):
    n = lax.axis_size(AXES)
    route = [(i - distance, i) for i in range(n) if 0 <= i - distance < n]
    return lax.ppermute(block, AXES, route)


def active(d, band, position):
    return jnp.logical_and(band[0] >= d + 1, position[0] >= d + 1)


def split_store(value, first, second):
    half = first.shape[0]
    first[...] = value[:half]
    second[...] = value[half:]


GROUP = 4


def fetched(low, tiles, arrived, order):
    count, rows = tiles.shape[0] // len(order), tiles.shape[1]
    copies = []
    for place in range(tiles.shape[0]):
        source = low.at[order[place // count], pl.ds(place % count * rows, rows)]
        copies.append(pltpu.make_async_copy(source, tiles.at[place], arrived.at[place]))
        copies[-1].start()
    return copies


def rounded_rows(copies, tiles, place, alive):
    for copy in copies[place : place + GROUP]:
        copy.wait()
    tile = tiles[place : place + GROUP].reshape(GROUP * tiles.shape[1], tiles.shape[2])
    return jnp.where(alive, tile, 0.0).astype(BF16)


def first_kernel(band, position, vec, low, one_a, one_b, own, tiles, arrived):
    fetch = pltpu.make_async_copy(vec, own, arrived.at[tiles.shape[0]])
    fetch.start()
    copies = fetched(low, tiles, arrived, (0,))
    fetch.wait()
    across = own[...].T.astype(BF16)
    rows = GROUP * tiles.shape[1]
    acc = None
    for place in range(0, tiles.shape[0], GROUP):
        tile = rounded_rows(copies, tiles, place, active(0, band, position))
        start = place * tiles.shape[1]
        term = jnp.dot(across[:, start : start + rows], tile, preferred_element_type=F32)
        acc = term if acc is None else acc + term
    split_store(acc.T, one_a, one_b)


def second_kernel(band, position, vec, low, far_a, far_b, low_one, low_two, own, tiles, arrived):
    fetch = pltpu.make_async_copy(vec, own, arrived.at[tiles.shape[0]])
    fetch.start()
    copies = fetched(low, tiles, arrived, (1, 0))
    fetch.wait()
    across = own[...].T.astype(BF16)
    rows = GROUP * tiles.shape[1]
    count = tiles.shape[0] // 2
    acc = None
    for place in range(0, count, GROUP):
        tile = rounded_rows(copies, tiles, place, active(1, band, position))
        start = place * tiles.shape[1]
        low_two[start : start + rows] = tile
        term = jnp.dot(across[:, start : start + rows], tile, preferred_element_type=F32)
        acc = term if acc is None else acc + term
    split_store(acc.T, far_a, far_b)
    for place in range(0, count, GROUP):
        start = place * tiles.shape[1]
        low_one[start : start + rows] = rounded_rows(copies, tiles, count + place, active(0, band, position))


def from_tiles(kernel, tiles, narrow, mib, band, position, vec, low):
    size, k = vec.shape
    count = 16
    return pl.pallas_call(
        kernel,
        in_specs=[SMEM] * 2 + [pl.BlockSpec(memory_space=pltpu.HBM)] * 2,
        out_specs=[VMEM] * (2 + narrow),
        out_shape=[jax.ShapeDtypeStruct((size // 2, k), F32)] * 2 + [jax.ShapeDtypeStruct((size, size), BF16)] * narrow,
        scratch_shapes=[
            pltpu.VMEM((size, k), F32),
            pltpu.VMEM((tiles * count, size // count, size), F32),
            pltpu.SemaphoreType.DMA((tiles * count + 1,)),
        ],
        compiler_params=params(mib),
        cost_estimate=cost(2 * size * size * k, 4 * tiles * size * size),
    )(band, position, vec, low)


def coupling_kernel(vec, low_one, low_two, one_a, one_b, far_a, far_b):
    across = vec[...].T.astype(BF16)
    split_store(jnp.dot(across, low_one[...], preferred_element_type=F32).T, one_a, one_b)
    split_store(jnp.dot(across, low_two[...], preferred_element_type=F32).T, far_a, far_b)


def coupling(vec, low_one, low_two):
    size, k = vec.shape
    return pl.pallas_call(
        coupling_kernel,
        in_specs=[VMEM] * 3,
        out_specs=[VMEM] * 4,
        out_shape=[jax.ShapeDtypeStruct((size // 2, k), F32)] * 4,
        compiler_params=params(),
        cost_estimate=cost(4 * size * size * k, 4 * size * size),
    )(vec, low_one, low_two)


def relay_kernel(odd, far, pair, after, out):
    out[...] = far[...] + jnp.where(odd[0] > 0, pair[...], 0.0)


def choose_kernel(odd, vec, two, after, *parts):
    rows = parts[0].shape[0]
    for place, part in enumerate(parts):
        here = slice(place * rows, (place + 1) * rows)
        part[...] = jnp.where(odd[0] > 0, two[here], vec[here])


def choose(odd, vec, two, after, parts):
    rows, k = vec.shape
    return pl.pallas_call(
        choose_kernel,
        in_specs=[SMEM, VMEM, VMEM, ANY],
        out_specs=[VMEM] * parts,
        out_shape=[jax.ShapeDtypeStruct((rows // parts, k), F32)] * parts,
        compiler_params=params(),
        cost_estimate=cost(vec.size, 12 * vec.size),
    )(odd, vec, two, after)


def relay(odd, far, pair, after):
    return pl.pallas_call(
        relay_kernel,
        in_specs=[SMEM, VMEM, VMEM, ANY],
        out_specs=VMEM,
        out_shape=jax.ShapeDtypeStruct(far.shape, F32),
        compiler_params=params(),
        cost_estimate=cost(far.size, 12 * far.size),
    )(odd, far, pair, after)


def first_diag_kernel(vec, diag, after, narrow, product):
    tile = diag[...].astype(BF16)
    narrow[...] = tile
    product[...] = jnp.dot(tile, vec[...].astype(BF16), preferred_element_type=F32)


def first_diag(vec, diag, after):
    size, k = vec.shape
    rows = size // 4
    return pl.pallas_call(
        first_diag_kernel,
        grid=(4,),
        in_specs=[pl.BlockSpec((size, k), lambda r: (0, 0)), pl.BlockSpec((rows, size), lambda r: (r, 0)), ANY],
        out_specs=[pl.BlockSpec((rows, size), lambda r: (r, 0)), pl.BlockSpec((rows, k), lambda r: (r, 0))],
        out_shape=[jax.ShapeDtypeStruct(diag.shape, BF16), jax.ShapeDtypeStruct(vec.shape, F32)],
        compiler_params=params(),
        cost_estimate=cost(2 * size * size * k, 6 * size * size),
    )(vec, diag, after)


def diag_kernel(vec, diag, after, product):
    product[...] = jnp.dot(diag[...], vec[...].astype(BF16), preferred_element_type=F32)


def diag_times(vec, diag, after):
    size, k = vec.shape
    return pl.pallas_call(
        diag_kernel,
        in_specs=[VMEM, VMEM, ANY],
        out_specs=VMEM,
        out_shape=jax.ShapeDtypeStruct(vec.shape, F32),
        compiler_params=params(),
        cost_estimate=cost(2 * size * size * k, 6 * size * size),
    )(vec, diag, after)


def finish_kernel(odd, part, low, one, ahead_a, ahead_b, pair_a, pair_b, out, upper):
    acc = jnp.dot(low[...], one[...].astype(BF16), preferred_element_type=F32) + part[...]
    half = upper.shape[0]
    for place, (straight, pair) in enumerate(((ahead_a, pair_a), (ahead_b, pair_b))):
        rows = slice(place * half, (place + 1) * half)
        out[rows] = acc[rows] + straight[...] + jnp.where(odd[0] > 0, 0.0, pair[...])
    upper[...] = out[:half]


def finish(odd, part, low, *arrived):
    size, k = part.shape
    return pl.pallas_call(
        finish_kernel,
        in_specs=[SMEM] + [VMEM] * 7,
        out_specs=[VMEM] * 2,
        out_shape=[jax.ShapeDtypeStruct(part.shape, F32), jax.ShapeDtypeStruct((size // 2, k), F32)],
        compiler_params=params(),
        cost_estimate=cost(2 * size * size * k, 2 * size * size),
    )(odd, part, low, *arrived)


def two_kernel(own, low, two, product):
    product[...] = own[...] + jnp.dot(low[...], two[...].astype(BF16), preferred_element_type=F32)


def add_two(own, low, two):
    size, k = two.shape
    return pl.pallas_call(
        two_kernel,
        in_specs=[VMEM] * 3,
        out_specs=VMEM,
        out_shape=jax.ShapeDtypeStruct(two.shape, F32),
        compiler_params=params(),
        cost_estimate=cost(2 * size * size * k, 2 * size * size),
    )(own, low, two)


def lower_kernel(vec, low_one, low_two, one, far):
    across = vec[...].T.astype(BF16)
    half = one.shape[0]
    one[...] = jnp.dot(across, low_one[:, half:], preferred_element_type=F32).T
    far[...] = jnp.dot(across, low_two[:, half:], preferred_element_type=F32).T


def lower_coupling(vec, low_one, low_two):
    size, k = vec.shape
    return pl.pallas_call(
        lower_kernel,
        in_specs=[VMEM] * 3,
        out_specs=[VMEM] * 2,
        out_shape=[jax.ShapeDtypeStruct((size // 2, k), F32)] * 2,
        compiler_params=params(),
        cost_estimate=cost(2 * size * size * k, 2 * size * size),
    )(vec, low_one, low_two)


def own_kernel(v0, v1, v2, diag, after, moments):
    image = jnp.dot(diag[...], v2[...].astype(BF16), preferred_element_type=F32)
    pairs = [(v0, v0), (v0, v1), (v1, v1), (v1, v2), (v2, v2)]
    for row, (a, b) in enumerate(pairs):
        moments[row : row + 1] = jnp.sum(a[...] * b[...], axis=0, keepdims=True)
    moments[5:6] = jnp.sum(v2[...] * image, axis=0, keepdims=True)
    moments[6:8] = jnp.zeros_like(moments[6:8])


def own_moments(v0, v1, v2, diag, after):
    size, k = v0.shape
    return pl.pallas_call(
        own_kernel,
        in_specs=[VMEM] * 4 + [ANY],
        out_specs=VMEM,
        out_shape=jax.ShapeDtypeStruct((8, k), F32),
        compiler_params=params(),
        cost_estimate=cost(2 * size * size * k, 6 * size * size),
    )(v0, v1, v2, diag, after)


def last_kernel(odd, low_one, low_two, one_a, one_b, two, v2, up, pair, moments, out):
    quarter, half = one_a.shape[0], two.shape[0]
    below = jnp.dot(low_two[:, :half], two[...].astype(BF16), preferred_element_type=F32)
    below = below + jnp.dot(low_one[:, :quarter], one_a[...].astype(BF16), preferred_element_type=F32)
    below = below + jnp.dot(low_one[:, quarter:half], one_b[...].astype(BF16), preferred_element_type=F32)
    above = up[...] + jnp.where(odd[0] > 0, 0.0, pair[...])
    coupled = jnp.sum(v2[...] * below, axis=0, keepdims=True) + jnp.sum(v2[half:] * above, axis=0, keepdims=True)
    out[...] = moments[...]
    out[5:6] = moments[5:6] + 2.0 * coupled


def last(odd, low_one, low_two, one_a, one_b, two, v2, up, pair, moments):
    size, k = v2.shape
    return pl.pallas_call(
        last_kernel,
        in_specs=[SMEM] + [VMEM] * 9,
        out_specs=VMEM,
        out_shape=jax.ShapeDtypeStruct((8, k), F32),
        compiler_params=params(),
        cost_estimate=cost(2 * size * size * k, 2 * size * size),
    )(odd, low_one, low_two, one_a, one_b, two, v2, up, pair, moments)


def group_rows(genotypes, groups, group):
    rows = genotypes.shape[0] // groups
    return genotypes[pl.ds(pl.multiple_of(group * rows, rows), rows)]


def send_kernel(groups, row, pieces, penalty, v0, v1, v2, genotypes, effects, rounded, send):
    sums = pieces[0]
    for piece in range(1, pieces.shape[0]):
        sums = sums + pieces[piece]
    moments = [sums[m : m + 1] for m in range(6)]
    c0, c1, c2 = coefficients(moments, penalty[...])
    value = c0 * v0[...] + c1 * v1[...] + c2 * v2[...]
    effects[...] = value
    narrow = value.astype(BF16)
    rounded[...] = narrow
    other = 1 - row[0] % 2
    for g in range(groups // 2):
        send[g] = jnp.dot(group_rows(genotypes, groups, 2 * g + other), narrow, preferred_element_type=F32)


def keep_kernel(groups, row, rounded, genotypes, keep):
    mine = row[0] % 2
    for g in range(groups // 2):
        keep[g] = jnp.dot(group_rows(genotypes, groups, 2 * g + mine), rounded[...], preferred_element_type=F32)


def partial_scores(row, groups, pieces, penalty, v0, v1, v2, genotypes):
    people, size = genotypes.shape
    k = v0.shape[1]
    half = jax.ShapeDtypeStruct((groups // 2, people // groups, k), F32)
    effects, rounded, send = pl.pallas_call(
        functools.partial(send_kernel, groups),
        in_specs=[SMEM] + [VMEM] * 6,
        out_specs=[VMEM] * 3,
        out_shape=[jax.ShapeDtypeStruct(v0.shape, F32), jax.ShapeDtypeStruct(v0.shape, BF16), half],
        compiler_params=params(),
        cost_estimate=cost(people * size * k, 2 * people * size),
    )(row, pieces, penalty, v0, v1, v2, genotypes)
    keep = pl.pallas_call(
        functools.partial(keep_kernel, groups),
        in_specs=[SMEM, VMEM, VMEM],
        out_specs=VMEM,
        out_shape=half,
        compiler_params=params(),
        cost_estimate=cost(people * size * k, 2 * people * size),
    )(row, rounded, genotypes)
    return effects, send, keep


def pick_kernel(index, keep, received, mine, other):
    mine[...] = keep[index[0]] + received[index[0]]
    other[...] = keep[1 - index[0]] + received[1 - index[0]]


def pick(index, keep, received):
    half = jax.ShapeDtypeStruct(keep.shape[1:], F32)
    return pl.pallas_call(
        pick_kernel,
        in_specs=[SMEM, VMEM, VMEM],
        out_specs=[VMEM] * 2,
        out_shape=[half] * 2,
        compiler_params=params(),
        cost_estimate=cost(keep.size, 12 * keep.size),
    )(index, keep, received)


def scattered_over(values, axis):
    n = lax.axis_size(axis)
    pieces = values.reshape((n, values.shape[0] // n) + values.shape[1:])
    return jnp.sum(lax.all_to_all(pieces, axis, 0, 0, tiled=True), axis=0)


def routed(block, pairs):
    return lax.ppermute(block, AXES, pairs)


def coefficients(moments, penalty):
    def inner(u, v):
        return sum(a * b * moments[i + j] for i, a in enumerate(u) for j, b in enumerate(v))

    n0 = moments[0]
    a0 = n0 / (moments[1] + penalty * n0)
    r1 = [1.0 - a0 * penalty, -a0]
    n1 = inner(r1, r1)
    b0 = n1 / n0
    d1 = [r1[0] + b0, r1[1]]
    ad1 = [penalty * d1[0], d1[0] + penalty * d1[1], d1[1]]
    a1 = n1 / inner(d1, ad1)
    e1 = [a0 + a1 * d1[0], a1 * d1[1]]
    r2 = [r1[0] - a1 * ad1[0], r1[1] - a1 * ad1[1], -a1 * ad1[2]]
    n2 = inner(r2, r2)
    b1 = n2 / n1
    d2 = [r2[0] + b1 * d1[0], r2[1] + b1 * d1[1], r2[2]]
    ad2 = [penalty * d2[0], d2[0] + penalty * d2[1], d2[1] + penalty * d2[2], d2[2]]
    a2 = n2 / inner(d2, ad2)
    return e1[0] + a2 * d2[0], e1[1] + a2 * d2[1], a2 * d2[2]


def swapped(block, bit):
    return routed(block, [(i, i ^ bit) for i in range(lax.axis_size(AXES))])


def body(marginal, penalty, ld_diag, ld_low, band, genotypes):
    n = lax.axis_size(AXES)
    rows, cols = lax.axis_size("row"), lax.axis_size("col")
    position = lax.axis_index(AXES)
    row = lax.axis_index("row")
    site = position.astype(jnp.int32)[None]
    odd = (position % 2).astype(jnp.int32)[None]
    half = marginal.shape[0] // 2

    def halos(vec, two, first, second):
        one_a, one_b = first()
        pair_a, pair_b = swapped(one_a, 1), swapped(one_b, 1)
        far_a, far_b = second(one_b)
        sum_a = relay(odd, far_a, pair_a, far_b)
        up_a = shifted(sum_a, -2)
        [chosen] = choose(odd, vec, two, sum_a, 1)
        one = swapped(chosen, 1)
        sum_b = relay(odd, far_b, pair_b, chosen)
        return sum_b, (one, up_a, shifted(sum_b, -2), pair_a, pair_b)

    v0 = marginal
    two = shifted(v0, 2)

    lows = []

    def second_tile(after):
        vec, _ = lax.optimization_barrier((v0, after))
        *products, low_one, low_two = from_tiles(second_kernel, 2, 2, 46, band, site, vec, ld_low[0])
        lows.extend((low_one, low_two))
        return products

    last_sum, arrived = halos(
        v0, two, lambda: from_tiles(first_kernel, 1, 0, 58, band, site, v0, ld_low[0]), second_tile
    )
    low_one, low_two = lows
    diag, own = first_diag(v0, ld_diag[0], last_sum)
    v1, _ = finish(odd, add_two(own, low_two, two), low_one, *arrived)

    two = shifted(v1, 2)
    products = coupling(v1, low_one, low_two)
    last_sum, arrived = halos(v1, two, lambda: products[:2], lambda after: products[2:])
    own = diag_times(v1, diag, last_sum)
    v2, upper = finish(odd, add_two(own, low_two, two), low_one, *arrived)

    two = shifted(upper, 2)
    one, far = lower_coupling(v2, low_one, low_two)
    pair = swapped(one, 1)
    above = relay(odd, far, pair, far)
    up = shifted(above, -2)
    chosen_a, chosen_b = choose(odd, upper, two, above, 2)
    moments = own_moments(v0, v1, v2, diag, chosen_b)
    one_a, one_b = swapped(chosen_a, 1), swapped(chosen_b, 1)
    moments = last(odd, low_one, low_two, one_a, one_b, two, v2, up, pair, moments)
    pieces = lax.all_to_all(jnp.broadcast_to(moments[None], (n,) + moments.shape), AXES, 0, 0, tiled=True)

    effects, send, keep = partial_scores(row.astype(jnp.int32)[None], rows, pieces, penalty[None], v0, v1, v2, genotypes)
    received = swapped(send, cols)
    bit = rows // 4
    while bit:
        mine = (row // (2 * bit)) % 2
        keep = keep.reshape((2, -1) + keep.shape[1:])
        received = received.reshape((2, -1) + received.shape[1:])

        keep, send = pick(mine.astype(jnp.int32)[None], keep, received)
        received = swapped(send, 2 * bit * cols)
        bit //= 2
    return effects, scattered_over((keep + received)[0], "col")


def solution(mesh):
    placed = (
        P(AXES, None),
        P(),
        P(AXES, None, None),
        P(AXES, None, None, None),
        P(AXES),
        P(None, AXES),
    )
    return jax.shard_map(
        body,
        mesh=mesh,
        in_specs=placed,
        out_specs=(P(AXES, None), P(AXES, None)),
        check_vma=False,
    )
```

```python
import functools

import jax
import jax.numpy as jnp
from jax import lax
from jax.experimental import pallas as pl
from jax.experimental.pallas import tpu as pltpu
from jax.sharding import PartitionSpec as P

AXES = ("row", "col")
F32 = jnp.float32
BF16 = jnp.bfloat16
MIB = 1024 * 1024
VMEM = pl.BlockSpec(memory_space=pltpu.VMEM)
SMEM = pl.BlockSpec(memory_space=pltpu.SMEM)
ANY = pl.BlockSpec(memory_space=pl.ANY)


def params(mib=20):
    return pltpu.CompilerParams(vmem_limit_bytes=mib * MIB)


def cost(flops, num_bytes):
    return pl.CostEstimate(flops=int(flops), bytes_accessed=int(num_bytes), transcendentals=0)


def shifted(block, distance):
    n = lax.axis_size(AXES)
    route = [(i - distance, i) for i in range(n) if 0 <= i - distance < n]
    return lax.ppermute(block, AXES, route)


def active(d, band, position):
    return jnp.logical_and(band[0] >= d + 1, position[0] >= d + 1)


def split_store(value, first, second):
    half = first.shape[0]
    first[...] = value[:half]
    second[...] = value[half:]


GROUP = 4


def fetched(low, tiles, arrived, order):
    count, rows = tiles.shape[0] // len(order), tiles.shape[1]
    copies = []
    for place in range(tiles.shape[0]):
        source = low.at[order[place // count], pl.ds(place % count * rows, rows)]
        copies.append(pltpu.make_async_copy(source, tiles.at[place], arrived.at[place]))
        copies[-1].start()
    return copies


def rounded_rows(copies, tiles, place, alive):
    for copy in copies[place : place + GROUP]:
        copy.wait()
    tile = tiles[place : place + GROUP].reshape(GROUP * tiles.shape[1], tiles.shape[2])
    return jnp.where(alive, tile, 0.0).astype(BF16)


def first_kernel(band, position, vec, low, one_a, one_b, own, tiles, arrived):
    fetch = pltpu.make_async_copy(vec, own, arrived.at[tiles.shape[0]])
    fetch.start()
    copies = fetched(low, tiles, arrived, (0,))
    fetch.wait()
    across = own[...].T.astype(BF16)
    rows = GROUP * tiles.shape[1]
    acc = None
    for place in range(0, tiles.shape[0], GROUP):
        tile = rounded_rows(copies, tiles, place, active(0, band, position))
        start = place * tiles.shape[1]
        term = jnp.dot(across[:, start : start + rows], tile, preferred_element_type=F32)
        acc = term if acc is None else acc + term
    split_store(acc.T, one_a, one_b)


def second_kernel(band, position, vec, low, far_a, far_b, low_one, low_two, own, tiles, arrived):
    fetch = pltpu.make_async_copy(vec, own, arrived.at[tiles.shape[0]])
    fetch.start()
    copies = fetched(low, tiles, arrived, (1, 0))
    fetch.wait()
    across = own[...].T.astype(BF16)
    rows = GROUP * tiles.shape[1]
    count = tiles.shape[0] // 2
    acc = None
    for place in range(0, count, GROUP):
        tile = rounded_rows(copies, tiles, place, active(1, band, position))
        start = place * tiles.shape[1]
        low_two[start : start + rows] = tile
        term = jnp.dot(across[:, start : start + rows], tile, preferred_element_type=F32)
        acc = term if acc is None else acc + term
    split_store(acc.T, far_a, far_b)
    for place in range(0, count, GROUP):
        start = place * tiles.shape[1]
        low_one[start : start + rows] = rounded_rows(copies, tiles, count + place, active(0, band, position))


def from_tiles(kernel, tiles, narrow, mib, band, position, vec, low):
    size, k = vec.shape
    count = 16
    return pl.pallas_call(
        kernel,
        in_specs=[SMEM] * 2 + [pl.BlockSpec(memory_space=pltpu.HBM)] * 2,
        out_specs=[VMEM] * (2 + narrow),
        out_shape=[jax.ShapeDtypeStruct((size // 2, k), F32)] * 2 + [jax.ShapeDtypeStruct((size, size), BF16)] * narrow,
        scratch_shapes=[
            pltpu.VMEM((size, k), F32),
            pltpu.VMEM((tiles * count, size // count, size), F32),
            pltpu.SemaphoreType.DMA((tiles * count + 1,)),
        ],
        compiler_params=params(mib),
        cost_estimate=cost(2 * size * size * k, 4 * tiles * size * size),
    )(band, position, vec, low)


def coupling_kernel(vec, low_one, low_two, one_a, one_b, far_a, far_b):
    across = vec[...].T.astype(BF16)
    split_store(jnp.dot(across, low_one[...], preferred_element_type=F32).T, one_a, one_b)
    split_store(jnp.dot(across, low_two[...], preferred_element_type=F32).T, far_a, far_b)


def coupling(vec, low_one, low_two):
    size, k = vec.shape
    return pl.pallas_call(
        coupling_kernel,
        in_specs=[VMEM] * 3,
        out_specs=[VMEM] * 4,
        out_shape=[jax.ShapeDtypeStruct((size // 2, k), F32)] * 4,
        compiler_params=params(),
        cost_estimate=cost(4 * size * size * k, 4 * size * size),
    )(vec, low_one, low_two)


def relay_kernel(odd, far, pair, after, out):
    out[...] = far[...] + jnp.where(odd[0] > 0, pair[...], 0.0)


def choose_kernel(odd, vec, two, after, *parts):
    rows = parts[0].shape[0]
    for place, part in enumerate(parts):
        here = slice(place * rows, (place + 1) * rows)
        part[...] = jnp.where(odd[0] > 0, two[here], vec[here])


def choose(odd, vec, two, after, parts):
    rows, k = vec.shape
    return pl.pallas_call(
        choose_kernel,
        in_specs=[SMEM, VMEM, VMEM, ANY],
        out_specs=[VMEM] * parts,
        out_shape=[jax.ShapeDtypeStruct((rows // parts, k), F32)] * parts,
        compiler_params=params(),
        cost_estimate=cost(vec.size, 12 * vec.size),
    )(odd, vec, two, after)


def relay(odd, far, pair, after):
    return pl.pallas_call(
        relay_kernel,
        in_specs=[SMEM, VMEM, VMEM, ANY],
        out_specs=VMEM,
        out_shape=jax.ShapeDtypeStruct(far.shape, F32),
        compiler_params=params(),
        cost_estimate=cost(far.size, 12 * far.size),
    )(odd, far, pair, after)


def first_diag_kernel(vec, diag, after, narrow, product):
    tile = diag[...].astype(BF16)
    narrow[...] = tile
    product[...] = jnp.dot(tile, vec[...].astype(BF16), preferred_element_type=F32)


def first_diag(vec, diag, after):
    size, k = vec.shape
    rows = size // 4
    return pl.pallas_call(
        first_diag_kernel,
        grid=(4,),
        in_specs=[pl.BlockSpec((size, k), lambda r: (0, 0)), pl.BlockSpec((rows, size), lambda r: (r, 0)), ANY],
        out_specs=[pl.BlockSpec((rows, size), lambda r: (r, 0)), pl.BlockSpec((rows, k), lambda r: (r, 0))],
        out_shape=[jax.ShapeDtypeStruct(diag.shape, BF16), jax.ShapeDtypeStruct(vec.shape, F32)],
        compiler_params=params(),
        cost_estimate=cost(2 * size * size * k, 6 * size * size),
    )(vec, diag, after)


def diag_kernel(vec, diag, after, product):
    product[...] = jnp.dot(diag[...], vec[...].astype(BF16), preferred_element_type=F32)


def diag_times(vec, diag, after):
    size, k = vec.shape
    return pl.pallas_call(
        diag_kernel,
        in_specs=[VMEM, VMEM, ANY],
        out_specs=VMEM,
        out_shape=jax.ShapeDtypeStruct(vec.shape, F32),
        compiler_params=params(),
        cost_estimate=cost(2 * size * size * k, 6 * size * size),
    )(vec, diag, after)


def finish_kernel(odd, part, low, one, ahead_a, ahead_b, pair_a, pair_b, out, upper):
    acc = jnp.dot(low[...], one[...].astype(BF16), preferred_element_type=F32) + part[...]
    half = upper.shape[0]
    for place, (straight, pair) in enumerate(((ahead_a, pair_a), (ahead_b, pair_b))):
        rows = slice(place * half, (place + 1) * half)
        out[rows] = acc[rows] + straight[...] + jnp.where(odd[0] > 0, 0.0, pair[...])
    upper[...] = out[:half]


def finish(odd, part, low, *arrived):
    size, k = part.shape
    return pl.pallas_call(
        finish_kernel,
        in_specs=[SMEM] + [VMEM] * 7,
        out_specs=[VMEM] * 2,
        out_shape=[jax.ShapeDtypeStruct(part.shape, F32), jax.ShapeDtypeStruct((size // 2, k), F32)],
        compiler_params=params(),
        cost_estimate=cost(2 * size * size * k, 2 * size * size),
    )(odd, part, low, *arrived)


def two_kernel(own, low, two, product):
    product[...] = own[...] + jnp.dot(low[...], two[...].astype(BF16), preferred_element_type=F32)


def add_two(own, low, two):
    size, k = two.shape
    return pl.pallas_call(
        two_kernel,
        in_specs=[VMEM] * 3,
        out_specs=VMEM,
        out_shape=jax.ShapeDtypeStruct(two.shape, F32),
        compiler_params=params(),
        cost_estimate=cost(2 * size * size * k, 2 * size * size),
    )(own, low, two)


def lower_kernel(vec, low_one, low_two, one, far):
    across = vec[...].T.astype(BF16)
    half = one.shape[0]
    one[...] = jnp.dot(across, low_one[:, half:], preferred_element_type=F32).T
    far[...] = jnp.dot(across, low_two[:, half:], preferred_element_type=F32).T


def lower_coupling(vec, low_one, low_two):
    size, k = vec.shape
    return pl.pallas_call(
        lower_kernel,
        in_specs=[VMEM] * 3,
        out_specs=[VMEM] * 2,
        out_shape=[jax.ShapeDtypeStruct((size // 2, k), F32)] * 2,
        compiler_params=params(),
        cost_estimate=cost(2 * size * size * k, 2 * size * size),
    )(vec, low_one, low_two)


def own_kernel(v0, v1, v2, diag, after, moments):
    image = jnp.dot(diag[...], v2[...].astype(BF16), preferred_element_type=F32)
    pairs = [(v0, v0), (v0, v1), (v1, v1), (v1, v2), (v2, v2)]
    for row, (a, b) in enumerate(pairs):
        moments[row : row + 1] = jnp.sum(a[...] * b[...], axis=0, keepdims=True)
    moments[5:6] = jnp.sum(v2[...] * image, axis=0, keepdims=True)
    moments[6:8] = jnp.zeros_like(moments[6:8])


def own_moments(v0, v1, v2, diag, after):
    size, k = v0.shape
    return pl.pallas_call(
        own_kernel,
        in_specs=[VMEM] * 4 + [ANY],
        out_specs=VMEM,
        out_shape=jax.ShapeDtypeStruct((8, k), F32),
        compiler_params=params(),
        cost_estimate=cost(2 * size * size * k, 6 * size * size),
    )(v0, v1, v2, diag, after)


def last_kernel(odd, low_one, low_two, one_a, one_b, two, v2, up, pair, moments, out):
    quarter, half = one_a.shape[0], two.shape[0]
    below = jnp.dot(low_two[:, :half], two[...].astype(BF16), preferred_element_type=F32)
    below = below + jnp.dot(low_one[:, :quarter], one_a[...].astype(BF16), preferred_element_type=F32)
    below = below + jnp.dot(low_one[:, quarter:half], one_b[...].astype(BF16), preferred_element_type=F32)
    above = up[...] + jnp.where(odd[0] > 0, 0.0, pair[...])
    coupled = jnp.sum(v2[...] * below, axis=0, keepdims=True) + jnp.sum(v2[half:] * above, axis=0, keepdims=True)
    out[...] = moments[...]
    out[5:6] = moments[5:6] + 2.0 * coupled


def last(odd, low_one, low_two, one_a, one_b, two, v2, up, pair, moments):
    size, k = v2.shape
    return pl.pallas_call(
        last_kernel,
        in_specs=[SMEM] + [VMEM] * 9,
        out_specs=VMEM,
        out_shape=jax.ShapeDtypeStruct((8, k), F32),
        compiler_params=params(),
        cost_estimate=cost(2 * size * size * k, 2 * size * size),
    )(odd, low_one, low_two, one_a, one_b, two, v2, up, pair, moments)


def group_rows(genotypes, groups, group):
    rows = genotypes.shape[0] // groups
    return genotypes[pl.ds(pl.multiple_of(group * rows, rows), rows)]


def send_kernel(groups, row, pieces, penalty, v0, v1, v2, genotypes, effects, rounded, send):
    sums = pieces[0]
    for piece in range(1, pieces.shape[0]):
        sums = sums + pieces[piece]
    moments = [sums[m : m + 1] for m in range(6)]
    c0, c1, c2 = coefficients(moments, penalty[...])
    value = c0 * v0[...] + c1 * v1[...] + c2 * v2[...]
    effects[...] = value
    narrow = value.astype(BF16)
    rounded[...] = narrow
    other = 1 - row[0] % 2
    for g in range(groups // 2):
        send[g] = jnp.dot(group_rows(genotypes, groups, 2 * g + other), narrow, preferred_element_type=F32)


def keep_kernel(groups, row, rounded, genotypes, keep):
    mine = row[0] % 2
    for g in range(groups // 2):
        keep[g] = jnp.dot(group_rows(genotypes, groups, 2 * g + mine), rounded[...], preferred_element_type=F32)


def partial_scores(row, groups, pieces, penalty, v0, v1, v2, genotypes):
    people, size = genotypes.shape
    k = v0.shape[1]
    half = jax.ShapeDtypeStruct((groups // 2, people // groups, k), F32)
    effects, rounded, send = pl.pallas_call(
        functools.partial(send_kernel, groups),
        in_specs=[SMEM] + [VMEM] * 6,
        out_specs=[VMEM] * 3,
        out_shape=[jax.ShapeDtypeStruct(v0.shape, F32), jax.ShapeDtypeStruct(v0.shape, BF16), half],
        compiler_params=params(),
        cost_estimate=cost(people * size * k, 2 * people * size),
    )(row, pieces, penalty, v0, v1, v2, genotypes)
    keep = pl.pallas_call(
        functools.partial(keep_kernel, groups),
        in_specs=[SMEM, VMEM, VMEM],
        out_specs=VMEM,
        out_shape=half,
        compiler_params=params(),
        cost_estimate=cost(people * size * k, 2 * people * size),
    )(row, rounded, genotypes)
    return effects, send, keep


def pick_kernel(index, keep, received, mine, other):
    mine[...] = keep[index[0]] + received[index[0]]
    other[...] = keep[1 - index[0]] + received[1 - index[0]]


def pick(index, keep, received):
    half = jax.ShapeDtypeStruct(keep.shape[1:], F32)
    return pl.pallas_call(
        pick_kernel,
        in_specs=[SMEM, VMEM, VMEM],
        out_specs=[VMEM] * 2,
        out_shape=[half] * 2,
        compiler_params=params(),
        cost_estimate=cost(keep.size, 12 * keep.size),
    )(index, keep, received)


def local(kernel, outs, operands, scalars=0, after=None, scratch=()):
    count = len(operands)

    def run(*refs):
        kernel(*refs[:count], *refs[count + (after is not None) :])

    specs = [SMEM] * scalars + [VMEM] * (count - scalars)
    return pl.pallas_call(
        run,
        in_specs=specs + ([ANY] if after is not None else []),
        out_specs=[VMEM] * len(outs),
        out_shape=outs,
        scratch_shapes=scratch,
        compiler_params=params(),
        cost_estimate=cost(1, 1),
    )(*operands, *([after] if after is not None else []))


def reduced_over_chips(site, keep, received):
    cols = lax.axis_size("col")
    rows, k = keep.shape[1] // cols, keep.shape[2]
    deep = cols // 2
    half = deep // 2
    keep, received = [value.reshape(2, deep, 2, rows, k) for value in (keep, received)]

    def shape(*lead):
        return jax.ShapeDtypeStruct((*lead, rows, k), F32)

    def spread_kernel(site, keep, received, a_mine, a_other, b_mine, b_other):
        y, x = site[0], site[1]
        for z in range(half):
            for there in range(2):
                a_mine[z, there] = keep[y, z, there] + received[y, z, there]
                a_other[z, there] = keep[1 - y, z, there] + received[1 - y, z, there]
                b_mine[there, z] = keep[there, half + z, x] + received[there, half + z, x]
                b_other[there, z] = keep[there, half + z, 1 - x] + received[there, half + z, 1 - x]

    def cross_kernel(site, a, a_in, b, b_in, a_mine, a_other, b_mine, b_other):
        y, x = site[0], site[1]
        for z in range(half):
            a_mine[z] = a[z, x] + a_in[z, x]
            a_other[z] = a[z, 1 - x] + a_in[z, 1 - x]
            b_mine[z] = b[y, z] + b_in[y, z]
            b_other[z] = b[1 - y, z] + b_in[1 - y, z]

    def along_kernel(site, a, a_in, b, b_in, mine, *rest):
        *others, total = rest
        total[:half] = a[...] + a_in[...]
        total[half:] = b[...] + b_in[...]
        mine[...] = total[site[2]]
        for step, other in enumerate(others):
            other[...] = total[jnp.bitwise_xor(site[2], step + 1)]

    outs = [shape(half, 2)] * 2 + [shape(2, half)] * 2
    a, a_other, b, b_other = local(spread_kernel, outs, [site, keep, received], 1)
    a_in, b_in = swapped(a_other, 2 * cols), swapped(b_other, 1)
    a, a_other, b, b_other = local(cross_kernel, [shape(half)] * 4, [site, a, a_in, b, b_in], 1)
    a_in, b_in = swapped(a_other, 1), swapped(b_other, 2 * cols)
    scratch = [pltpu.VMEM((deep, rows, k), F32)]
    mine, *others = local(along_kernel, [shape()] * deep, [site, a, a_in, b, b_in], 1, scratch=scratch)
    for step, other in enumerate(others):
        mine = mine + swapped(other, 2 * (step + 1))
    return mine


def routed(block, pairs):
    return lax.ppermute(block, AXES, pairs)


def coefficients(moments, penalty):
    def inner(u, v):
        return sum(a * b * moments[i + j] for i, a in enumerate(u) for j, b in enumerate(v))

    n0 = moments[0]
    a0 = n0 / (moments[1] + penalty * n0)
    r1 = [1.0 - a0 * penalty, -a0]
    n1 = inner(r1, r1)
    b0 = n1 / n0
    d1 = [r1[0] + b0, r1[1]]
    ad1 = [penalty * d1[0], d1[0] + penalty * d1[1], d1[1]]
    a1 = n1 / inner(d1, ad1)
    e1 = [a0 + a1 * d1[0], a1 * d1[1]]
    r2 = [r1[0] - a1 * ad1[0], r1[1] - a1 * ad1[1], -a1 * ad1[2]]
    n2 = inner(r2, r2)
    b1 = n2 / n1
    d2 = [r2[0] + b1 * d1[0], r2[1] + b1 * d1[1], r2[2]]
    ad2 = [penalty * d2[0], d2[0] + penalty * d2[1], d2[1] + penalty * d2[2], d2[2]]
    a2 = n2 / inner(d2, ad2)
    return e1[0] + a2 * d2[0], e1[1] + a2 * d2[1], a2 * d2[2]


def swapped(block, bit):
    return routed(block, [(i, i ^ bit) for i in range(lax.axis_size(AXES))])


def body(marginal, penalty, ld_diag, ld_low, band, genotypes):
    n = lax.axis_size(AXES)
    rows, cols = lax.axis_size("row"), lax.axis_size("col")
    position = lax.axis_index(AXES)
    row = lax.axis_index("row")
    site = position.astype(jnp.int32)[None]
    odd = (position % 2).astype(jnp.int32)[None]
    half = marginal.shape[0] // 2

    def halos(vec, two, first, second):
        one_a, one_b = first()
        pair_a, pair_b = swapped(one_a, 1), swapped(one_b, 1)
        far_a, far_b = second(one_b)
        sum_a = relay(odd, far_a, pair_a, far_b)
        up_a = shifted(sum_a, -2)
        [chosen] = choose(odd, vec, two, sum_a, 1)
        one = swapped(chosen, 1)
        sum_b = relay(odd, far_b, pair_b, chosen)
        return sum_b, (one, up_a, shifted(sum_b, -2), pair_a, pair_b)

    v0 = marginal
    two = shifted(v0, 2)

    lows = []

    def second_tile(after):
        vec, _ = lax.optimization_barrier((v0, after))
        *products, low_one, low_two = from_tiles(second_kernel, 2, 2, 46, band, site, vec, ld_low[0])
        lows.extend((low_one, low_two))
        return products

    last_sum, arrived = halos(
        v0, two, lambda: from_tiles(first_kernel, 1, 0, 58, band, site, v0, ld_low[0]), second_tile
    )
    low_one, low_two = lows
    diag, own = first_diag(v0, ld_diag[0], last_sum)
    v1, _ = finish(odd, add_two(own, low_two, two), low_one, *arrived)

    two = shifted(v1, 2)
    products = coupling(v1, low_one, low_two)
    last_sum, arrived = halos(v1, two, lambda: products[:2], lambda after: products[2:])
    own = diag_times(v1, diag, last_sum)
    v2, upper = finish(odd, add_two(own, low_two, two), low_one, *arrived)

    two = shifted(upper, 2)
    one, far = lower_coupling(v2, low_one, low_two)
    pair = swapped(one, 1)
    above = relay(odd, far, pair, far)
    up = shifted(above, -2)
    chosen_a, chosen_b = choose(odd, upper, two, above, 2)
    moments = own_moments(v0, v1, v2, diag, chosen_b)
    one_a, one_b = swapped(chosen_a, 1), swapped(chosen_b, 1)
    moments = last(odd, low_one, low_two, one_a, one_b, two, v2, up, pair, moments)
    pieces = lax.all_to_all(jnp.broadcast_to(moments[None], (n,) + moments.shape), AXES, 0, 0, tiled=True)

    effects, send, keep = partial_scores(row.astype(jnp.int32)[None], rows, pieces, penalty[None], v0, v1, v2, genotypes)
    received = swapped(send, cols)
    bit = rows // 4
    while bit > 1:
        keep, received = [value.reshape((2, -1) + value.shape[1:]) for value in (keep, received)]
        keep, send = pick((row // (2 * bit) % 2).astype(jnp.int32)[None], keep, received)
        received = swapped(send, 2 * bit * cols)
        bit //= 2
    col = lax.axis_index("col")
    chip = jnp.stack([row // 2 % 2, col % 2, col // 2]).astype(jnp.int32)
    return effects, reduced_over_chips(chip, keep, received)


def solution(mesh):
    placed = (
        P(AXES, None),
        P(),
        P(AXES, None, None),
        P(AXES, None, None, None),
        P(AXES),
        P(None, AXES),
    )
    return jax.shard_map(
        body,
        mesh=mesh,
        in_specs=placed,
        out_specs=(P(AXES, None), P(AXES, None)),
        check_vma=False,
    )
```

```python
import functools

import jax
import jax.numpy as jnp
from jax import lax
from jax.experimental import pallas as pl
from jax.experimental.pallas import tpu as pltpu
from jax.sharding import PartitionSpec as P

AXES = ("row", "col")
F32 = jnp.float32
BF16 = jnp.bfloat16
MIB = 1024 * 1024
VMEM = pl.BlockSpec(memory_space=pltpu.VMEM)
SMEM = pl.BlockSpec(memory_space=pltpu.SMEM)
ANY = pl.BlockSpec(memory_space=pl.ANY)


def params(mib=20):
    return pltpu.CompilerParams(vmem_limit_bytes=mib * MIB)


def cost(flops, num_bytes):
    return pl.CostEstimate(flops=int(flops), bytes_accessed=int(num_bytes), transcendentals=0)


def shifted(block, distance):
    n = lax.axis_size(AXES)
    route = [(i - distance, i) for i in range(n) if 0 <= i - distance < n]
    return lax.ppermute(block, AXES, route)


def active(d, band, position):
    return jnp.logical_and(band[0] >= d + 1, position[0] >= d + 1)


def split(size):
    return size * 65 // 128, size - size * 65 // 128


def split_store(value, first, second):
    half = first.shape[0]
    first[...] = value[:half]
    second[...] = value[half:]


GROUP = 4


def fetched(low, tiles, arrived, order):
    count, rows = tiles.shape[0] // len(order), tiles.shape[1]
    copies = []
    for place in range(tiles.shape[0]):
        source = low.at[order[place // count], pl.ds(place % count * rows, rows)]
        copies.append(pltpu.make_async_copy(source, tiles.at[place], arrived.at[place]))
        copies[-1].start()
    return copies


def rounded_rows(copies, tiles, place, alive):
    for copy in copies[place : place + GROUP]:
        copy.wait()
    tile = tiles[place : place + GROUP].reshape(GROUP * tiles.shape[1], tiles.shape[2])
    return jnp.where(alive, tile, 0.0).astype(BF16)


def first_kernel(band, position, vec, low, one_a, one_b, own, tiles, arrived):
    fetch = pltpu.make_async_copy(vec, own, arrived.at[tiles.shape[0]])
    fetch.start()
    copies = fetched(low, tiles, arrived, (0,))
    fetch.wait()
    across = own[...].T.astype(BF16)
    rows = GROUP * tiles.shape[1]
    acc = None
    for place in range(0, tiles.shape[0], GROUP):
        tile = rounded_rows(copies, tiles, place, active(0, band, position))
        start = place * tiles.shape[1]
        term = jnp.dot(across[:, start : start + rows], tile, preferred_element_type=F32)
        acc = term if acc is None else acc + term
    split_store(acc.T, one_a, one_b)


def second_kernel(band, position, vec, low, far_a, far_b, low_one, low_two, own, tiles, arrived):
    fetch = pltpu.make_async_copy(vec, own, arrived.at[tiles.shape[0]])
    fetch.start()
    copies = fetched(low, tiles, arrived, (1, 0))
    fetch.wait()
    across = own[...].T.astype(BF16)
    rows = GROUP * tiles.shape[1]
    count = tiles.shape[0] // 2
    acc = None
    for place in range(0, count, GROUP):
        tile = rounded_rows(copies, tiles, place, active(1, band, position))
        start = place * tiles.shape[1]
        low_two[start : start + rows] = tile
        term = jnp.dot(across[:, start : start + rows], tile, preferred_element_type=F32)
        acc = term if acc is None else acc + term
    split_store(acc.T, far_a, far_b)
    for place in range(0, count, GROUP):
        start = place * tiles.shape[1]
        low_one[start : start + rows] = rounded_rows(copies, tiles, count + place, active(0, band, position))


def from_tiles(kernel, tiles, narrow, mib, band, position, vec, low):
    size, k = vec.shape
    count = 16
    return pl.pallas_call(
        kernel,
        in_specs=[SMEM] * 2 + [pl.BlockSpec(memory_space=pltpu.HBM)] * 2,
        out_specs=[VMEM] * (2 + narrow),
        out_shape=[jax.ShapeDtypeStruct((size // 2, k), F32)] * 2 + [jax.ShapeDtypeStruct((size, size), BF16)] * narrow,
        scratch_shapes=[
            pltpu.VMEM((size, k), F32),
            pltpu.VMEM((tiles * count, size // count, size), F32),
            pltpu.SemaphoreType.DMA((tiles * count + 1,)),
        ],
        compiler_params=params(mib),
        cost_estimate=cost(2 * size * size * k, 4 * tiles * size * size),
    )(band, position, vec, low)


def coupling_kernel(vec, low_one, low_two, one_a, one_b, far_a, far_b):
    across = vec[...].T.astype(BF16)
    split_store(jnp.dot(across, low_one[...], preferred_element_type=F32).T, one_a, one_b)
    split_store(jnp.dot(across, low_two[...], preferred_element_type=F32).T, far_a, far_b)


def coupling(vec, low_one, low_two):
    size, k = vec.shape
    return pl.pallas_call(
        coupling_kernel,
        in_specs=[VMEM] * 3,
        out_specs=[VMEM] * 4,
        out_shape=[jax.ShapeDtypeStruct((rows, k), F32) for rows in split(size) * 2],
        compiler_params=params(),
        cost_estimate=cost(4 * size * size * k, 4 * size * size),
    )(vec, low_one, low_two)


def relay_kernel(odd, far, pair, after, out):
    out[...] = far[...] + jnp.where(odd[0] > 0, pair[...], 0.0)


def choose(odd, vec, two, after, parts):
    rows, k = vec.shape
    most = -(-rows // (8 * parts)) * 8

    def kernel(odd, vec, *refs):
        arrived, outs = refs[: len(two)], refs[len(two) + 1 :]
        value = [part[...] for part in arrived]
        value = value[0] if len(value) == 1 else jnp.concatenate(value, axis=0)
        value = jnp.where(odd[0] > 0, value, vec[...])
        start = 0
        for out in outs:
            out[...] = value[start : start + out.shape[0]]
            start += out.shape[0]

    return pl.pallas_call(
        kernel,
        in_specs=[SMEM] + [VMEM] * (1 + len(two)) + [ANY],
        out_specs=[VMEM] * parts,
        out_shape=[jax.ShapeDtypeStruct((min(most, rows - most * place), k), F32) for place in range(parts)],
        compiler_params=params(),
        cost_estimate=cost(vec.size, 12 * vec.size),
    )(odd, vec, *two, after)


def relay(odd, far, pair, after):
    return pl.pallas_call(
        relay_kernel,
        in_specs=[SMEM, VMEM, VMEM, ANY],
        out_specs=VMEM,
        out_shape=jax.ShapeDtypeStruct(far.shape, F32),
        compiler_params=params(),
        cost_estimate=cost(far.size, 12 * far.size),
    )(odd, far, pair, after)


def first_diag_kernel(vec, diag, after, narrow, product):
    tile = diag[...].astype(BF16)
    narrow[...] = tile
    product[...] = jnp.dot(tile, vec[...].astype(BF16), preferred_element_type=F32)


def first_diag(vec, diag, after):
    size, k = vec.shape
    rows = size // 4
    return pl.pallas_call(
        first_diag_kernel,
        grid=(4,),
        in_specs=[pl.BlockSpec((size, k), lambda r: (0, 0)), pl.BlockSpec((rows, size), lambda r: (r, 0)), ANY],
        out_specs=[pl.BlockSpec((rows, size), lambda r: (r, 0)), pl.BlockSpec((rows, k), lambda r: (r, 0))],
        out_shape=[jax.ShapeDtypeStruct(diag.shape, BF16), jax.ShapeDtypeStruct(vec.shape, F32)],
        compiler_params=params(),
        cost_estimate=cost(2 * size * size * k, 6 * size * size),
    )(vec, diag, after)


def diag_kernel(vec, diag, after, product):
    product[...] = jnp.dot(diag[...], vec[...].astype(BF16), preferred_element_type=F32)


def diag_times(vec, diag, after):
    size, k = vec.shape
    return pl.pallas_call(
        diag_kernel,
        in_specs=[VMEM, VMEM, ANY],
        out_specs=VMEM,
        out_shape=jax.ShapeDtypeStruct(vec.shape, F32),
        compiler_params=params(),
        cost_estimate=cost(1, 1),
    )(vec, diag, after)


def matched(low, parts):
    values = [part[...] for part in parts]
    value = values[0] if len(values) == 1 else jnp.concatenate(values, axis=0)
    return jnp.dot(low[...], value.astype(BF16), preferred_element_type=F32)


def finish_kernel(odd, part, low, ahead_a, ahead_b, pair_a, pair_b, *rest):
    *ones, out, upper, lower = rest
    acc = matched(low, ones) + part[...]
    start = 0
    for straight, pair in ((ahead_a, pair_a), (ahead_b, pair_b)):
        rows = slice(start, start + pair.shape[0])
        out[rows] = acc[rows] + straight[...] + jnp.where(odd[0] > 0, 0.0, pair[...])
        start += pair.shape[0]
    half = upper.shape[0]
    upper[...] = out[:half]
    lower[...] = out[half:]


def finish(odd, part, low, *arrived):
    size, k = part.shape
    return pl.pallas_call(
        finish_kernel,
        in_specs=[SMEM] + [VMEM] * (2 + len(arrived)),
        out_specs=[VMEM] * 3,
        out_shape=[jax.ShapeDtypeStruct(part.shape, F32), *[jax.ShapeDtypeStruct((size // 2, k), F32)] * 2],
        compiler_params=params(),
        cost_estimate=cost(1, 1),
    )(odd, part, low, *arrived)


def add_two(own, low, two):
    size, k = own.shape

    def kernel(own, low, *refs):
        *parts, product = refs
        product[...] = own[...] + matched(low, parts)

    return pl.pallas_call(
        kernel,
        in_specs=[VMEM] * (2 + len(two)),
        out_specs=VMEM,
        out_shape=jax.ShapeDtypeStruct(own.shape, F32),
        compiler_params=params(),
        cost_estimate=cost(1, 1),
    )(own, low, *two)


def lower_kernel(vec, low_one, low_two, one, far):
    across = vec[...].T.astype(BF16)
    half = one.shape[0]
    one[...] = jnp.dot(across, low_one[:, half:], preferred_element_type=F32).T
    far[...] = jnp.dot(across, low_two[:, half:], preferred_element_type=F32).T


def lower_coupling(vec, low_one, low_two):
    size, k = vec.shape
    return pl.pallas_call(
        lower_kernel,
        in_specs=[VMEM] * 3,
        out_specs=[VMEM] * 2,
        out_shape=[jax.ShapeDtypeStruct((size // 2, k), F32)] * 2,
        compiler_params=params(),
        cost_estimate=cost(2 * size * size * k, 2 * size * size),
    )(vec, low_one, low_two)


def own_kernel(v0, v1, v2, diag, after, moments):
    image = jnp.dot(diag[...], v2[...].astype(BF16), preferred_element_type=F32)
    pairs = [(v0, v0), (v0, v1), (v1, v1), (v1, v2), (v2, v2)]
    for row, (a, b) in enumerate(pairs):
        moments[row : row + 1] = jnp.sum(a[...] * b[...], axis=0, keepdims=True)
    moments[5:6] = jnp.sum(v2[...] * image, axis=0, keepdims=True)
    moments[6:8] = jnp.zeros_like(moments[6:8])


def own_moments(v0, v1, v2, diag, after):
    size, k = v0.shape
    return pl.pallas_call(
        own_kernel,
        in_specs=[VMEM] * 4 + [ANY],
        out_specs=VMEM,
        out_shape=jax.ShapeDtypeStruct((8, k), F32),
        compiler_params=params(),
        cost_estimate=cost(2 * size * size * k, 6 * size * size),
    )(v0, v1, v2, diag, after)


def last_kernel(odd, low_one, low_two, one_a, one_b, two, v2, up, pair, moments, out):
    quarter, half = one_a.shape[0], two.shape[0]
    below = jnp.dot(low_two[:, :half], two[...].astype(BF16), preferred_element_type=F32)
    below = below + jnp.dot(low_one[:, :quarter], one_a[...].astype(BF16), preferred_element_type=F32)
    below = below + jnp.dot(low_one[:, quarter:half], one_b[...].astype(BF16), preferred_element_type=F32)
    above = up[...] + jnp.where(odd[0] > 0, 0.0, pair[...])
    coupled = jnp.sum(v2[...] * below, axis=0, keepdims=True) + jnp.sum(v2[half:] * above, axis=0, keepdims=True)
    out[...] = moments[...]
    out[5:6] = moments[5:6] + 2.0 * coupled


def last(odd, low_one, low_two, one_a, one_b, two, v2, up, pair, moments):
    size, k = v2.shape
    return pl.pallas_call(
        last_kernel,
        in_specs=[SMEM] + [VMEM] * 9,
        out_specs=VMEM,
        out_shape=jax.ShapeDtypeStruct((8, k), F32),
        compiler_params=params(),
        cost_estimate=cost(2 * size * size * k, 2 * size * size),
    )(odd, low_one, low_two, one_a, one_b, two, v2, up, pair, moments)


def group_rows(genotypes, groups, group):
    rows = genotypes.shape[0] // groups
    return genotypes[pl.ds(pl.multiple_of(group * rows, rows), rows)]


def send_kernel(groups, row, pieces, penalty, v0, v1, v2, genotypes, effects, rounded, send):
    sums = pieces[0]
    for piece in range(1, pieces.shape[0]):
        sums = sums + pieces[piece]
    moments = [sums[m : m + 1] for m in range(6)]
    c0, c1, c2 = coefficients(moments, penalty[...])
    value = c0 * v0[...] + c1 * v1[...] + c2 * v2[...]
    effects[...] = value
    narrow = value.astype(BF16)
    rounded[...] = narrow
    other = 1 - row[0] % 2
    for g in range(groups // 2):
        send[g] = jnp.dot(group_rows(genotypes, groups, 2 * g + other), narrow, preferred_element_type=F32)


def keep_kernel(groups, row, rounded, genotypes, keep):
    mine = row[0] % 2
    for g in range(groups // 2):
        keep[g] = jnp.dot(group_rows(genotypes, groups, 2 * g + mine), rounded[...], preferred_element_type=F32)


def partial_scores(row, groups, pieces, penalty, v0, v1, v2, genotypes):
    people, size = genotypes.shape
    k = v0.shape[1]
    half = jax.ShapeDtypeStruct((groups // 2, people // groups, k), F32)
    effects, rounded, send = pl.pallas_call(
        functools.partial(send_kernel, groups),
        in_specs=[SMEM] + [VMEM] * 6,
        out_specs=[VMEM] * 3,
        out_shape=[jax.ShapeDtypeStruct(v0.shape, F32), jax.ShapeDtypeStruct(v0.shape, BF16), half],
        compiler_params=params(),
        cost_estimate=cost(people * size * k, 2 * people * size),
    )(row, pieces, penalty, v0, v1, v2, genotypes)
    keep = pl.pallas_call(
        functools.partial(keep_kernel, groups),
        in_specs=[SMEM, VMEM, VMEM],
        out_specs=VMEM,
        out_shape=half,
        compiler_params=params(),
        cost_estimate=cost(people * size * k, 2 * people * size),
    )(row, rounded, genotypes)
    return effects, send, keep


def pick_kernel(index, keep, received, mine, other):
    mine[...] = keep[index[0]] + received[index[0]]
    other[...] = keep[1 - index[0]] + received[1 - index[0]]


def pick(index, keep, received):
    half = jax.ShapeDtypeStruct(keep.shape[1:], F32)
    return pl.pallas_call(
        pick_kernel,
        in_specs=[SMEM, VMEM, VMEM],
        out_specs=[VMEM] * 2,
        out_shape=[half] * 2,
        compiler_params=params(),
        cost_estimate=cost(keep.size, 12 * keep.size),
    )(index, keep, received)


def scattered_over(values, axis):
    n = lax.axis_size(axis)
    pieces = values.reshape((n, values.shape[0] // n) + values.shape[1:])
    return jnp.sum(lax.all_to_all(pieces, axis, 0, 0, tiled=True), axis=0)


def routed(block, pairs):
    return lax.ppermute(block, AXES, pairs)


def coefficients(moments, penalty):
    def inner(u, v):
        return sum(a * b * moments[i + j] for i, a in enumerate(u) for j, b in enumerate(v))

    n0 = moments[0]
    a0 = n0 / (moments[1] + penalty * n0)
    r1 = [1.0 - a0 * penalty, -a0]
    n1 = inner(r1, r1)
    b0 = n1 / n0
    d1 = [r1[0] + b0, r1[1]]
    ad1 = [penalty * d1[0], d1[0] + penalty * d1[1], d1[1]]
    a1 = n1 / inner(d1, ad1)
    e1 = [a0 + a1 * d1[0], a1 * d1[1]]
    r2 = [r1[0] - a1 * ad1[0], r1[1] - a1 * ad1[1], -a1 * ad1[2]]
    n2 = inner(r2, r2)
    b1 = n2 / n1
    d2 = [r2[0] + b1 * d1[0], r2[1] + b1 * d1[1], r2[2]]
    ad2 = [penalty * d2[0], d2[0] + penalty * d2[1], d2[1] + penalty * d2[2], d2[2]]
    a2 = n2 / inner(d2, ad2)
    return e1[0] + a2 * d2[0], e1[1] + a2 * d2[1], a2 * d2[2]


def swapped(block, bit):
    return routed(block, [(i, i ^ bit) for i in range(lax.axis_size(AXES))])


def body(marginal, penalty, ld_diag, ld_low, band, genotypes):
    n = lax.axis_size(AXES)
    rows, cols = lax.axis_size("row"), lax.axis_size("col")
    position = lax.axis_index(AXES)
    row = lax.axis_index("row")
    site = position.astype(jnp.int32)[None]
    odd = (position % 2).astype(jnp.int32)[None]
    half = marginal.shape[0] // 2

    def halos(vec, two, first, second, parts):
        one_a, one_b = first()
        pair_a, pair_b = swapped(one_a, 1), swapped(one_b, 1)
        far_a, far_b = second(one_b)
        sum_a = relay(odd, far_a, pair_a, far_b)
        up_a = shifted(sum_a, -2)
        if parts == 1:
            chosen = choose(odd, vec, two, sum_a, parts)
            sum_b = relay(odd, far_b, pair_b, chosen[0])
        else:
            sum_b = relay(odd, far_b, pair_b, sum_a)
            chosen = choose(odd, vec, two, sum_b, parts)
        up_b = shifted(sum_b, -2)
        ones = [swapped(part, 1) for part in chosen]
        return sum_b, (up_a, up_b, pair_a, pair_b, *ones)

    v0 = marginal
    two = shifted(v0, 2)

    lows = []

    def second_tile(after):
        vec, _ = lax.optimization_barrier((v0, after))
        *products, low_one, low_two = from_tiles(second_kernel, 2, 2, 46, band, site, vec, ld_low[0])
        lows.extend((low_one, low_two))
        return products

    last_sum, arrived = halos(
        v0, (two,), lambda: from_tiles(first_kernel, 1, 0, 58, band, site, v0, ld_low[0]), second_tile, 1
    )
    low_one, low_two = lows
    diag, own = first_diag(v0, ld_diag[0], last_sum)
    v1, *halves = finish(odd, add_two(own, low_two, (two,)), low_one, *arrived)

    products = coupling(v1, low_one, low_two)
    *halves, one_b = lax.optimization_barrier((*halves, products[1]))
    two = [shifted(part, 2) for part in halves]
    products = products[0], one_b, *products[2:]
    last_sum, arrived = halos(v1, two, lambda: products[:2], lambda after: products[2:], 3)
    own = diag_times(v1, diag, last_sum)
    v2, upper, _ = finish(odd, add_two(own, low_two, two), low_one, *arrived)

    two = shifted(upper, 2)
    one, far = lower_coupling(v2, low_one, low_two)
    pair = swapped(one, 1)
    above = relay(odd, far, pair, far)
    up = shifted(above, -2)
    chosen_a, chosen_b = choose(odd, upper, (two,), above, 2)
    moments = own_moments(v0, v1, v2, diag, chosen_b)
    one_a, one_b = swapped(chosen_a, 1), swapped(chosen_b, 1)
    moments = last(odd, low_one, low_two, one_a, one_b, two, v2, up, pair, moments)
    pieces = lax.all_to_all(jnp.broadcast_to(moments[None], (n,) + moments.shape), AXES, 0, 0, tiled=True)

    effects, send, keep = partial_scores(row.astype(jnp.int32)[None], rows, pieces, penalty[None], v0, v1, v2, genotypes)
    received = swapped(send, cols)
    bit = rows // 4
    while bit:
        mine = (row // (2 * bit)) % 2
        keep = keep.reshape((2, -1) + keep.shape[1:])
        received = received.reshape((2, -1) + received.shape[1:])

        keep, send = pick(mine.astype(jnp.int32)[None], keep, received)
        received = swapped(send, 2 * bit * cols)
        bit //= 2
    return effects, scattered_over((keep + received)[0], "col")


def solution(mesh):
    placed = (
        P(AXES, None),
        P(),
        P(AXES, None, None),
        P(AXES, None, None, None),
        P(AXES),
        P(None, AXES),
    )
    return jax.shard_map(
        body,
        mesh=mesh,
        in_specs=placed,
        out_specs=(P(AXES, None), P(AXES, None)),
        check_vma=False,
    )
```

```python
import functools

import jax
import jax.numpy as jnp
from jax import lax
from jax.experimental import pallas as pl
from jax.experimental.pallas import tpu as pltpu
from jax.sharding import PartitionSpec as P

AXES = ("row", "col")
F32 = jnp.float32
BF16 = jnp.bfloat16
MIB = 1024 * 1024
VMEM = pl.BlockSpec(memory_space=pltpu.VMEM)
SMEM = pl.BlockSpec(memory_space=pltpu.SMEM)
ANY = pl.BlockSpec(memory_space=pl.ANY)


def params(mib=20):
    return pltpu.CompilerParams(vmem_limit_bytes=mib * MIB)


def cost(flops, num_bytes):
    return pl.CostEstimate(flops=int(flops), bytes_accessed=int(num_bytes), transcendentals=0)


def shifted(block, distance):
    n = lax.axis_size(AXES)
    route = [(i - distance, i) for i in range(n) if 0 <= i - distance < n]
    return lax.ppermute(block, AXES, route)


def active(d, band, position):
    return jnp.logical_and(band[0] >= d + 1, position[0] >= d + 1)


def split_store(value, first, second):
    half = first.shape[0]
    first[...] = value[:half]
    second[...] = value[half:]


GROUP = 4


def fetched(low, tiles, arrived, order):
    count, rows = tiles.shape[0] // len(order), tiles.shape[1]
    copies = []
    for place in range(tiles.shape[0]):
        source = low.at[order[place // count], pl.ds(place % count * rows, rows)]
        copies.append(pltpu.make_async_copy(source, tiles.at[place], arrived.at[place]))
        copies[-1].start()
    return copies


def rounded_rows(copies, tiles, place, alive):
    for copy in copies[place : place + GROUP]:
        copy.wait()
    tile = tiles[place : place + GROUP].reshape(GROUP * tiles.shape[1], tiles.shape[2])
    return jnp.where(alive, tile, 0.0).astype(BF16)


def first_kernel(band, position, vec, low, one_a, one_b, own, tiles, arrived):
    fetch = pltpu.make_async_copy(vec, own, arrived.at[tiles.shape[0]])
    fetch.start()
    copies = fetched(low, tiles, arrived, (0,))
    fetch.wait()
    across = own[...].T.astype(BF16)
    rows = GROUP * tiles.shape[1]
    acc = None
    for place in range(0, tiles.shape[0], GROUP):
        tile = rounded_rows(copies, tiles, place, active(0, band, position))
        start = place * tiles.shape[1]
        term = jnp.dot(across[:, start : start + rows], tile, preferred_element_type=F32)
        acc = term if acc is None else acc + term
    split_store(acc.T, one_a, one_b)


def second_kernel(band, position, vec, low, far_a, far_b, low_one, low_two, own, tiles, arrived):
    fetch = pltpu.make_async_copy(vec, own, arrived.at[tiles.shape[0]])
    fetch.start()
    copies = fetched(low, tiles, arrived, (1, 0))
    fetch.wait()
    across = own[...].T.astype(BF16)
    rows = GROUP * tiles.shape[1]
    count = tiles.shape[0] // 2
    acc = None
    for place in range(0, count, GROUP):
        tile = rounded_rows(copies, tiles, place, active(1, band, position))
        start = place * tiles.shape[1]
        low_two[start : start + rows] = tile
        term = jnp.dot(across[:, start : start + rows], tile, preferred_element_type=F32)
        acc = term if acc is None else acc + term
    split_store(acc.T, far_a, far_b)
    for place in range(0, count, GROUP):
        start = place * tiles.shape[1]
        low_one[start : start + rows] = rounded_rows(copies, tiles, count + place, active(0, band, position))


def from_tiles(kernel, tiles, narrow, mib, band, position, vec, low):
    size, k = vec.shape
    count = 16
    return pl.pallas_call(
        kernel,
        in_specs=[SMEM] * 2 + [pl.BlockSpec(memory_space=pltpu.HBM)] * 2,
        out_specs=[VMEM] * (2 + narrow),
        out_shape=[jax.ShapeDtypeStruct((size // 2, k), F32)] * 2 + [jax.ShapeDtypeStruct((size, size), BF16)] * narrow,
        scratch_shapes=[
            pltpu.VMEM((size, k), F32),
            pltpu.VMEM((tiles * count, size // count, size), F32),
            pltpu.SemaphoreType.DMA((tiles * count + 1,)),
        ],
        compiler_params=params(mib),
        cost_estimate=cost(2 * size * size * k, 4 * tiles * size * size),
    )(band, position, vec, low)


def coupling_kernel(vec, low_one, low_two, one_a, one_b, far_a, far_b):
    across = vec[...].T.astype(BF16)
    split_store(jnp.dot(across, low_one[...], preferred_element_type=F32).T, one_a, one_b)
    split_store(jnp.dot(across, low_two[...], preferred_element_type=F32).T, far_a, far_b)


def coupling(vec, low_one, low_two):
    size, k = vec.shape
    return pl.pallas_call(
        coupling_kernel,
        in_specs=[VMEM] * 3,
        out_specs=[VMEM] * 4,
        out_shape=[jax.ShapeDtypeStruct((size // 2, k), F32)] * 4,
        compiler_params=params(),
        cost_estimate=cost(4 * size * size * k, 4 * size * size),
    )(vec, low_one, low_two)


def relay_kernel(odd, far, pair, after, out):
    out[...] = far[...] + jnp.where(odd[0] > 0, pair[...], 0.0)


def choose_kernel(odd, vec, two, after, *parts):
    rows = parts[0].shape[0]
    for place, part in enumerate(parts):
        here = slice(place * rows, (place + 1) * rows)
        part[...] = jnp.where(odd[0] > 0, two[here], vec[here])


def choose(odd, vec, two, after, parts):
    rows, k = vec.shape
    return pl.pallas_call(
        choose_kernel,
        in_specs=[SMEM, VMEM, VMEM, ANY],
        out_specs=[VMEM] * parts,
        out_shape=[jax.ShapeDtypeStruct((rows // parts, k), F32)] * parts,
        compiler_params=params(),
        cost_estimate=cost(vec.size, 12 * vec.size),
    )(odd, vec, two, after)


def relay(odd, far, pair, after):
    return pl.pallas_call(
        relay_kernel,
        in_specs=[SMEM, VMEM, VMEM, ANY],
        out_specs=VMEM,
        out_shape=jax.ShapeDtypeStruct(far.shape, F32),
        compiler_params=params(),
        cost_estimate=cost(far.size, 12 * far.size),
    )(odd, far, pair, after)


def first_diag_kernel(vec, diag, after, narrow, product):
    tile = diag[...].astype(BF16)
    rest = (diag[...] - tile.astype(F32)).astype(BF16)
    narrow[...] = tile
    value = vec[...]
    high = value.astype(BF16)
    low = (value - high.astype(F32)).astype(BF16)
    both = jnp.dot(tile, jnp.concatenate([high, low], axis=1), preferred_element_type=F32)
    k = value.shape[1]
    product[...] = both[:, :k] + both[:, k:] + jnp.dot(rest, high, preferred_element_type=F32)


def first_diag(vec, diag, after):
    size, k = vec.shape
    rows = size // 4
    return pl.pallas_call(
        first_diag_kernel,
        grid=(4,),
        in_specs=[pl.BlockSpec((size, k), lambda r: (0, 0)), pl.BlockSpec((rows, size), lambda r: (r, 0)), ANY],
        out_specs=[pl.BlockSpec((rows, size), lambda r: (r, 0)), pl.BlockSpec((rows, k), lambda r: (r, 0))],
        out_shape=[jax.ShapeDtypeStruct(diag.shape, BF16), jax.ShapeDtypeStruct(vec.shape, F32)],
        compiler_params=params(),
        cost_estimate=cost(2 * size * size * k, 6 * size * size),
    )(vec, diag, after)


def diag_kernel(vec, diag, after, product):
    product[...] = jnp.dot(diag[...], vec[...].astype(BF16), preferred_element_type=F32)


def diag_times(vec, diag, after):
    size, k = vec.shape
    return pl.pallas_call(
        diag_kernel,
        in_specs=[VMEM, VMEM, ANY],
        out_specs=VMEM,
        out_shape=jax.ShapeDtypeStruct(vec.shape, F32),
        compiler_params=params(),
        cost_estimate=cost(2 * size * size * k, 6 * size * size),
    )(vec, diag, after)


def finish_kernel(odd, part, low, one, ahead_a, ahead_b, pair_a, pair_b, out, *upper):
    acc = jnp.dot(low[...], one[...].astype(BF16), preferred_element_type=F32) + part[...]
    half = ahead_a.shape[0]
    for place, (straight, pair) in enumerate(((ahead_a, pair_a), (ahead_b, pair_b))):
        rows = slice(place * half, (place + 1) * half)
        out[rows] = acc[rows] + straight[...] + jnp.where(odd[0] > 0, 0.0, pair[...])
    for copy in upper:
        copy[...] = out[:half]


def finish(odd, uppers, part, low, *arrived):
    size, k = part.shape
    return pl.pallas_call(
        finish_kernel,
        in_specs=[SMEM] + [VMEM] * 7,
        out_specs=[VMEM] * (1 + uppers),
        out_shape=[jax.ShapeDtypeStruct(part.shape, F32)] + [jax.ShapeDtypeStruct((size // 2, k), F32)] * uppers,
        compiler_params=params(),
        cost_estimate=cost(2 * size * size * k, 2 * size * size),
    )(odd, part, low, *arrived)


def two_kernel(own, low, two, product):
    product[...] = own[...] + jnp.dot(low[...], two[...].astype(BF16), preferred_element_type=F32)


def add_two(own, low, two):
    size, k = two.shape
    return pl.pallas_call(
        two_kernel,
        in_specs=[VMEM] * 3,
        out_specs=VMEM,
        out_shape=jax.ShapeDtypeStruct(two.shape, F32),
        compiler_params=params(),
        cost_estimate=cost(2 * size * size * k, 2 * size * size),
    )(own, low, two)


def lower_kernel(vec, low_one, low_two, one, far):
    across = vec[...].T.astype(BF16)
    half = one.shape[0]
    one[...] = jnp.dot(across, low_one[:, half:], preferred_element_type=F32).T
    far[...] = jnp.dot(across, low_two[:, half:], preferred_element_type=F32).T


def lower_coupling(vec, low_one, low_two):
    size, k = vec.shape
    return pl.pallas_call(
        lower_kernel,
        in_specs=[VMEM] * 3,
        out_specs=[VMEM] * 2,
        out_shape=[jax.ShapeDtypeStruct((size // 2, k), F32)] * 2,
        compiler_params=params(),
        cost_estimate=cost(2 * size * size * k, 2 * size * size),
    )(vec, low_one, low_two)


def own_kernel(v0, v1, v2, diag, after, moments):
    image = jnp.dot(diag[...], v2[...].astype(BF16), preferred_element_type=F32)
    pairs = [(v0, v0), (v0, v1), (v1, v1), (v1, v2), (v2, v2)]
    for row, (a, b) in enumerate(pairs):
        moments[row : row + 1] = jnp.sum(a[...] * b[...], axis=0, keepdims=True)
    moments[5:6] = jnp.sum(v2[...] * image, axis=0, keepdims=True)
    moments[6:8] = jnp.zeros_like(moments[6:8])


def own_moments(v0, v1, v2, diag, after):
    size, k = v0.shape
    return pl.pallas_call(
        own_kernel,
        in_specs=[VMEM] * 4 + [ANY],
        out_specs=VMEM,
        out_shape=jax.ShapeDtypeStruct((8, k), F32),
        compiler_params=params(),
        cost_estimate=cost(2 * size * size * k, 6 * size * size),
    )(v0, v1, v2, diag, after)


def last_kernel(odd, low_one, low_two, one_a, one_b, two, v2, up, pair, moments, out):
    quarter, half = one_a.shape[0], two.shape[0]
    below = jnp.dot(low_two[:, :half], two[...].astype(BF16), preferred_element_type=F32)
    below = below + jnp.dot(low_one[:, :quarter], one_a[...].astype(BF16), preferred_element_type=F32)
    below = below + jnp.dot(low_one[:, quarter:half], one_b[...].astype(BF16), preferred_element_type=F32)
    above = up[...] + jnp.where(odd[0] > 0, 0.0, pair[...])
    coupled = jnp.sum(v2[...] * below, axis=0, keepdims=True) + jnp.sum(v2[half:] * above, axis=0, keepdims=True)
    out[...] = moments[...]
    out[5:6] = moments[5:6] + 2.0 * coupled


def last(odd, low_one, low_two, one_a, one_b, two, v2, up, pair, moments):
    size, k = v2.shape
    return pl.pallas_call(
        last_kernel,
        in_specs=[SMEM] + [VMEM] * 9,
        out_specs=VMEM,
        out_shape=jax.ShapeDtypeStruct((8, k), F32),
        compiler_params=params(),
        cost_estimate=cost(2 * size * size * k, 2 * size * size),
    )(odd, low_one, low_two, one_a, one_b, two, v2, up, pair, moments)


def group_rows(genotypes, groups, group):
    rows = genotypes.shape[0] // groups
    return genotypes[pl.ds(pl.multiple_of(group * rows, rows), rows)]


def send_kernel(groups, row, pieces, penalty, v0, v1, v2, genotypes, effects, rounded, send):
    sums = pieces[0]
    for piece in range(1, pieces.shape[0]):
        sums = sums + pieces[piece]
    moments = [sums[m : m + 1] for m in range(6)]
    c0, c1, c2 = coefficients(moments, penalty[...])
    value = c0 * v0[...] + c1 * v1[...] + c2 * v2[...]
    effects[...] = value
    narrow = value.astype(BF16)
    rounded[...] = narrow
    other = 1 - row[0] % 2
    for g in range(groups // 2):
        value = jnp.dot(group_rows(genotypes, groups, 2 * g + other), narrow, preferred_element_type=F32)
        send[:, g] = value.reshape(send.shape[0], send.shape[2], send.shape[3])


def keep_kernel(groups, row, rounded, genotypes, keep):
    mine = row[0] % 2
    for g in range(groups // 2):
        value = jnp.dot(group_rows(genotypes, groups, 2 * g + mine), rounded[...], preferred_element_type=F32)
        keep[:, g] = value.reshape(keep.shape[0], keep.shape[2], keep.shape[3])


def partial_scores(row, groups, pieces, penalty, v0, v1, v2, genotypes):
    people, size = genotypes.shape
    k = v0.shape[1]
    cols = lax.axis_size("col")
    half = jax.ShapeDtypeStruct((cols, groups // 2, people // groups // cols, k), F32)
    effects, rounded, send = pl.pallas_call(
        functools.partial(send_kernel, groups),
        in_specs=[SMEM] + [VMEM] * 6,
        out_specs=[VMEM] * 3,
        out_shape=[jax.ShapeDtypeStruct(v0.shape, F32), jax.ShapeDtypeStruct(v0.shape, BF16), half],
        compiler_params=params(),
        cost_estimate=cost(people * size * k, 2 * people * size),
    )(row, pieces, penalty, v0, v1, v2, genotypes)
    keep = pl.pallas_call(
        functools.partial(keep_kernel, groups),
        in_specs=[SMEM, VMEM, VMEM],
        out_specs=VMEM,
        out_shape=half,
        compiler_params=params(),
        cost_estimate=cost(people * size * k, 2 * people * size),
    )(row, rounded, genotypes)
    return effects, send, keep


def pick_kernel(index, keep, received, mine, other):
    mine[...] = keep[index[0]] + received[index[0]]
    other[...] = keep[1 - index[0]] + received[1 - index[0]]


def pick(index, keep, received):
    half = jax.ShapeDtypeStruct(keep.shape[1:], F32)
    return pl.pallas_call(
        pick_kernel,
        in_specs=[SMEM, VMEM, VMEM],
        out_specs=[VMEM] * 2,
        out_shape=[half] * 2,
        compiler_params=params(),
        cost_estimate=cost(keep.size, 12 * keep.size),
    )(index, keep, received)


def scattered_over(values, axis):
    n = lax.axis_size(axis)
    pieces = values.reshape((n, values.shape[0] // n) + values.shape[1:])
    return jnp.sum(lax.all_to_all(pieces, axis, 0, 0, tiled=True), axis=0)


def routed(block, pairs):
    return lax.ppermute(block, AXES, pairs)


def coefficients(moments, penalty):
    def inner(u, v):
        return sum(a * b * moments[i + j] for i, a in enumerate(u) for j, b in enumerate(v))

    n0 = moments[0]
    a0 = n0 / (moments[1] + penalty * n0)
    r1 = [1.0 - a0 * penalty, -a0]
    n1 = inner(r1, r1)
    b0 = n1 / n0
    d1 = [r1[0] + b0, r1[1]]
    ad1 = [penalty * d1[0], d1[0] + penalty * d1[1], d1[1]]
    a1 = n1 / inner(d1, ad1)
    e1 = [a0 + a1 * d1[0], a1 * d1[1]]
    r2 = [r1[0] - a1 * ad1[0], r1[1] - a1 * ad1[1], -a1 * ad1[2]]
    n2 = inner(r2, r2)
    b1 = n2 / n1
    d2 = [r2[0] + b1 * d1[0], r2[1] + b1 * d1[1], r2[2]]
    ad2 = [penalty * d2[0], d2[0] + penalty * d2[1], d2[1] + penalty * d2[2], d2[2]]
    a2 = n2 / inner(d2, ad2)
    return e1[0] + a2 * d2[0], e1[1] + a2 * d2[1], a2 * d2[2]


def swapped(block, bit):
    return routed(block, [(i, i ^ bit) for i in range(lax.axis_size(AXES))])


def body(marginal, penalty, ld_diag, ld_low, band, genotypes):
    n = lax.axis_size(AXES)
    rows, cols = lax.axis_size("row"), lax.axis_size("col")
    position = lax.axis_index(AXES)
    row = lax.axis_index("row")
    site = position.astype(jnp.int32)[None]
    odd = (position % 2).astype(jnp.int32)[None]
    half = marginal.shape[0] // 2

    def halos(vec, two, first, second):
        one_a, one_b = first()
        pair_a, pair_b = swapped(one_a, 1), swapped(one_b, 1)
        far_a, far_b = second(one_b)
        sum_a = relay(odd, far_a, pair_a, far_b)
        up_a = shifted(sum_a, -2)
        [chosen] = choose(odd, vec, two, sum_a, 1)
        one = swapped(chosen, 1)
        sum_b = relay(odd, far_b, pair_b, chosen)
        return sum_b, (one, up_a, shifted(sum_b, -2), pair_a, pair_b)

    v0 = marginal
    two = shifted(v0, 2)

    lows = []

    def second_tile(after):
        vec, _ = lax.optimization_barrier((v0, after))
        *products, low_one, low_two = from_tiles(second_kernel, 2, 2, 46, band, site, vec, ld_low[0])
        lows.extend((low_one, low_two))
        return products

    last_sum, arrived = halos(
        v0, two, lambda: from_tiles(first_kernel, 1, 0, 58, band, site, v0, ld_low[0]), second_tile
    )
    low_one, low_two = lows
    diag, own = first_diag(v0, ld_diag[0], last_sum)
    [v1] = finish(odd, 0, add_two(own, low_two, two), low_one, *arrived)

    two = shifted(v1, 2)
    products = coupling(v1, low_one, low_two)
    last_sum, arrived = halos(v1, two, lambda: products[:2], lambda after: products[2:])
    own = diag_times(v1, diag, last_sum)
    v2, upper = finish(odd, 1, add_two(own, low_two, two), low_one, *arrived)

    two = shifted(upper, 2)
    one, far = lower_coupling(v2, low_one, low_two)
    pair = swapped(one, 1)
    above = relay(odd, far, pair, far)
    up = shifted(above, -2)
    chosen_a, chosen_b = choose(odd, upper, two, above, 2)
    moments = own_moments(v0, v1, v2, diag, chosen_b)
    one_a, one_b = swapped(chosen_a, 1), swapped(chosen_b, 1)
    moments = last(odd, low_one, low_two, one_a, one_b, two, v2, up, pair, moments)
    pieces = lax.all_to_all(jnp.broadcast_to(moments[None], (n,) + moments.shape), AXES, 0, 0, tiled=True)

    effects, send, keep = partial_scores(row.astype(jnp.int32)[None], rows, pieces, penalty[None], v0, v1, v2, genotypes)
    received = swapped(send, cols)
    total = jnp.sum(lax.all_to_all(keep + received, "col", 0, 0, tiled=True), axis=0)
    bit = rows // 4
    while bit:
        index = (row // (2 * bit)) % 2
        total = total.reshape((2, -1) + total.shape[1:])
        send = lax.dynamic_index_in_dim(total, 1 - index, 0, False)
        total = lax.dynamic_index_in_dim(total, index, 0, False) + swapped(send, 2 * bit * cols)
        bit //= 2
    return effects, total[0]


def solution(mesh):
    placed = (
        P(AXES, None),
        P(),
        P(AXES, None, None),
        P(AXES, None, None, None),
        P(AXES),
        P(None, AXES),
    )
    return jax.shard_map(
        body,
        mesh=mesh,
        in_specs=placed,
        out_specs=(P(AXES, None), P(AXES, None)),
        check_vma=False,
    )
```

```python
import functools

import jax
import jax.numpy as jnp
from jax import lax
from jax.experimental import pallas as pl
from jax.experimental.pallas import tpu as pltpu
from jax.sharding import PartitionSpec as P

AXES = ("row", "col")
F32 = jnp.float32
BF16 = jnp.bfloat16
MIB = 1024 * 1024
VMEM = pl.BlockSpec(memory_space=pltpu.VMEM)
SMEM = pl.BlockSpec(memory_space=pltpu.SMEM)
ANY = pl.BlockSpec(memory_space=pl.ANY)


def params(mib=20):
    return pltpu.CompilerParams(vmem_limit_bytes=mib * MIB)


def cost(flops, num_bytes):
    return pl.CostEstimate(flops=int(flops), bytes_accessed=int(num_bytes), transcendentals=0)


def shifted(block, distance):
    n = lax.axis_size(AXES)
    route = [(i - distance, i) for i in range(n) if 0 <= i - distance < n]
    return lax.ppermute(block, AXES, route)


def active(d, band, position):
    return jnp.logical_and(band[0] >= d + 1, position[0] >= d + 1)


def split_store(value, first, second):
    half = first.shape[0]
    first[...] = value[:half]
    second[...] = value[half:]


GROUP = 4


def fetched(low, tiles, arrived, order):
    count, rows = tiles.shape[0] // len(order), tiles.shape[1]
    copies = []
    for place in range(tiles.shape[0]):
        source = low.at[order[place // count], pl.ds(place % count * rows, rows)]
        copies.append(pltpu.make_async_copy(source, tiles.at[place], arrived.at[place]))
        copies[-1].start()
    return copies


def rounded_rows(copies, tiles, place, alive):
    for copy in copies[place : place + GROUP]:
        copy.wait()
    tile = tiles[place : place + GROUP].reshape(GROUP * tiles.shape[1], tiles.shape[2])
    return jnp.where(alive, tile, 0.0).astype(BF16)


def first_kernel(band, position, vec, low, one_a, one_b, own, tiles, arrived):
    fetch = pltpu.make_async_copy(vec, own, arrived.at[tiles.shape[0]])
    fetch.start()
    copies = fetched(low, tiles, arrived, (0,))
    fetch.wait()
    across = own[...].T.astype(BF16)
    rows = GROUP * tiles.shape[1]
    acc = None
    for place in range(0, tiles.shape[0], GROUP):
        tile = rounded_rows(copies, tiles, place, active(0, band, position))
        start = place * tiles.shape[1]
        term = jnp.dot(across[:, start : start + rows], tile, preferred_element_type=F32)
        acc = term if acc is None else acc + term
    split_store(acc.T, one_a, one_b)


def second_kernel(band, position, vec, low, far_a, far_b, low_one, low_two, own, tiles, arrived):
    fetch = pltpu.make_async_copy(vec, own, arrived.at[tiles.shape[0]])
    fetch.start()
    copies = fetched(low, tiles, arrived, (1, 0))
    fetch.wait()
    across = own[...].T.astype(BF16)
    rows = GROUP * tiles.shape[1]
    count = tiles.shape[0] // 2
    acc = None
    for place in range(0, count, GROUP):
        tile = rounded_rows(copies, tiles, place, active(1, band, position))
        start = place * tiles.shape[1]
        low_two[start : start + rows] = tile
        term = jnp.dot(across[:, start : start + rows], tile, preferred_element_type=F32)
        acc = term if acc is None else acc + term
    split_store(acc.T, far_a, far_b)
    for place in range(0, count, GROUP):
        start = place * tiles.shape[1]
        low_one[start : start + rows] = rounded_rows(copies, tiles, count + place, active(0, band, position))


def from_tiles(kernel, tiles, narrow, mib, band, position, vec, low):
    size, k = vec.shape
    count = 16
    return pl.pallas_call(
        kernel,
        in_specs=[SMEM] * 2 + [pl.BlockSpec(memory_space=pltpu.HBM)] * 2,
        out_specs=[VMEM] * (2 + narrow),
        out_shape=[jax.ShapeDtypeStruct((size // 2, k), F32)] * 2 + [jax.ShapeDtypeStruct((size, size), BF16)] * narrow,
        scratch_shapes=[
            pltpu.VMEM((size, k), F32),
            pltpu.VMEM((tiles * count, size // count, size), F32),
            pltpu.SemaphoreType.DMA((tiles * count + 1,)),
        ],
        compiler_params=params(mib),
        cost_estimate=cost(2 * size * size * k, 4 * tiles * size * size),
    )(band, position, vec, low)


def coupling_kernel(vec, low_one, low_two, one_a, one_b, far_a, far_b):
    across = vec[...].T.astype(BF16)
    split_store(jnp.dot(across, low_one[...], preferred_element_type=F32).T, one_a, one_b)
    split_store(jnp.dot(across, low_two[...], preferred_element_type=F32).T, far_a, far_b)


def coupling(vec, low_one, low_two):
    size, k = vec.shape
    return pl.pallas_call(
        coupling_kernel,
        in_specs=[VMEM] * 3,
        out_specs=[VMEM] * 4,
        out_shape=[jax.ShapeDtypeStruct((size // 2, k), F32)] * 4,
        compiler_params=params(),
        cost_estimate=cost(4 * size * size * k, 4 * size * size),
    )(vec, low_one, low_two)


def relay_kernel(odd, far, pair, after, out):
    out[...] = far[...] + jnp.where(odd[0] > 0, pair[...], 0.0)


def choose_kernel(odd, vec, two, after, *parts):
    rows = parts[0].shape[0]
    for place, part in enumerate(parts):
        here = slice(place * rows, (place + 1) * rows)
        part[...] = jnp.where(odd[0] > 0, two[here], vec[here])


def choose(odd, vec, two, after, parts):
    rows, k = vec.shape
    return pl.pallas_call(
        choose_kernel,
        in_specs=[SMEM, VMEM, VMEM, ANY],
        out_specs=[VMEM] * parts,
        out_shape=[jax.ShapeDtypeStruct((rows // parts, k), F32)] * parts,
        compiler_params=params(),
        cost_estimate=cost(vec.size, 12 * vec.size),
    )(odd, vec, two, after)


def relay(odd, far, pair, after):
    return pl.pallas_call(
        relay_kernel,
        in_specs=[SMEM, VMEM, VMEM, ANY],
        out_specs=VMEM,
        out_shape=jax.ShapeDtypeStruct(far.shape, F32),
        compiler_params=params(),
        cost_estimate=cost(far.size, 12 * far.size),
    )(odd, far, pair, after)


def first_diag_kernel(vec, diag, after, narrow, product):
    tile = diag[...].astype(BF16)
    rest = (diag[...] - tile.astype(F32)).astype(BF16)
    narrow[...] = tile
    value = vec[...]
    high = value.astype(BF16)
    low = (value - high.astype(F32)).astype(BF16)
    both = jnp.dot(tile, jnp.concatenate([high, low], axis=1), preferred_element_type=F32)
    k = value.shape[1]
    product[...] = both[:, :k] + both[:, k:] + jnp.dot(rest, high, preferred_element_type=F32)


def first_diag(vec, diag, after):
    size, k = vec.shape
    rows = size // 4
    return pl.pallas_call(
        first_diag_kernel,
        grid=(4,),
        in_specs=[pl.BlockSpec((size, k), lambda r: (0, 0)), pl.BlockSpec((rows, size), lambda r: (r, 0)), ANY],
        out_specs=[pl.BlockSpec((rows, size), lambda r: (r, 0)), pl.BlockSpec((rows, k), lambda r: (r, 0))],
        out_shape=[jax.ShapeDtypeStruct(diag.shape, BF16), jax.ShapeDtypeStruct(vec.shape, F32)],
        compiler_params=params(),
        cost_estimate=cost(2 * size * size * k, 6 * size * size),
    )(vec, diag, after)


def diag_kernel(vec, diag, after, product):
    product[...] = jnp.dot(diag[...], vec[...].astype(BF16), preferred_element_type=F32)


def diag_times(vec, diag, after):
    size, k = vec.shape
    return pl.pallas_call(
        diag_kernel,
        in_specs=[VMEM, VMEM, ANY],
        out_specs=VMEM,
        out_shape=jax.ShapeDtypeStruct(vec.shape, F32),
        compiler_params=params(),
        cost_estimate=cost(2 * size * size * k, 6 * size * size),
    )(vec, diag, after)


def finish_kernel(odd, part, low, one, ahead_a, ahead_b, pair_a, pair_b, out, *upper):
    acc = jnp.dot(low[...], one[...].astype(BF16), preferred_element_type=F32) + part[...]
    half = ahead_a.shape[0]
    for place, (straight, pair) in enumerate(((ahead_a, pair_a), (ahead_b, pair_b))):
        rows = slice(place * half, (place + 1) * half)
        out[rows] = acc[rows] + straight[...] + jnp.where(odd[0] > 0, 0.0, pair[...])
    for copy in upper:
        copy[...] = out[:half]


def finish(odd, uppers, part, low, *arrived):
    size, k = part.shape
    return pl.pallas_call(
        finish_kernel,
        in_specs=[SMEM] + [VMEM] * 7,
        out_specs=[VMEM] * (1 + uppers),
        out_shape=[jax.ShapeDtypeStruct(part.shape, F32)] + [jax.ShapeDtypeStruct((size // 2, k), F32)] * uppers,
        compiler_params=params(),
        cost_estimate=cost(2 * size * size * k, 2 * size * size),
    )(odd, part, low, *arrived)


def two_kernel(own, low, two, product):
    product[...] = own[...] + jnp.dot(low[...], two[...].astype(BF16), preferred_element_type=F32)


def add_two(own, low, two):
    size, k = two.shape
    return pl.pallas_call(
        two_kernel,
        in_specs=[VMEM] * 3,
        out_specs=VMEM,
        out_shape=jax.ShapeDtypeStruct(two.shape, F32),
        compiler_params=params(),
        cost_estimate=cost(2 * size * size * k, 2 * size * size),
    )(own, low, two)


def lower_kernel(vec, low_one, low_two, one, far):
    across = vec[...].T.astype(BF16)
    half = one.shape[0]
    one[...] = jnp.dot(across, low_one[:, half:], preferred_element_type=F32).T
    far[...] = jnp.dot(across, low_two[:, half:], preferred_element_type=F32).T


def lower_coupling(vec, low_one, low_two):
    size, k = vec.shape
    return pl.pallas_call(
        lower_kernel,
        in_specs=[VMEM] * 3,
        out_specs=[VMEM] * 2,
        out_shape=[jax.ShapeDtypeStruct((size // 2, k), F32)] * 2,
        compiler_params=params(),
        cost_estimate=cost(2 * size * size * k, 2 * size * size),
    )(vec, low_one, low_two)


def own_kernel(v0, v1, v2, diag, after, moments):
    image = jnp.dot(diag[...], v2[...].astype(BF16), preferred_element_type=F32)
    pairs = [(v0, v0), (v0, v1), (v1, v1), (v1, v2), (v2, v2)]
    for row, (a, b) in enumerate(pairs):
        moments[row : row + 1] = jnp.sum(a[...] * b[...], axis=0, keepdims=True)
    moments[5:6] = jnp.sum(v2[...] * image, axis=0, keepdims=True)
    moments[6:8] = jnp.zeros_like(moments[6:8])


def own_moments(v0, v1, v2, diag, after):
    size, k = v0.shape
    return pl.pallas_call(
        own_kernel,
        in_specs=[VMEM] * 4 + [ANY],
        out_specs=VMEM,
        out_shape=jax.ShapeDtypeStruct((8, k), F32),
        compiler_params=params(),
        cost_estimate=cost(2 * size * size * k, 6 * size * size),
    )(v0, v1, v2, diag, after)


def last_kernel(odd, low_one, low_two, one_a, one_b, two, v2, up, pair, moments, out):
    quarter, half = one_a.shape[0], two.shape[0]
    below = jnp.dot(low_two[:, :half], two[...].astype(BF16), preferred_element_type=F32)
    below = below + jnp.dot(low_one[:, :quarter], one_a[...].astype(BF16), preferred_element_type=F32)
    below = below + jnp.dot(low_one[:, quarter:half], one_b[...].astype(BF16), preferred_element_type=F32)
    above = up[...] + jnp.where(odd[0] > 0, 0.0, pair[...])
    coupled = jnp.sum(v2[...] * below, axis=0, keepdims=True) + jnp.sum(v2[half:] * above, axis=0, keepdims=True)
    out[...] = moments[...]
    out[5:6] = moments[5:6] + 2.0 * coupled


def last(odd, low_one, low_two, one_a, one_b, two, v2, up, pair, moments):
    size, k = v2.shape
    return pl.pallas_call(
        last_kernel,
        in_specs=[SMEM] + [VMEM] * 9,
        out_specs=VMEM,
        out_shape=jax.ShapeDtypeStruct((8, k), F32),
        compiler_params=params(),
        cost_estimate=cost(2 * size * size * k, 2 * size * size),
    )(odd, low_one, low_two, one_a, one_b, two, v2, up, pair, moments)


def group_rows(genotypes, groups, group):
    rows = genotypes.shape[0] // groups
    return genotypes[pl.ds(pl.multiple_of(group * rows, rows), rows)]


def send_kernel(groups, row, pieces, penalty, v0, v1, v2, genotypes, effects, rounded, send):
    sums = pieces[0]
    for piece in range(1, pieces.shape[0]):
        sums = sums + pieces[piece]
    moments = [sums[m : m + 1] for m in range(6)]
    c0, c1, c2 = coefficients(moments, penalty[...])
    value = c0 * v0[...] + c1 * v1[...] + c2 * v2[...]
    effects[...] = value
    narrow = value.astype(BF16)
    rounded[...] = narrow
    other = 1 - row[0] % 2
    for g in range(groups // 2):
        send[g] = jnp.dot(group_rows(genotypes, groups, 2 * g + other), narrow, preferred_element_type=F32)


def keep_kernel(groups, row, rounded, genotypes, keep):
    mine = row[0] % 2
    for g in range(groups // 2):
        keep[g] = jnp.dot(group_rows(genotypes, groups, 2 * g + mine), rounded[...], preferred_element_type=F32)


def partial_scores(row, groups, pieces, penalty, v0, v1, v2, genotypes):
    people, size = genotypes.shape
    k = v0.shape[1]
    half = jax.ShapeDtypeStruct((groups // 2, people // groups, k), F32)
    effects, rounded, send = pl.pallas_call(
        functools.partial(send_kernel, groups),
        in_specs=[SMEM] + [VMEM] * 6,
        out_specs=[VMEM] * 3,
        out_shape=[jax.ShapeDtypeStruct(v0.shape, F32), jax.ShapeDtypeStruct(v0.shape, BF16), half],
        compiler_params=params(),
        cost_estimate=cost(people * size * k, 2 * people * size),
    )(row, pieces, penalty, v0, v1, v2, genotypes)
    keep = pl.pallas_call(
        functools.partial(keep_kernel, groups),
        in_specs=[SMEM, VMEM, VMEM],
        out_specs=VMEM,
        out_shape=half,
        compiler_params=params(),
        cost_estimate=cost(people * size * k, 2 * people * size),
    )(row, rounded, genotypes)
    return effects, send, keep


def pick_kernel(index, keep, received, mine, other):
    mine[...] = keep[index[0]] + received[index[0]]
    other[...] = keep[1 - index[0]] + received[1 - index[0]]


def pick(index, keep, received):
    half = jax.ShapeDtypeStruct(keep.shape[1:], F32)
    return pl.pallas_call(
        pick_kernel,
        in_specs=[SMEM, VMEM, VMEM],
        out_specs=[VMEM] * 2,
        out_shape=[half] * 2,
        compiler_params=params(),
        cost_estimate=cost(keep.size, 12 * keep.size),
    )(index, keep, received)


def scattered_over(values, axis):
    n = lax.axis_size(axis)
    pieces = values.reshape((n, values.shape[0] // n) + values.shape[1:])
    return jnp.sum(lax.all_to_all(pieces, axis, 0, 0, tiled=True), axis=0)


def routed(block, pairs):
    return lax.ppermute(block, AXES, pairs)


def coefficients(moments, penalty):
    def inner(u, v):
        return sum(a * b * moments[i + j] for i, a in enumerate(u) for j, b in enumerate(v))

    n0 = moments[0]
    a0 = n0 / (moments[1] + penalty * n0)
    r1 = [1.0 - a0 * penalty, -a0]
    n1 = inner(r1, r1)
    b0 = n1 / n0
    d1 = [r1[0] + b0, r1[1]]
    ad1 = [penalty * d1[0], d1[0] + penalty * d1[1], d1[1]]
    a1 = n1 / inner(d1, ad1)
    e1 = [a0 + a1 * d1[0], a1 * d1[1]]
    r2 = [r1[0] - a1 * ad1[0], r1[1] - a1 * ad1[1], -a1 * ad1[2]]
    n2 = inner(r2, r2)
    b1 = n2 / n1
    d2 = [r2[0] + b1 * d1[0], r2[1] + b1 * d1[1], r2[2]]
    ad2 = [penalty * d2[0], d2[0] + penalty * d2[1], d2[1] + penalty * d2[2], d2[2]]
    a2 = n2 / inner(d2, ad2)
    return e1[0] + a2 * d2[0], e1[1] + a2 * d2[1], a2 * d2[2]


def swapped(block, bit):
    return routed(block, [(i, i ^ bit) for i in range(lax.axis_size(AXES))])


def body(marginal, penalty, ld_diag, ld_low, band, genotypes):
    n = lax.axis_size(AXES)
    rows, cols = lax.axis_size("row"), lax.axis_size("col")
    position = lax.axis_index(AXES)
    row = lax.axis_index("row")
    site = position.astype(jnp.int32)[None]
    odd = (position % 2).astype(jnp.int32)[None]
    half = marginal.shape[0] // 2

    def halos(vec, two, first, second):
        one_a, one_b = first()
        pair_a, pair_b = swapped(one_a, 1), swapped(one_b, 1)
        far_a, far_b = second(one_b)
        sum_a = relay(odd, far_a, pair_a, far_b)
        up_a = shifted(sum_a, -2)
        [chosen] = choose(odd, vec, two, sum_a, 1)
        one = swapped(chosen, 1)
        sum_b = relay(odd, far_b, pair_b, chosen)
        return sum_b, (one, up_a, shifted(sum_b, -2), pair_a, pair_b)

    v0 = marginal
    two = shifted(v0, 2)

    lows = []

    def second_tile(after):
        vec, _ = lax.optimization_barrier((v0, after))
        *products, low_one, low_two = from_tiles(second_kernel, 2, 2, 46, band, site, vec, ld_low[0])
        lows.extend((low_one, low_two))
        return products

    last_sum, arrived = halos(
        v0, two, lambda: from_tiles(first_kernel, 1, 0, 58, band, site, v0, ld_low[0]), second_tile
    )
    low_one, low_two = lows
    diag, own = first_diag(v0, ld_diag[0], last_sum)
    [v1] = finish(odd, 0, add_two(own, low_two, two), low_one, *arrived)

    two = shifted(v1, 2)
    products = coupling(v1, low_one, low_two)
    last_sum, arrived = halos(v1, two, lambda: products[:2], lambda after: products[2:])
    own = diag_times(v1, diag, last_sum)
    v2, upper = finish(odd, 1, add_two(own, low_two, two), low_one, *arrived)

    two = shifted(upper, 2)
    one, far = lower_coupling(v2, low_one, low_two)
    pair = swapped(one, 1)
    above = relay(odd, far, pair, far)
    up = shifted(above, -2)
    chosen_a, chosen_b = choose(odd, upper, two, above, 2)
    moments = own_moments(v0, v1, v2, diag, chosen_b)
    one_a, one_b = swapped(chosen_a, 1), swapped(chosen_b, 1)
    moments = last(odd, low_one, low_two, one_a, one_b, two, v2, up, pair, moments)
    pieces = lax.all_to_all(jnp.broadcast_to(moments[None], (n,) + moments.shape), AXES, 0, 0, tiled=True)

    effects, send, keep = partial_scores(row.astype(jnp.int32)[None], rows, pieces, penalty[None], v0, v1, v2, genotypes)
    received = swapped(send, cols)
    bit = rows // 4
    while bit:
        mine = (row // (2 * bit)) % 2
        keep = keep.reshape((2, -1) + keep.shape[1:])
        received = received.reshape((2, -1) + received.shape[1:])

        keep, send = pick(mine.astype(jnp.int32)[None], keep, received)
        received = swapped(send, 2 * bit * cols)
        bit //= 2
    return effects, scattered_over((keep + received)[0], "col")


def solution(mesh):
    placed = (
        P(AXES, None),
        P(),
        P(AXES, None, None),
        P(AXES, None, None, None),
        P(AXES),
        P(None, AXES),
    )
    return jax.shard_map(
        body,
        mesh=mesh,
        in_specs=placed,
        out_specs=(P(AXES, None), P(AXES, None)),
        check_vma=False,
    )
```

```python
import functools

import jax
import jax.numpy as jnp
from jax import lax
from jax.experimental import pallas as pl
from jax.experimental.pallas import tpu as pltpu
from jax.sharding import PartitionSpec as P

AXES = ("row", "col")
F32 = jnp.float32
BF16 = jnp.bfloat16
MIB = 1024 * 1024
VMEM = pl.BlockSpec(memory_space=pltpu.VMEM)
SMEM = pl.BlockSpec(memory_space=pltpu.SMEM)
ANY = pl.BlockSpec(memory_space=pl.ANY)


def params(mib=20):
    return pltpu.CompilerParams(vmem_limit_bytes=mib * MIB)


def cost(flops, num_bytes):
    return pl.CostEstimate(flops=int(flops), bytes_accessed=int(num_bytes), transcendentals=0)


def shifted(block, distance):
    n = lax.axis_size(AXES)
    route = [(i - distance, i) for i in range(n) if 0 <= i - distance < n]
    return lax.ppermute(block, AXES, route)


def active(d, band, position):
    return jnp.logical_and(band[0] >= d + 1, position[0] >= d + 1)


def split(size):
    return size * 5 // 8, size - size * 5 // 8


def split_store(value, first, second):
    rows = first.shape[0]
    first[...] = value[:rows]
    second[...] = value[rows:]


def joined(parts):
    values = [part[...] for part in parts]
    return values[0] if len(values) == 1 else jnp.concatenate(values, axis=0)


def like(rows, k, kind=F32):
    return jax.ShapeDtypeStruct((rows, k), kind)


def local(kernel, outs, operands, scalars=0, after=None, scratch=()):
    count = len(operands)

    def run(*refs):
        kernel(*refs[:count], *refs[count + (after is not None) :])

    specs = [SMEM] * scalars + [VMEM] * (count - scalars)
    return pl.pallas_call(
        run,
        in_specs=specs + ([ANY] if after is not None else []),
        out_specs=[VMEM] * len(outs),
        out_shape=outs,
        scratch_shapes=scratch,
        compiler_params=params(),
        cost_estimate=cost(1, 1),
    )(*operands, *([after] if after is not None else []))


GROUP = 4


def fetched(low, tiles, arrived, order):
    count, rows = tiles.shape[0] // len(order), tiles.shape[1]
    copies = []
    for place in range(tiles.shape[0]):
        source = low.at[order[place // count], pl.ds(place % count * rows, rows)]
        copies.append(pltpu.make_async_copy(source, tiles.at[place], arrived.at[place]))
        copies[-1].start()
    return copies


def rounded_rows(copies, tiles, place, alive):
    for copy in copies[place : place + GROUP]:
        copy.wait()
    tile = tiles[place : place + GROUP].reshape(GROUP * tiles.shape[1], tiles.shape[2])
    return jnp.where(alive, tile, 0.0).astype(BF16)


def first_kernel(band, position, vec, low, one_a, one_b, own, tiles, arrived):
    fetch = pltpu.make_async_copy(vec, own, arrived.at[tiles.shape[0]])
    fetch.start()
    copies = fetched(low, tiles, arrived, (0,))
    fetch.wait()
    across = own[...].T.astype(BF16)
    rows = GROUP * tiles.shape[1]
    acc = None
    for place in range(0, tiles.shape[0], GROUP):
        tile = rounded_rows(copies, tiles, place, active(0, band, position))
        start = place * tiles.shape[1]
        term = jnp.dot(across[:, start : start + rows], tile, preferred_element_type=F32)
        acc = term if acc is None else acc + term
    split_store(acc.T, one_a, one_b)


def second_kernel(band, position, vec, low, far_a, far_b, low_one, low_two, own, tiles, arrived):
    fetch = pltpu.make_async_copy(vec, own, arrived.at[tiles.shape[0]])
    fetch.start()
    copies = fetched(low, tiles, arrived, (1, 0))
    fetch.wait()
    across = own[...].T.astype(BF16)
    rows = GROUP * tiles.shape[1]
    count = tiles.shape[0] // 2
    acc = None
    for place in range(0, count, GROUP):
        tile = rounded_rows(copies, tiles, place, active(1, band, position))
        start = place * tiles.shape[1]
        low_two[start : start + rows] = tile
        term = jnp.dot(across[:, start : start + rows], tile, preferred_element_type=F32)
        acc = term if acc is None else acc + term
    split_store(acc.T, far_a, far_b)
    for place in range(0, count, GROUP):
        start = place * tiles.shape[1]
        low_one[start : start + rows] = rounded_rows(copies, tiles, count + place, active(0, band, position))


def from_tiles(kernel, tiles, narrow, mib, band, position, vec, low):
    size, k = vec.shape
    count = 16
    return pl.pallas_call(
        kernel,
        in_specs=[SMEM] * 2 + [pl.BlockSpec(memory_space=pltpu.HBM)] * 2,
        out_specs=[VMEM] * (2 + narrow),
        out_shape=[jax.ShapeDtypeStruct((part, k), F32) for part in split(size)] + [jax.ShapeDtypeStruct((size, size), BF16)] * narrow,
        scratch_shapes=[
            pltpu.VMEM((size, k), F32),
            pltpu.VMEM((tiles * count, size // count, size), F32),
            pltpu.SemaphoreType.DMA((tiles * count + 1,)),
        ],
        compiler_params=params(mib),
        cost_estimate=cost(2 * size * size * k, 4 * tiles * size * size),
    )(band, position, vec, low)


def coupling(vec, low_one, low_two):
    size, k = low_one.shape[0], vec[0].shape[1]

    def kernel(*refs):
        *vec, low_one, low_two, one_a, one_b, far_a, far_b = refs
        across = joined(vec).T.astype(BF16)
        split_store(jnp.dot(across, low_one[...], preferred_element_type=F32).T, one_a, one_b)
        split_store(jnp.dot(across, low_two[...], preferred_element_type=F32).T, far_a, far_b)

    return local(kernel, [like(rows, k) for rows in split(size) * 2], [*vec, low_one, low_two])


def lower_coupling(vec, low_one, low_two):
    size, k = low_one.shape[0], vec[0].shape[1]
    start, rows = split(size)

    def kernel(*refs):
        *vec, low_one, low_two, one, far = refs
        across = joined(vec).T.astype(BF16)
        one[...] = jnp.dot(across, low_one[:, start:], preferred_element_type=F32).T
        far[...] = jnp.dot(across, low_two[:, start:], preferred_element_type=F32).T

    return local(kernel, [like(rows, k)] * 2, [*vec, low_one, low_two])


def relay(odd, far, pair, after):
    def kernel(odd, far, pair, out):
        out[...] = far[...] + jnp.where(odd[0] > 0, pair[...], 0.0)

    return local(kernel, [like(*far.shape)], [odd, far, pair], 1, after)[0]


def choose(odd, vec, two, after, parts):
    rows, k = sum(part.shape[0] for part in vec) // parts, vec[0].shape[1]

    def kernel(odd, *refs):
        count = len(vec)
        value = jnp.where(odd[0] > 0, joined(refs[count : 2 * count]), joined(refs[:count]))
        for place, out in enumerate(refs[2 * count :]):
            out[...] = value[place * rows : (place + 1) * rows]

    return local(kernel, [like(rows, k)] * parts, [odd, *vec, *two], 1, after)


def first_diag_kernel(vec, diag, after, narrow, product):
    tile = diag[...].astype(BF16)
    rest = (diag[...] - tile.astype(F32)).astype(BF16)
    narrow[...] = tile
    value = vec[...]
    high = value.astype(BF16)
    low = (value - high.astype(F32)).astype(BF16)
    both = jnp.dot(tile, jnp.concatenate([high, low], axis=1), preferred_element_type=F32)
    k = value.shape[1]
    product[...] = both[:, :k] + both[:, k:] + jnp.dot(rest, high, preferred_element_type=F32)


def first_diag(vec, diag, after):
    size, k = vec.shape
    rows = size // 4
    return pl.pallas_call(
        first_diag_kernel,
        grid=(4,),
        in_specs=[pl.BlockSpec((size, k), lambda r: (0, 0)), pl.BlockSpec((rows, size), lambda r: (r, 0)), ANY],
        out_specs=[pl.BlockSpec((rows, size), lambda r: (r, 0)), pl.BlockSpec((rows, k), lambda r: (r, 0))],
        out_shape=[jax.ShapeDtypeStruct(diag.shape, BF16), jax.ShapeDtypeStruct(vec.shape, F32)],
        compiler_params=params(),
        cost_estimate=cost(2 * size * size * k, 6 * size * size),
    )(vec, diag, after)


def diag_times(vec, diag, after):
    size, k = diag.shape[0], vec[0].shape[1]

    def kernel(*refs):
        *vec, diag, product = refs
        product[...] = jnp.dot(diag[...], joined(vec).astype(BF16), preferred_element_type=F32)

    return local(kernel, [like(size, k)], [*vec, diag], after=after)[0]


def add_two(own, low, two):
    def kernel(own, low, *refs):
        *two, product = refs
        product[...] = own[...] + jnp.dot(low[...], joined(two).astype(BF16), preferred_element_type=F32)

    return local(kernel, [like(*own.shape)], [own, low, *two])[0]


def finish(number, odd, part, low, ones, ahead, pair, after=None):
    start = number * (part.shape[0] - ahead.shape[0])
    rows = slice(start, start + ahead.shape[0])

    def kernel(odd, part, low, one_a, one_b, ahead, pair, out):
        one = joined((one_a, one_b)).astype(BF16)
        acc = jnp.dot(low[rows], one, preferred_element_type=F32) + part[rows]
        out[...] = acc + ahead[...] + jnp.where(odd[0] > 0, 0.0, pair[...])

    return local(kernel, [like(*ahead.shape)], [odd, part, low, *ones, ahead, pair], 1, after)[0]


def own_moments(v0, v1, v2, diag, after):
    def kernel(v0, v1_a, v1_b, v2_a, v2_b, diag, moments):
        first, second, third = v0[...], joined((v1_a, v1_b)), joined((v2_a, v2_b))
        image = jnp.dot(diag[...], third.astype(BF16), preferred_element_type=F32)
        pairs = [(first, first), (first, second), (second, second), (second, third), (third, third), (third, image)]
        for row, (a, b) in enumerate(pairs):
            moments[row : row + 1] = jnp.sum(a * b, axis=0, keepdims=True)
        moments[6:8] = jnp.zeros_like(moments[6:8])

    return local(kernel, [like(8, v0.shape[1])], [v0, *v1, *v2, diag], after=after)[0]


def last(odd, low_one, low_two, one_a, one_b, two, v2, up, pair, moments):
    quarter, half = one_a.shape[0], two.shape[0]

    def kernel(odd, low_one, low_two, one_a, one_b, two, v2_a, v2_b, up, pair, moments, out):
        below = jnp.dot(low_two[:, :half], two[...].astype(BF16), preferred_element_type=F32)
        below = below + jnp.dot(low_one[:, :quarter], one_a[...].astype(BF16), preferred_element_type=F32)
        below = below + jnp.dot(low_one[:, quarter:half], one_b[...].astype(BF16), preferred_element_type=F32)
        above = below[half:] + up[...] + jnp.where(odd[0] > 0, 0.0, pair[...])
        coupled = jnp.sum(v2_a[...] * below[:half], axis=0, keepdims=True)
        coupled = coupled + jnp.sum(v2_b[...] * above, axis=0, keepdims=True)
        out[...] = moments[...]
        out[5:6] = moments[5:6] + 2.0 * coupled

    operands = [odd, low_one, low_two, one_a, one_b, two, *v2, up, pair, moments]
    return local(kernel, [like(8, two.shape[1])], operands, 1)[0]


def group_rows(genotypes, groups, group):
    rows = genotypes.shape[0] // groups
    return genotypes[pl.ds(pl.multiple_of(group * rows, rows), rows)]


def partial_scores(row, groups, pieces, penalty, v0, v1, v2, genotypes):
    people, k = genotypes.shape[0], v0.shape[1]
    half = jax.ShapeDtypeStruct((groups // 2, people // groups, k), F32)

    def send_kernel(row, pieces, penalty, v0, v1_a, v1_b, v2_a, v2_b, genotypes, effects, rounded, send):
        sums = pieces[0]
        for piece in range(1, pieces.shape[0]):
            sums = sums + pieces[piece]
        moments = [sums[m : m + 1] for m in range(6)]
        c0, c1, c2 = coefficients(moments, penalty[...])
        value = c0 * v0[...] + c1 * joined((v1_a, v1_b)) + c2 * joined((v2_a, v2_b))
        effects[...] = value
        narrow = value.astype(BF16)
        rounded[...] = narrow
        other = 1 - row[0] % 2
        for g in range(groups // 2):
            send[g] = jnp.dot(group_rows(genotypes, groups, 2 * g + other), narrow, preferred_element_type=F32)

    def keep_kernel(row, rounded, genotypes, keep):
        mine = row[0] % 2
        for g in range(groups // 2):
            keep[g] = jnp.dot(group_rows(genotypes, groups, 2 * g + mine), rounded[...], preferred_element_type=F32)

    outs = [like(*v0.shape), like(*v0.shape, BF16), half]
    effects, rounded, send = local(send_kernel, outs, [row, pieces, penalty, v0, *v1, *v2, genotypes], 1)
    return effects, send, local(keep_kernel, [half], [row, rounded, genotypes], 1)[0]


def pick(index, keep, received):
    def kernel(index, keep, received, mine, other):
        mine[...] = keep[index[0]] + received[index[0]]
        other[...] = keep[1 - index[0]] + received[1 - index[0]]

    return local(kernel, [jax.ShapeDtypeStruct(keep.shape[1:], F32)] * 2, [index, keep, received], 1)


def scattered_over(values, axis):
    n = lax.axis_size(axis)
    pieces = values.reshape((n, values.shape[0] // n) + values.shape[1:])
    return jnp.sum(lax.all_to_all(pieces, axis, 0, 0, tiled=True), axis=0)


def coefficients(moments, penalty):
    def inner(u, v):
        return sum(a * b * moments[i + j] for i, a in enumerate(u) for j, b in enumerate(v))

    n0 = moments[0]
    a0 = n0 / (moments[1] + penalty * n0)
    r1 = [1.0 - a0 * penalty, -a0]
    n1 = inner(r1, r1)
    b0 = n1 / n0
    d1 = [r1[0] + b0, r1[1]]
    ad1 = [penalty * d1[0], d1[0] + penalty * d1[1], d1[1]]
    a1 = n1 / inner(d1, ad1)
    e1 = [a0 + a1 * d1[0], a1 * d1[1]]
    r2 = [r1[0] - a1 * ad1[0], r1[1] - a1 * ad1[1], -a1 * ad1[2]]
    n2 = inner(r2, r2)
    b1 = n2 / n1
    d2 = [r2[0] + b1 * d1[0], r2[1] + b1 * d1[1], r2[2]]
    ad2 = [penalty * d2[0], d2[0] + penalty * d2[1], d2[1] + penalty * d2[2], d2[2]]
    a2 = n2 / inner(d2, ad2)
    return e1[0] + a2 * d2[0], e1[1] + a2 * d2[1], a2 * d2[2]


def swapped(block, bit):
    return lax.ppermute(block, AXES, [(i, i ^ bit) for i in range(lax.axis_size(AXES))])


def body(marginal, penalty, ld_diag, ld_low, band, genotypes):
    n = lax.axis_size(AXES)
    rows, cols = lax.axis_size("row"), lax.axis_size("col")
    place = lax.axis_index(AXES).astype(jnp.int32)
    row = lax.axis_index("row").astype(jnp.int32)
    odd = (place % 2)[None]

    def halos(vec, two, first, second):
        one_a, one_b = first()
        pairs = swapped(one_a, 1), swapped(one_b, 1)
        far_a, far_b = second(one_b)
        chosen_a, chosen_b = choose(odd, vec, two, far_b, 2)
        one = swapped(chosen_a, 1), swapped(chosen_b, 1)
        sum_a = relay(odd, far_a, pairs[0], chosen_b)
        sum_b = relay(odd, far_b, pairs[1], sum_a)
        return sum_b, one, (shifted(sum_a, -2), shifted(sum_b, -2)), pairs

    v0 = marginal
    two = shifted(v0, 2)
    lows = []

    def second_tile(after):
        vec, _ = lax.optimization_barrier((v0, after))
        *products, low_one, low_two = from_tiles(second_kernel, 2, 2, 46, band, place[None], vec, ld_low[0])
        lows.extend((low_one, low_two))
        return products

    last_sum, one, ups, pairs = halos(
        (v0,), (two,), lambda: from_tiles(first_kernel, 1, 0, 58, band, place[None], v0, ld_low[0]), second_tile
    )
    low_one, low_two = lows
    diag, own = first_diag(v0, ld_diag[0], last_sum)
    part = add_two(own, low_two, (two,))
    v1_a = finish(0, odd, part, low_one, one, ups[0], pairs[0])
    two_a = shifted(v1_a, 2)
    v1_b = finish(1, odd, part, low_one, one, ups[1], pairs[1], v1_a)
    two_b = shifted(v1_b, 2)
    v1 = v1_a, v1_b

    products = coupling(v1, low_one, low_two)
    last_sum, one, ups, pairs = halos(v1, (two_a, two_b), lambda: products[:2], lambda after: products[2:])
    part = add_two(diag_times(v1, diag, last_sum), low_two, (two_a, two_b))
    v2_a = finish(0, odd, part, low_one, one, ups[0], pairs[0])
    two = shifted(v2_a, 2)
    v2_b = finish(1, odd, part, low_one, one, ups[1], pairs[1], v2_a)
    v2 = v2_a, v2_b

    one, far = lower_coupling(v2, low_one, low_two)
    pair = swapped(one, 1)
    above = relay(odd, far, pair, far)
    up = shifted(above, -2)
    chosen_a, chosen_b = choose(odd, (v2_a,), (two,), above, 2)
    moments = own_moments(v0, v1, v2, diag, chosen_b)
    one_a, one_b = swapped(chosen_a, 1), swapped(chosen_b, 1)
    moments = last(odd, low_one, low_two, one_a, one_b, two, v2, up, pair, moments)
    pieces = lax.all_to_all(jnp.broadcast_to(moments[None], (n,) + moments.shape), AXES, 0, 0, tiled=True)

    effects, send, keep = partial_scores(row[None], rows, pieces, penalty[None], v0, v1, v2, genotypes)
    received = swapped(send, cols)
    bit = rows // 4
    while bit:
        keep, received = [value.reshape((2, -1) + value.shape[1:]) for value in (keep, received)]
        keep, send = pick((row // (2 * bit) % 2)[None], keep, received)
        received = swapped(send, 2 * bit * cols)
        bit //= 2
    return effects, scattered_over((keep + received)[0], "col")


def solution(mesh):
    placed = (
        P(AXES, None),
        P(),
        P(AXES, None, None),
        P(AXES, None, None, None),
        P(AXES),
        P(None, AXES),
    )
    return jax.shard_map(
        body,
        mesh=mesh,
        in_specs=placed,
        out_specs=(P(AXES, None), P(AXES, None)),
        check_vma=False,
    )
```

```python
import functools

import jax
import jax.numpy as jnp
from jax import lax
from jax.experimental import pallas as pl
from jax.experimental.pallas import tpu as pltpu
from jax.sharding import PartitionSpec as P

AXES = ("row", "col")
F32 = jnp.float32
BF16 = jnp.bfloat16
MIB = 1024 * 1024
VMEM = pl.BlockSpec(memory_space=pltpu.VMEM)
SMEM = pl.BlockSpec(memory_space=pltpu.SMEM)
ANY = pl.BlockSpec(memory_space=pl.ANY)


def params(mib=20):
    return pltpu.CompilerParams(vmem_limit_bytes=mib * MIB)


def cost(flops, num_bytes):
    return pl.CostEstimate(flops=int(flops), bytes_accessed=int(num_bytes), transcendentals=0)


def shifted(block, distance):
    n = lax.axis_size(AXES)
    route = [(i - distance, i) for i in range(n) if 0 <= i - distance < n]
    return lax.ppermute(block, AXES, route)


def active(d, band, position):
    return jnp.logical_and(band[0] >= d + 1, position[0] >= d + 1)


def split_store(value, first, second):
    half = first.shape[0]
    first[...] = value[:half]
    second[...] = value[half:]


GROUP = 4


def fetched(low, tiles, arrived, order):
    count, rows = tiles.shape[0] // len(order), tiles.shape[1]
    copies = []
    for place in range(tiles.shape[0]):
        source = low.at[order[place // count], pl.ds(place % count * rows, rows)]
        copies.append(pltpu.make_async_copy(source, tiles.at[place], arrived.at[place]))
        copies[-1].start()
    return copies


def rounded_rows(copies, tiles, place, alive):
    for copy in copies[place : place + GROUP]:
        copy.wait()
    tile = tiles[place : place + GROUP].reshape(GROUP * tiles.shape[1], tiles.shape[2])
    return jnp.where(alive, tile, 0.0).astype(BF16)


def first_kernel(band, position, vec, low, one_a, one_b, own, tiles, arrived):
    fetch = pltpu.make_async_copy(vec, own, arrived.at[tiles.shape[0]])
    fetch.start()
    copies = fetched(low, tiles, arrived, (0,))
    fetch.wait()
    across = own[...].T.astype(BF16)
    rows = GROUP * tiles.shape[1]
    acc = None
    for place in range(0, tiles.shape[0], GROUP):
        tile = rounded_rows(copies, tiles, place, active(0, band, position))
        start = place * tiles.shape[1]
        term = jnp.dot(across[:, start : start + rows], tile, preferred_element_type=F32)
        acc = term if acc is None else acc + term
    split_store(acc.T, one_a, one_b)


def second_kernel(band, position, vec, low, far_a, far_b, low_one, low_two, own, tiles, arrived):
    fetch = pltpu.make_async_copy(vec, own, arrived.at[tiles.shape[0]])
    fetch.start()
    copies = fetched(low, tiles, arrived, (1, 0))
    fetch.wait()
    across = own[...].T.astype(BF16)
    rows = GROUP * tiles.shape[1]
    count = tiles.shape[0] // 2
    acc = None
    for place in range(0, count, GROUP):
        tile = rounded_rows(copies, tiles, place, active(1, band, position))
        start = place * tiles.shape[1]
        low_two[start : start + rows] = tile
        term = jnp.dot(across[:, start : start + rows], tile, preferred_element_type=F32)
        acc = term if acc is None else acc + term
    split_store(acc.T, far_a, far_b)
    for place in range(0, count, GROUP):
        start = place * tiles.shape[1]
        low_one[start : start + rows] = rounded_rows(copies, tiles, count + place, active(0, band, position))


def from_tiles(kernel, tiles, narrow, mib, band, position, vec, low):
    size, k = vec.shape
    count = 16
    return pl.pallas_call(
        kernel,
        in_specs=[SMEM] * 2 + [pl.BlockSpec(memory_space=pltpu.HBM)] * 2,
        out_specs=[VMEM] * (2 + narrow),
        out_shape=[jax.ShapeDtypeStruct((size // 2, k), F32)] * 2 + [jax.ShapeDtypeStruct((size, size), BF16)] * narrow,
        scratch_shapes=[
            pltpu.VMEM((size, k), F32),
            pltpu.VMEM((tiles * count, size // count, size), F32),
            pltpu.SemaphoreType.DMA((tiles * count + 1,)),
        ],
        compiler_params=params(mib),
        cost_estimate=cost(2 * size * size * k, 4 * tiles * size * size),
    )(band, position, vec, low)


def coupling_kernel(vec, low_one, low_two, one_a, one_b, far_a, far_b):
    across = vec[...].T.astype(BF16)
    split_store(jnp.dot(across, low_one[...], preferred_element_type=F32).T, one_a, one_b)
    split_store(jnp.dot(across, low_two[...], preferred_element_type=F32).T, far_a, far_b)


def coupling(vec, low_one, low_two):
    size, k = vec.shape
    return pl.pallas_call(
        coupling_kernel,
        in_specs=[VMEM] * 3,
        out_specs=[VMEM] * 4,
        out_shape=[jax.ShapeDtypeStruct((size // 2, k), F32)] * 4,
        compiler_params=params(),
        cost_estimate=cost(4 * size * size * k, 4 * size * size),
    )(vec, low_one, low_two)


def relay_kernel(odd, far, pair, after, out):
    out[...] = far[...] + jnp.where(odd[0] > 0, pair[...], 0.0)


def choose_kernel(odd, vec, two, after, *parts):
    rows = parts[0].shape[0]
    for place, part in enumerate(parts):
        here = slice(place * rows, (place + 1) * rows)
        part[...] = jnp.where(odd[0] > 0, two[here], vec[here])


def choose(odd, vec, two, after, parts):
    rows, k = vec.shape
    return pl.pallas_call(
        choose_kernel,
        in_specs=[SMEM, VMEM, VMEM, ANY],
        out_specs=[VMEM] * parts,
        out_shape=[jax.ShapeDtypeStruct((rows // parts, k), F32)] * parts,
        compiler_params=params(),
        cost_estimate=cost(vec.size, 12 * vec.size),
    )(odd, vec, two, after)


def relay(odd, far, pair, after):
    return pl.pallas_call(
        relay_kernel,
        in_specs=[SMEM, VMEM, VMEM, ANY],
        out_specs=VMEM,
        out_shape=jax.ShapeDtypeStruct(far.shape, F32),
        compiler_params=params(),
        cost_estimate=cost(far.size, 12 * far.size),
    )(odd, far, pair, after)


def first_diag_kernel(vec, diag, after, narrow, product):
    tile = diag[...].astype(BF16)
    rest = (diag[...] - tile.astype(F32)).astype(BF16)
    narrow[...] = tile
    value = vec[...]
    high = value.astype(BF16)
    low = (value - high.astype(F32)).astype(BF16)
    both = jnp.dot(tile, jnp.concatenate([high, low], axis=1), preferred_element_type=F32)
    k = value.shape[1]
    product[...] = both[:, :k] + both[:, k:] + jnp.dot(rest, high, preferred_element_type=F32)


def first_diag(vec, diag, after):
    size, k = vec.shape
    rows = size // 4
    return pl.pallas_call(
        first_diag_kernel,
        grid=(4,),
        in_specs=[pl.BlockSpec((size, k), lambda r: (0, 0)), pl.BlockSpec((rows, size), lambda r: (r, 0)), ANY],
        out_specs=[pl.BlockSpec((rows, size), lambda r: (r, 0)), pl.BlockSpec((rows, k), lambda r: (r, 0))],
        out_shape=[jax.ShapeDtypeStruct(diag.shape, BF16), jax.ShapeDtypeStruct(vec.shape, F32)],
        compiler_params=params(),
        cost_estimate=cost(2 * size * size * k, 6 * size * size),
    )(vec, diag, after)


def diag_kernel(vec, diag, after, product):
    product[...] = jnp.dot(diag[...], vec[...].astype(BF16), preferred_element_type=F32)


def diag_times(vec, diag, after):
    size, k = vec.shape
    return pl.pallas_call(
        diag_kernel,
        in_specs=[VMEM, VMEM, ANY],
        out_specs=VMEM,
        out_shape=jax.ShapeDtypeStruct(vec.shape, F32),
        compiler_params=params(),
        cost_estimate=cost(2 * size * size * k, 6 * size * size),
    )(vec, diag, after)


def finish_kernel(odd, part, low, one, ahead_a, ahead_b, pair_a, pair_b, out, *upper):
    acc = jnp.dot(low[...], one[...].astype(BF16), preferred_element_type=F32) + part[...]
    half = ahead_a.shape[0]
    for place, (straight, pair) in enumerate(((ahead_a, pair_a), (ahead_b, pair_b))):
        rows = slice(place * half, (place + 1) * half)
        out[rows] = acc[rows] + straight[...] + jnp.where(odd[0] > 0, 0.0, pair[...])
    for copy in upper:
        copy[...] = out[:half]


def finish(odd, uppers, part, low, *arrived):
    size, k = part.shape
    return pl.pallas_call(
        finish_kernel,
        in_specs=[SMEM] + [VMEM] * 7,
        out_specs=[VMEM] * (1 + uppers),
        out_shape=[jax.ShapeDtypeStruct(part.shape, F32)] + [jax.ShapeDtypeStruct((size // 2, k), F32)] * uppers,
        compiler_params=params(),
        cost_estimate=cost(2 * size * size * k, 2 * size * size),
    )(odd, part, low, *arrived)


def two_kernel(own, low, two, product):
    product[...] = own[...] + jnp.dot(low[...], two[...].astype(BF16), preferred_element_type=F32)


def add_two(own, low, two):
    size, k = two.shape
    return pl.pallas_call(
        two_kernel,
        in_specs=[VMEM] * 3,
        out_specs=VMEM,
        out_shape=jax.ShapeDtypeStruct(two.shape, F32),
        compiler_params=params(),
        cost_estimate=cost(2 * size * size * k, 2 * size * size),
    )(own, low, two)


def lower_kernel(vec, low_one, low_two, one, far):
    across = vec[...].T.astype(BF16)
    half = one.shape[0]
    one[...] = jnp.dot(across, low_one[:, half:], preferred_element_type=F32).T
    far[...] = jnp.dot(across, low_two[:, half:], preferred_element_type=F32).T


def lower_coupling(vec, low_one, low_two):
    size, k = vec.shape
    return pl.pallas_call(
        lower_kernel,
        in_specs=[VMEM] * 3,
        out_specs=[VMEM] * 2,
        out_shape=[jax.ShapeDtypeStruct((size // 2, k), F32)] * 2,
        compiler_params=params(),
        cost_estimate=cost(2 * size * size * k, 2 * size * size),
    )(vec, low_one, low_two)


def own_kernel(v0, v1, v2, diag, after, moments):
    image = jnp.dot(diag[...], v2[...].astype(BF16), preferred_element_type=F32)
    pairs = [(v0, v0), (v0, v1), (v1, v1), (v1, v2), (v2, v2)]
    for row, (a, b) in enumerate(pairs):
        moments[row : row + 1] = jnp.sum(a[...] * b[...], axis=0, keepdims=True)
    moments[5:6] = jnp.sum(v2[...] * image, axis=0, keepdims=True)
    moments[6:8] = jnp.zeros_like(moments[6:8])


def own_moments(v0, v1, v2, diag, after):
    size, k = v0.shape
    return pl.pallas_call(
        own_kernel,
        in_specs=[VMEM] * 4 + [ANY],
        out_specs=VMEM,
        out_shape=jax.ShapeDtypeStruct((8, k), F32),
        compiler_params=params(),
        cost_estimate=cost(2 * size * size * k, 6 * size * size),
    )(v0, v1, v2, diag, after)


def last_kernel(odd, low_one, low_two, one_a, one_b, two, v2, up, pair, moments, out):
    quarter, half = one_a.shape[0], two.shape[0]
    below = jnp.dot(low_two[:, :half], two[...].astype(BF16), preferred_element_type=F32)
    below = below + jnp.dot(low_one[:, :quarter], one_a[...].astype(BF16), preferred_element_type=F32)
    below = below + jnp.dot(low_one[:, quarter:half], one_b[...].astype(BF16), preferred_element_type=F32)
    above = up[...] + jnp.where(odd[0] > 0, 0.0, pair[...])
    coupled = jnp.sum(v2[...] * below, axis=0, keepdims=True) + jnp.sum(v2[half:] * above, axis=0, keepdims=True)
    whole = moments[...]
    row = lax.broadcasted_iota(jnp.int32, whole.shape, 0)
    whole = jnp.where(row == 5, whole + 2.0 * coupled, whole)
    for place in range(out.shape[0]):
        out[place] = whole


def last(odd, low_one, low_two, one_a, one_b, two, v2, up, pair, moments):
    size, k = v2.shape
    return pl.pallas_call(
        last_kernel,
        in_specs=[SMEM] + [VMEM] * 9,
        out_specs=VMEM,
        out_shape=jax.ShapeDtypeStruct((lax.axis_size(AXES), 8, k), F32),
        compiler_params=params(),
        cost_estimate=cost(2 * size * size * k, 2 * size * size),
    )(odd, low_one, low_two, one_a, one_b, two, v2, up, pair, moments)


def group_rows(genotypes, groups, group):
    rows = genotypes.shape[0] // groups
    return genotypes[pl.ds(pl.multiple_of(group * rows, rows), rows)]


def combined(pieces, penalty, v0, v1, v2):
    sums = pieces[0]
    for piece in range(1, pieces.shape[0]):
        sums = sums + pieces[piece]
    moments = [sums[m : m + 1] for m in range(6)]
    c0, c1, c2 = coefficients(moments, penalty[...])
    return c0 * v0[...] + c1 * v1[...] + c2 * v2[...]


def send_kernel(groups, row, pieces, penalty, v0, v1, v2, genotypes, send):
    narrow = combined(pieces, penalty, v0, v1, v2).astype(BF16)
    other = 1 - row[0] % 2
    for g in range(groups // 2):
        send[g] = jnp.dot(group_rows(genotypes, groups, 2 * g + other), narrow, preferred_element_type=F32)


def keep_kernel(groups, row, pieces, penalty, v0, v1, v2, genotypes, keep, effects):
    value = combined(pieces, penalty, v0, v1, v2)
    effects[...] = value
    mine = row[0] % 2
    for g in range(groups // 2):
        keep[g] = jnp.dot(group_rows(genotypes, groups, 2 * g + mine), value.astype(BF16), preferred_element_type=F32)


def partial_scores(*operands):
    row, groups, *arrays = operands
    v0, genotypes = arrays[2], arrays[5]
    people, size = genotypes.shape
    k = v0.shape[1]
    half = jax.ShapeDtypeStruct((groups // 2, people // groups, k), F32)
    results = []
    for kernel, outs in ((send_kernel, [half]), (keep_kernel, [half, jax.ShapeDtypeStruct(v0.shape, F32)])):
        results.extend(
            pl.pallas_call(
                functools.partial(kernel, groups),
                in_specs=[SMEM] + [VMEM] * len(arrays),
                out_specs=[VMEM] * len(outs),
                out_shape=outs,
                compiler_params=params(),
                cost_estimate=cost(people * size * k, 2 * people * size),
            )(row, *arrays)
        )
    return results


def sum_kernel(pieces, out):
    value = pieces[0]
    for piece in range(1, pieces.shape[0]):
        value = value + pieces[piece]
    out[...] = value


def pick_kernel(index, keep, received, mine, other):
    mine[...] = keep[index[0]] + received[index[0]]
    other[...] = keep[1 - index[0]] + received[1 - index[0]]


def pick(index, keep, received):
    half = jax.ShapeDtypeStruct(keep.shape[1:], F32)
    return pl.pallas_call(
        pick_kernel,
        in_specs=[SMEM, VMEM, VMEM],
        out_specs=[VMEM] * 2,
        out_shape=[half] * 2,
        compiler_params=params(),
        cost_estimate=cost(keep.size, 12 * keep.size),
    )(index, keep, received)


def scattered_over(values, axis):
    n = lax.axis_size(axis)
    pieces = values.reshape((n, values.shape[0] // n) + values.shape[1:])
    pieces = lax.all_to_all(pieces, axis, 0, 0, tiled=True)
    return pl.pallas_call(
        sum_kernel,
        in_specs=[VMEM],
        out_specs=VMEM,
        out_shape=jax.ShapeDtypeStruct(pieces.shape[1:], F32),
        compiler_params=params(),
        cost_estimate=cost(pieces.size, 4 * pieces.size),
    )(pieces)


def routed(block, pairs):
    return lax.ppermute(block, AXES, pairs)


def coefficients(moments, penalty):
    def inner(u, v):
        return sum(a * b * moments[i + j] for i, a in enumerate(u) for j, b in enumerate(v))

    n0 = moments[0]
    a0 = n0 / (moments[1] + penalty * n0)
    r1 = [1.0 - a0 * penalty, -a0]
    n1 = inner(r1, r1)
    b0 = n1 / n0
    d1 = [r1[0] + b0, r1[1]]
    ad1 = [penalty * d1[0], d1[0] + penalty * d1[1], d1[1]]
    a1 = n1 / inner(d1, ad1)
    e1 = [a0 + a1 * d1[0], a1 * d1[1]]
    r2 = [r1[0] - a1 * ad1[0], r1[1] - a1 * ad1[1], -a1 * ad1[2]]
    n2 = inner(r2, r2)
    b1 = n2 / n1
    d2 = [r2[0] + b1 * d1[0], r2[1] + b1 * d1[1], r2[2]]
    ad2 = [penalty * d2[0], d2[0] + penalty * d2[1], d2[1] + penalty * d2[2], d2[2]]
    a2 = n2 / inner(d2, ad2)
    return e1[0] + a2 * d2[0], e1[1] + a2 * d2[1], a2 * d2[2]


def swapped(block, bit):
    return routed(block, [(i, i ^ bit) for i in range(lax.axis_size(AXES))])


def body(marginal, penalty, ld_diag, ld_low, band, genotypes):
    n = lax.axis_size(AXES)
    rows, cols = lax.axis_size("row"), lax.axis_size("col")
    position = lax.axis_index(AXES)
    row = lax.axis_index("row")
    site = position.astype(jnp.int32)[None]
    odd = (position % 2).astype(jnp.int32)[None]
    half = marginal.shape[0] // 2

    def halos(vec, two, first, second):
        one_a, one_b = first()
        pair_a, pair_b = swapped(one_a, 1), swapped(one_b, 1)
        far_a, far_b = second(one_b)
        sum_a = relay(odd, far_a, pair_a, far_b)
        up_a = shifted(sum_a, -2)
        [chosen] = choose(odd, vec, two, sum_a, 1)
        one = swapped(chosen, 1)
        sum_b = relay(odd, far_b, pair_b, chosen)
        return sum_b, (one, up_a, shifted(sum_b, -2), pair_a, pair_b)

    v0 = marginal
    two = shifted(v0, 2)

    lows = []

    def second_tile(after):
        vec, _ = lax.optimization_barrier((v0, after))
        *products, low_one, low_two = from_tiles(second_kernel, 2, 2, 46, band, site, vec, ld_low[0])
        lows.extend((low_one, low_two))
        return products

    last_sum, arrived = halos(
        v0, two, lambda: from_tiles(first_kernel, 1, 0, 58, band, site, v0, ld_low[0]), second_tile
    )
    low_one, low_two = lows
    diag, own = first_diag(v0, ld_diag[0], last_sum)
    [v1] = finish(odd, 0, add_two(own, low_two, two), low_one, *arrived)

    two = shifted(v1, 2)
    products = coupling(v1, low_one, low_two)
    last_sum, arrived = halos(v1, two, lambda: products[:2], lambda after: products[2:])
    own = diag_times(v1, diag, last_sum)
    v2, upper = finish(odd, 1, add_two(own, low_two, two), low_one, *arrived)

    two = shifted(upper, 2)
    one, far = lower_coupling(v2, low_one, low_two)
    pair = swapped(one, 1)
    above = relay(odd, far, pair, far)
    up = shifted(above, -2)
    chosen_a, chosen_b = choose(odd, upper, two, above, 2)
    moments = own_moments(v0, v1, v2, diag, chosen_b)
    one_a, one_b = swapped(chosen_a, 1), swapped(chosen_b, 1)
    moments = last(odd, low_one, low_two, one_a, one_b, two, v2, up, pair, moments)
    pieces = lax.all_to_all(moments, AXES, 0, 0, tiled=True)

    send, keep, effects = partial_scores(row.astype(jnp.int32)[None], rows, pieces, penalty[None], v0, v1, v2, genotypes)
    received = swapped(send, cols)
    bit = rows // 4
    while bit:
        mine = (row // (2 * bit)) % 2
        keep = keep.reshape((2, -1) + keep.shape[1:])
        received = received.reshape((2, -1) + received.shape[1:])

        keep, send = pick(mine.astype(jnp.int32)[None], keep, received)
        received = swapped(send, 2 * bit * cols)
        bit //= 2
    return effects, scattered_over((keep + received)[0], "col")


def solution(mesh):
    placed = (
        P(AXES, None),
        P(),
        P(AXES, None, None),
        P(AXES, None, None, None),
        P(AXES),
        P(None, AXES),
    )
    return jax.shard_map(
        body,
        mesh=mesh,
        in_specs=placed,
        out_specs=(P(AXES, None), P(AXES, None)),
        check_vma=False,
    )
```

```python
import functools

import jax
import jax.numpy as jnp
from jax import lax
from jax.experimental import pallas as pl
from jax.experimental.pallas import tpu as pltpu
from jax.sharding import PartitionSpec as P

AXES = ("row", "col")
F32 = jnp.float32
BF16 = jnp.bfloat16
MIB = 1024 * 1024
VMEM = pl.BlockSpec(memory_space=pltpu.VMEM)
SMEM = pl.BlockSpec(memory_space=pltpu.SMEM)
ANY = pl.BlockSpec(memory_space=pl.ANY)


def params(mib=20):
    return pltpu.CompilerParams(vmem_limit_bytes=mib * MIB)


def cost(flops, num_bytes):
    return pl.CostEstimate(flops=int(flops), bytes_accessed=int(num_bytes), transcendentals=0)


def shifted(block, distance):
    n = lax.axis_size(AXES)
    route = [(i - distance, i) for i in range(n) if 0 <= i - distance < n]
    return lax.ppermute(block, AXES, route)


def active(d, band, position):
    return jnp.logical_and(band[0] >= d + 1, position[0] >= d + 1)


def split_store(value, first, second):
    half = first.shape[0]
    first[...] = value[:half]
    second[...] = value[half:]


GROUP = 4


def fetched(low, tiles, arrived, order):
    count, rows = tiles.shape[0] // len(order), tiles.shape[1]
    copies = []
    for place in range(tiles.shape[0]):
        source = low.at[order[place // count], pl.ds(place % count * rows, rows)]
        copies.append(pltpu.make_async_copy(source, tiles.at[place], arrived.at[place]))
        copies[-1].start()
    return copies


def rounded_rows(copies, tiles, place, alive):
    for copy in copies[place : place + GROUP]:
        copy.wait()
    tile = tiles[place : place + GROUP].reshape(GROUP * tiles.shape[1], tiles.shape[2])
    return jnp.where(alive, tile, 0.0).astype(BF16)


def first_kernel(band, position, vec, low, one_a, one_b, own, tiles, arrived):
    fetch = pltpu.make_async_copy(vec, own, arrived.at[tiles.shape[0]])
    fetch.start()
    copies = fetched(low, tiles, arrived, (0,))
    fetch.wait()
    across = own[...].T.astype(BF16)
    rows = GROUP * tiles.shape[1]
    acc = None
    for place in range(0, tiles.shape[0], GROUP):
        tile = rounded_rows(copies, tiles, place, active(0, band, position))
        start = place * tiles.shape[1]
        term = jnp.dot(across[:, start : start + rows], tile, preferred_element_type=F32)
        acc = term if acc is None else acc + term
    split_store(acc.T, one_a, one_b)


def second_kernel(band, position, vec, low, far_a, far_b, low_one, low_two, own, tiles, arrived):
    fetch = pltpu.make_async_copy(vec, own, arrived.at[tiles.shape[0]])
    fetch.start()
    copies = fetched(low, tiles, arrived, (1, 0))
    fetch.wait()
    across = own[...].T.astype(BF16)
    rows = GROUP * tiles.shape[1]
    count = tiles.shape[0] // 2
    acc = None
    for place in range(0, count, GROUP):
        tile = rounded_rows(copies, tiles, place, active(1, band, position))
        start = place * tiles.shape[1]
        low_two[start : start + rows] = tile
        term = jnp.dot(across[:, start : start + rows], tile, preferred_element_type=F32)
        acc = term if acc is None else acc + term
    split_store(acc.T, far_a, far_b)
    for place in range(0, count, GROUP):
        start = place * tiles.shape[1]
        low_one[start : start + rows] = rounded_rows(copies, tiles, count + place, active(0, band, position))


def from_tiles(kernel, tiles, narrow, mib, band, position, vec, low):
    size, k = vec.shape
    count = 16
    return pl.pallas_call(
        kernel,
        in_specs=[SMEM] * 2 + [pl.BlockSpec(memory_space=pltpu.HBM)] * 2,
        out_specs=[VMEM] * (2 + narrow),
        out_shape=[jax.ShapeDtypeStruct((size // 2, k), F32)] * 2 + [jax.ShapeDtypeStruct((size, size), BF16)] * narrow,
        scratch_shapes=[
            pltpu.VMEM((size, k), F32),
            pltpu.VMEM((tiles * count, size // count, size), F32),
            pltpu.SemaphoreType.DMA((tiles * count + 1,)),
        ],
        compiler_params=params(mib),
        cost_estimate=cost(2 * size * size * k, 4 * tiles * size * size),
    )(band, position, vec, low)


def coupling_kernel(vec, low_one, low_two, one_a, one_b, far_a, far_b):
    across = vec[...].T.astype(BF16)
    split_store(jnp.dot(across, low_one[...], preferred_element_type=F32).T, one_a, one_b)
    split_store(jnp.dot(across, low_two[...], preferred_element_type=F32).T, far_a, far_b)


def coupling(vec, low_one, low_two):
    size, k = vec.shape
    return pl.pallas_call(
        coupling_kernel,
        in_specs=[VMEM] * 3,
        out_specs=[VMEM] * 4,
        out_shape=[jax.ShapeDtypeStruct((size // 2, k), F32)] * 4,
        compiler_params=params(),
        cost_estimate=cost(4 * size * size * k, 4 * size * size),
    )(vec, low_one, low_two)


def relay_kernel(odd, far, pair, after, out):
    out[...] = far[...] + jnp.where(odd[0] > 0, pair[...], 0.0)


def choose_kernel(odd, vec, two, after, *parts):
    rows = parts[0].shape[0]
    for place, part in enumerate(parts):
        here = slice(place * rows, (place + 1) * rows)
        part[...] = jnp.where(odd[0] > 0, two[here], vec[here])


def choose(odd, vec, two, after, parts):
    rows, k = vec.shape
    return pl.pallas_call(
        choose_kernel,
        in_specs=[SMEM, VMEM, VMEM, ANY],
        out_specs=[VMEM] * parts,
        out_shape=[jax.ShapeDtypeStruct((rows // parts, k), F32)] * parts,
        compiler_params=params(),
        cost_estimate=cost(vec.size, 12 * vec.size),
    )(odd, vec, two, after)


def relay(odd, far, pair, after):
    return pl.pallas_call(
        relay_kernel,
        in_specs=[SMEM, VMEM, VMEM, ANY],
        out_specs=VMEM,
        out_shape=jax.ShapeDtypeStruct(far.shape, F32),
        compiler_params=params(),
        cost_estimate=cost(far.size, 12 * far.size),
    )(odd, far, pair, after)


def first_diag_kernel(vec, diag, after, narrow, product):
    tile = diag[...].astype(BF16)
    rest = (diag[...] - tile.astype(F32)).astype(BF16)
    narrow[...] = tile
    value = vec[...]
    high = value.astype(BF16)
    low = (value - high.astype(F32)).astype(BF16)
    both = jnp.dot(tile, jnp.concatenate([high, low], axis=1), preferred_element_type=F32)
    k = value.shape[1]
    product[...] = both[:, :k] + both[:, k:] + jnp.dot(rest, high, preferred_element_type=F32)


def first_diag(vec, diag, after):
    size, k = vec.shape
    rows = size // 4
    return pl.pallas_call(
        first_diag_kernel,
        grid=(4,),
        in_specs=[pl.BlockSpec((size, k), lambda r: (0, 0)), pl.BlockSpec((rows, size), lambda r: (r, 0)), ANY],
        out_specs=[pl.BlockSpec((rows, size), lambda r: (r, 0)), pl.BlockSpec((rows, k), lambda r: (r, 0))],
        out_shape=[jax.ShapeDtypeStruct(diag.shape, BF16), jax.ShapeDtypeStruct(vec.shape, F32)],
        compiler_params=params(),
        cost_estimate=cost(2 * size * size * k, 6 * size * size),
    )(vec, diag, after)


def diag_kernel(vec, diag, after, product):
    product[...] = jnp.dot(diag[...], vec[...].astype(BF16), preferred_element_type=F32)


def diag_times(vec, diag, after):
    size, k = vec.shape
    return pl.pallas_call(
        diag_kernel,
        in_specs=[VMEM, VMEM, ANY],
        out_specs=VMEM,
        out_shape=jax.ShapeDtypeStruct(vec.shape, F32),
        compiler_params=params(),
        cost_estimate=cost(2 * size * size * k, 6 * size * size),
    )(vec, diag, after)


def finish_kernel(odd, part, low, one, ahead_a, ahead_b, pair_a, pair_b, out, *upper):
    acc = jnp.dot(low[...], one[...].astype(BF16), preferred_element_type=F32) + part[...]
    half = ahead_a.shape[0]
    for place, (straight, pair) in enumerate(((ahead_a, pair_a), (ahead_b, pair_b))):
        rows = slice(place * half, (place + 1) * half)
        out[rows] = acc[rows] + straight[...] + jnp.where(odd[0] > 0, 0.0, pair[...])
    for copy in upper:
        copy[...] = out[:half]


def finish(odd, uppers, part, low, *arrived):
    size, k = part.shape
    return pl.pallas_call(
        finish_kernel,
        in_specs=[SMEM] + [VMEM] * 7,
        out_specs=[VMEM] * (1 + uppers),
        out_shape=[jax.ShapeDtypeStruct(part.shape, F32)] + [jax.ShapeDtypeStruct((size // 2, k), F32)] * uppers,
        compiler_params=params(),
        cost_estimate=cost(2 * size * size * k, 2 * size * size),
    )(odd, part, low, *arrived)


def two_kernel(own, low, two, product):
    product[...] = own[...] + jnp.dot(low[...], two[...].astype(BF16), preferred_element_type=F32)


def add_two(own, low, two):
    size, k = two.shape
    return pl.pallas_call(
        two_kernel,
        in_specs=[VMEM] * 3,
        out_specs=VMEM,
        out_shape=jax.ShapeDtypeStruct(two.shape, F32),
        compiler_params=params(),
        cost_estimate=cost(2 * size * size * k, 2 * size * size),
    )(own, low, two)


def lower_kernel(vec, low_one, low_two, one, far):
    across = vec[...].T.astype(BF16)
    half = one.shape[0]
    one[...] = jnp.dot(across, low_one[:, half:], preferred_element_type=F32).T
    far[...] = jnp.dot(across, low_two[:, half:], preferred_element_type=F32).T


def lower_coupling(vec, low_one, low_two):
    size, k = vec.shape
    return pl.pallas_call(
        lower_kernel,
        in_specs=[VMEM] * 3,
        out_specs=[VMEM] * 2,
        out_shape=[jax.ShapeDtypeStruct((size // 2, k), F32)] * 2,
        compiler_params=params(),
        cost_estimate=cost(2 * size * size * k, 2 * size * size),
    )(vec, low_one, low_two)


def own_kernel(v0, v1, v2, diag, after, moments):
    image = jnp.dot(diag[...], v2[...].astype(BF16), preferred_element_type=F32)
    pairs = [(v0, v0), (v0, v1), (v1, v1), (v1, v2), (v2, v2)]
    for row, (a, b) in enumerate(pairs):
        moments[row : row + 1] = jnp.sum(a[...] * b[...], axis=0, keepdims=True)
    moments[5:6] = jnp.sum(v2[...] * image, axis=0, keepdims=True)
    moments[6:8] = jnp.zeros_like(moments[6:8])


def own_moments(v0, v1, v2, diag, after):
    size, k = v0.shape
    return pl.pallas_call(
        own_kernel,
        in_specs=[VMEM] * 4 + [ANY],
        out_specs=VMEM,
        out_shape=jax.ShapeDtypeStruct((8, k), F32),
        compiler_params=params(),
        cost_estimate=cost(2 * size * size * k, 6 * size * size),
    )(v0, v1, v2, diag, after)


def last_kernel(odd, low_one, low_two, one_a, one_b, two, v2, up, pair, moments, out):
    quarter, half = one_a.shape[0], two.shape[0]
    below = jnp.dot(low_two[:, :half], two[...].astype(BF16), preferred_element_type=F32)
    below = below + jnp.dot(low_one[:, :quarter], one_a[...].astype(BF16), preferred_element_type=F32)
    below = below + jnp.dot(low_one[:, quarter:half], one_b[...].astype(BF16), preferred_element_type=F32)
    above = up[...] + jnp.where(odd[0] > 0, 0.0, pair[...])
    coupled = jnp.sum(v2[...] * below, axis=0, keepdims=True) + jnp.sum(v2[half:] * above, axis=0, keepdims=True)
    whole = moments[...]
    row = lax.broadcasted_iota(jnp.int32, whole.shape, 0)
    whole = jnp.where(row == 5, whole + 2.0 * coupled, whole)
    for place in range(out.shape[0]):
        out[place] = whole


def last(odd, low_one, low_two, one_a, one_b, two, v2, up, pair, moments):
    size, k = v2.shape
    return pl.pallas_call(
        last_kernel,
        in_specs=[SMEM] + [VMEM] * 9,
        out_specs=VMEM,
        out_shape=jax.ShapeDtypeStruct((lax.axis_size(AXES), 8, k), F32),
        compiler_params=params(),
        cost_estimate=cost(2 * size * size * k, 2 * size * size),
    )(odd, low_one, low_two, one_a, one_b, two, v2, up, pair, moments)


def group_rows(genotypes, groups, group):
    rows = genotypes.shape[0] // groups
    return genotypes[pl.ds(pl.multiple_of(group * rows, rows), rows)]


def combined(pieces, penalty, v0, v1, v2):
    sums = pieces[0]
    for piece in range(1, pieces.shape[0]):
        sums = sums + pieces[piece]
    moments = [sums[m : m + 1] for m in range(6)]
    c0, c1, c2 = coefficients(moments, penalty[...])
    return c0 * v0[...] + c1 * v1[...] + c2 * v2[...]


def send_kernel(groups, row, pieces, penalty, v0, v1, v2, genotypes, value, send):
    value[...] = combined(pieces, penalty, v0, v1, v2)
    narrow = value[...].astype(BF16)
    other = 1 - row[0] % 2
    for g in range(groups // 2):
        send[g] = jnp.dot(group_rows(genotypes, groups, 2 * g + other), narrow, preferred_element_type=F32)


def keep_kernel(groups, row, value, genotypes, keep, effects):
    narrow = value[...].astype(BF16)
    effects[...] = value[...]
    mine = row[0] % 2
    for g in range(groups // 2):
        keep[g] = jnp.dot(group_rows(genotypes, groups, 2 * g + mine), narrow, preferred_element_type=F32)


def partial_scores(row, groups, pieces, penalty, v0, v1, v2, genotypes):
    people, size = genotypes.shape
    k = v0.shape[1]
    whole = jax.ShapeDtypeStruct(v0.shape, F32)
    half = jax.ShapeDtypeStruct((groups // 2, people // groups, k), F32)

    def call(kernel, outs, *operands):
        return pl.pallas_call(
            functools.partial(kernel, groups),
            in_specs=[SMEM] + [VMEM] * (len(operands) - 1),
            out_specs=[VMEM] * 2,
            out_shape=outs,
            compiler_params=params(),
            cost_estimate=cost(people * size * k, 2 * people * size),
        )(*operands)

    value, send = call(send_kernel, [whole, half], row, pieces, penalty, v0, v1, v2, genotypes)
    keep, effects = call(keep_kernel, [half, whole], row, value, genotypes)
    return send, keep, effects


def sum_kernel(pieces, out):
    value = pieces[0]
    for piece in range(1, pieces.shape[0]):
        value = value + pieces[piece]
    out[...] = value


def pick_kernel(index, keep, received, mine, other):
    mine[...] = keep[index[0]] + received[index[0]]
    other[...] = keep[1 - index[0]] + received[1 - index[0]]


def pick(index, keep, received):
    half = jax.ShapeDtypeStruct(keep.shape[1:], F32)
    return pl.pallas_call(
        pick_kernel,
        in_specs=[SMEM, VMEM, VMEM],
        out_specs=[VMEM] * 2,
        out_shape=[half] * 2,
        compiler_params=params(),
        cost_estimate=cost(keep.size, 12 * keep.size),
    )(index, keep, received)


def scattered_over(values, axis):
    n = lax.axis_size(axis)
    pieces = values.reshape((n, values.shape[0] // n) + values.shape[1:])
    pieces = lax.all_to_all(pieces, axis, 0, 0, tiled=True)
    return pl.pallas_call(
        sum_kernel,
        in_specs=[VMEM],
        out_specs=VMEM,
        out_shape=jax.ShapeDtypeStruct(pieces.shape[1:], F32),
        compiler_params=params(),
        cost_estimate=cost(pieces.size, 4 * pieces.size),
    )(pieces)


def routed(block, pairs):
    return lax.ppermute(block, AXES, pairs)


def coefficients(moments, penalty):
    def inner(u, v):
        return sum(a * b * moments[i + j] for i, a in enumerate(u) for j, b in enumerate(v))

    n0 = moments[0]
    a0 = n0 / (moments[1] + penalty * n0)
    r1 = [1.0 - a0 * penalty, -a0]
    n1 = inner(r1, r1)
    b0 = n1 / n0
    d1 = [r1[0] + b0, r1[1]]
    ad1 = [penalty * d1[0], d1[0] + penalty * d1[1], d1[1]]
    a1 = n1 / inner(d1, ad1)
    e1 = [a0 + a1 * d1[0], a1 * d1[1]]
    r2 = [r1[0] - a1 * ad1[0], r1[1] - a1 * ad1[1], -a1 * ad1[2]]
    n2 = inner(r2, r2)
    b1 = n2 / n1
    d2 = [r2[0] + b1 * d1[0], r2[1] + b1 * d1[1], r2[2]]
    ad2 = [penalty * d2[0], d2[0] + penalty * d2[1], d2[1] + penalty * d2[2], d2[2]]
    a2 = n2 / inner(d2, ad2)
    return e1[0] + a2 * d2[0], e1[1] + a2 * d2[1], a2 * d2[2]


def swapped(block, bit):
    return routed(block, [(i, i ^ bit) for i in range(lax.axis_size(AXES))])


def body(marginal, penalty, ld_diag, ld_low, band, genotypes):
    n = lax.axis_size(AXES)
    rows, cols = lax.axis_size("row"), lax.axis_size("col")
    position = lax.axis_index(AXES)
    row = lax.axis_index("row")
    site = position.astype(jnp.int32)[None]
    odd = (position % 2).astype(jnp.int32)[None]
    half = marginal.shape[0] // 2

    def halos(vec, two, first, second):
        one_a, one_b = first()
        pair_a, pair_b = swapped(one_a, 1), swapped(one_b, 1)
        far_a, far_b = second(one_b)
        sum_a = relay(odd, far_a, pair_a, far_b)
        up_a = shifted(sum_a, -2)
        [chosen] = choose(odd, vec, two, sum_a, 1)
        one = swapped(chosen, 1)
        sum_b = relay(odd, far_b, pair_b, chosen)
        return sum_b, (one, up_a, shifted(sum_b, -2), pair_a, pair_b)

    v0 = marginal
    two = shifted(v0, 2)

    lows = []

    def second_tile(after):
        vec, _ = lax.optimization_barrier((v0, after))
        *products, low_one, low_two = from_tiles(second_kernel, 2, 2, 46, band, site, vec, ld_low[0])
        lows.extend((low_one, low_two))
        return products

    last_sum, arrived = halos(
        v0, two, lambda: from_tiles(first_kernel, 1, 0, 58, band, site, v0, ld_low[0]), second_tile
    )
    low_one, low_two = lows
    diag, own = first_diag(v0, ld_diag[0], last_sum)
    [v1] = finish(odd, 0, add_two(own, low_two, two), low_one, *arrived)

    two = shifted(v1, 2)
    products = coupling(v1, low_one, low_two)
    last_sum, arrived = halos(v1, two, lambda: products[:2], lambda after: products[2:])
    own = diag_times(v1, diag, last_sum)
    v2, upper = finish(odd, 1, add_two(own, low_two, two), low_one, *arrived)

    two = shifted(upper, 2)
    one, far = lower_coupling(v2, low_one, low_two)
    pair = swapped(one, 1)
    above = relay(odd, far, pair, far)
    up = shifted(above, -2)
    chosen_a, chosen_b = choose(odd, upper, two, above, 2)
    moments = own_moments(v0, v1, v2, diag, chosen_b)
    one_a, one_b = swapped(chosen_a, 1), swapped(chosen_b, 1)
    moments = last(odd, low_one, low_two, one_a, one_b, two, v2, up, pair, moments)
    pieces = lax.all_to_all(moments, AXES, 0, 0, tiled=True)

    send, keep, effects = partial_scores(row.astype(jnp.int32)[None], rows, pieces, penalty[None], v0, v1, v2, genotypes)
    received = swapped(send, cols)
    bit = rows // 4
    while bit:
        mine = (row // (2 * bit)) % 2
        keep = keep.reshape((2, -1) + keep.shape[1:])
        received = received.reshape((2, -1) + received.shape[1:])

        keep, send = pick(mine.astype(jnp.int32)[None], keep, received)
        received = swapped(send, 2 * bit * cols)
        bit //= 2
    return effects, scattered_over((keep + received)[0], "col")


def solution(mesh):
    placed = (
        P(AXES, None),
        P(),
        P(AXES, None, None),
        P(AXES, None, None, None),
        P(AXES),
        P(None, AXES),
    )
    return jax.shard_map(
        body,
        mesh=mesh,
        in_specs=placed,
        out_specs=(P(AXES, None), P(AXES, None)),
        check_vma=False,
    )
```

```python
import functools

import jax
import jax.numpy as jnp
from jax import lax
from jax.experimental import pallas as pl
from jax.experimental.pallas import tpu as pltpu
from jax.sharding import PartitionSpec as P

AXES = ("row", "col")
F32 = jnp.float32
BF16 = jnp.bfloat16
MIB = 1024 * 1024
VMEM = pl.BlockSpec(memory_space=pltpu.VMEM)
SMEM = pl.BlockSpec(memory_space=pltpu.SMEM)
ANY = pl.BlockSpec(memory_space=pl.ANY)


def params(mib=20):
    return pltpu.CompilerParams(vmem_limit_bytes=mib * MIB)


def cost(flops, num_bytes):
    return pl.CostEstimate(flops=int(flops), bytes_accessed=int(num_bytes), transcendentals=0)


def shifted(block, distance):
    n = lax.axis_size(AXES)
    route = [(i - distance, i) for i in range(n) if 0 <= i - distance < n]
    return lax.ppermute(block, AXES, route)


def active(d, band, position):
    return jnp.logical_and(band[0] >= d + 1, position[0] >= d + 1)


def split_store(value, first, second):
    half = first.shape[0]
    first[...] = value[:half]
    second[...] = value[half:]


GROUP = 4


def fetched(low, tiles, arrived, order):
    count, rows = tiles.shape[0] // len(order), tiles.shape[1]
    copies = []
    for place in range(tiles.shape[0]):
        source = low.at[order[place // count], pl.ds(place % count * rows, rows)]
        copies.append(pltpu.make_async_copy(source, tiles.at[place], arrived.at[place]))
        copies[-1].start()
    return copies


def rounded_rows(copies, tiles, place, alive):
    for copy in copies[place : place + GROUP]:
        copy.wait()
    tile = tiles[place : place + GROUP].reshape(GROUP * tiles.shape[1], tiles.shape[2])
    return jnp.where(alive, tile, 0.0).astype(BF16)


def first_kernel(band, position, vec, low, one_a, one_b, own, tiles, arrived):
    fetch = pltpu.make_async_copy(vec, own, arrived.at[tiles.shape[0]])
    fetch.start()
    copies = fetched(low, tiles, arrived, (0,))
    fetch.wait()
    across = own[...].T.astype(BF16)
    rows = GROUP * tiles.shape[1]
    acc = None
    for place in range(0, tiles.shape[0], GROUP):
        tile = rounded_rows(copies, tiles, place, active(0, band, position))
        start = place * tiles.shape[1]
        term = jnp.dot(across[:, start : start + rows], tile, preferred_element_type=F32)
        acc = term if acc is None else acc + term
    split_store(acc.T, one_a, one_b)


def second_kernel(band, position, vec, low, far_a, far_b, low_one, low_two, own, tiles, arrived):
    fetch = pltpu.make_async_copy(vec, own, arrived.at[tiles.shape[0]])
    fetch.start()
    copies = fetched(low, tiles, arrived, (1, 0))
    fetch.wait()
    across = own[...].T.astype(BF16)
    rows = GROUP * tiles.shape[1]
    count = tiles.shape[0] // 2
    acc = None
    for place in range(0, count, GROUP):
        tile = rounded_rows(copies, tiles, place, active(1, band, position))
        start = place * tiles.shape[1]
        low_two[start : start + rows] = tile
        term = jnp.dot(across[:, start : start + rows], tile, preferred_element_type=F32)
        acc = term if acc is None else acc + term
    split_store(acc.T, far_a, far_b)
    for place in range(0, count, GROUP):
        start = place * tiles.shape[1]
        low_one[start : start + rows] = rounded_rows(copies, tiles, count + place, active(0, band, position))


def from_tiles(kernel, tiles, narrow, mib, band, position, vec, low):
    size, k = vec.shape
    count = 16
    return pl.pallas_call(
        kernel,
        in_specs=[SMEM] * 2 + [pl.BlockSpec(memory_space=pltpu.HBM)] * 2,
        out_specs=[VMEM] * (2 + narrow),
        out_shape=[jax.ShapeDtypeStruct((size // 2, k), F32)] * 2 + [jax.ShapeDtypeStruct((size, size), BF16)] * narrow,
        scratch_shapes=[
            pltpu.VMEM((size, k), F32),
            pltpu.VMEM((tiles * count, size // count, size), F32),
            pltpu.SemaphoreType.DMA((tiles * count + 1,)),
        ],
        compiler_params=params(mib),
        cost_estimate=cost(2 * size * size * k, 4 * tiles * size * size),
    )(band, position, vec, low)


def coupling_kernel(vec, low_one, low_two, one_a, one_b, far_a, far_b):
    across = vec[...].T.astype(BF16)
    split_store(jnp.dot(across, low_one[...], preferred_element_type=F32).T, one_a, one_b)
    split_store(jnp.dot(across, low_two[...], preferred_element_type=F32).T, far_a, far_b)


def coupling(vec, low_one, low_two):
    size, k = vec.shape
    return pl.pallas_call(
        coupling_kernel,
        in_specs=[VMEM] * 3,
        out_specs=[VMEM] * 4,
        out_shape=[jax.ShapeDtypeStruct((size // 2, k), F32)] * 4,
        compiler_params=params(),
        cost_estimate=cost(4 * size * size * k, 4 * size * size),
    )(vec, low_one, low_two)


def relay_kernel(odd, far, pair, after, out):
    out[...] = far[...] + jnp.where(odd[0] > 0, pair[...], 0.0)


def choose_kernel(odd, vec, two, after, *parts):
    rows = parts[0].shape[0]
    for place, part in enumerate(parts):
        here = slice(place * rows, (place + 1) * rows)
        part[...] = jnp.where(odd[0] > 0, two[here], vec[here])


def choose(odd, vec, two, after, parts):
    rows, k = vec.shape
    return pl.pallas_call(
        choose_kernel,
        in_specs=[SMEM, VMEM, VMEM, ANY],
        out_specs=[VMEM] * parts,
        out_shape=[jax.ShapeDtypeStruct((rows // parts, k), F32)] * parts,
        compiler_params=params(),
        cost_estimate=cost(vec.size, 12 * vec.size),
    )(odd, vec, two, after)


def relay(odd, far, pair, after):
    return pl.pallas_call(
        relay_kernel,
        in_specs=[SMEM, VMEM, VMEM, ANY],
        out_specs=VMEM,
        out_shape=jax.ShapeDtypeStruct(far.shape, F32),
        compiler_params=params(),
        cost_estimate=cost(far.size, 12 * far.size),
    )(odd, far, pair, after)


def first_diag_kernel(vec, diag, after, narrow, product):
    tile = diag[...].astype(BF16)
    rest = (diag[...] - tile.astype(F32)).astype(BF16)
    narrow[...] = tile
    value = vec[...]
    high = value.astype(BF16)
    low = (value - high.astype(F32)).astype(BF16)
    both = jnp.dot(tile, jnp.concatenate([high, low], axis=1), preferred_element_type=F32)
    k = value.shape[1]
    product[...] = both[:, :k] + both[:, k:] + jnp.dot(rest, high, preferred_element_type=F32)


def first_diag(vec, diag, after):
    size, k = vec.shape
    rows = size // 4
    return pl.pallas_call(
        first_diag_kernel,
        grid=(4,),
        in_specs=[pl.BlockSpec((size, k), lambda r: (0, 0)), pl.BlockSpec((rows, size), lambda r: (r, 0)), ANY],
        out_specs=[pl.BlockSpec((rows, size), lambda r: (r, 0)), pl.BlockSpec((rows, k), lambda r: (r, 0))],
        out_shape=[jax.ShapeDtypeStruct(diag.shape, BF16), jax.ShapeDtypeStruct(vec.shape, F32)],
        compiler_params=params(),
        cost_estimate=cost(2 * size * size * k, 6 * size * size),
    )(vec, diag, after)


def diag_kernel(vec, diag, after, product):
    product[...] = jnp.dot(diag[...], vec[...].astype(BF16), preferred_element_type=F32)


def diag_times(vec, diag, after):
    size, k = vec.shape
    return pl.pallas_call(
        diag_kernel,
        in_specs=[VMEM, VMEM, ANY],
        out_specs=VMEM,
        out_shape=jax.ShapeDtypeStruct(vec.shape, F32),
        compiler_params=params(),
        cost_estimate=cost(2 * size * size * k, 6 * size * size),
    )(vec, diag, after)


def finish_kernel(odd, part, low, one, ahead_a, ahead_b, pair_a, pair_b, out, *upper):
    acc = jnp.dot(low[...], one[...].astype(BF16), preferred_element_type=F32) + part[...]
    half = ahead_a.shape[0]
    for place, (straight, pair) in enumerate(((ahead_a, pair_a), (ahead_b, pair_b))):
        rows = slice(place * half, (place + 1) * half)
        out[rows] = acc[rows] + straight[...] + jnp.where(odd[0] > 0, 0.0, pair[...])
    for copy in upper:
        copy[...] = out[:half]


def finish(odd, uppers, part, low, *arrived):
    size, k = part.shape
    return pl.pallas_call(
        finish_kernel,
        in_specs=[SMEM] + [VMEM] * 7,
        out_specs=[VMEM] * (1 + uppers),
        out_shape=[jax.ShapeDtypeStruct(part.shape, F32)] + [jax.ShapeDtypeStruct((size // 2, k), F32)] * uppers,
        compiler_params=params(),
        cost_estimate=cost(2 * size * size * k, 2 * size * size),
    )(odd, part, low, *arrived)


def two_kernel(own, low, two, product):
    product[...] = own[...] + jnp.dot(low[...], two[...].astype(BF16), preferred_element_type=F32)


def add_two(own, low, two):
    size, k = two.shape
    return pl.pallas_call(
        two_kernel,
        in_specs=[VMEM] * 3,
        out_specs=VMEM,
        out_shape=jax.ShapeDtypeStruct(two.shape, F32),
        compiler_params=params(),
        cost_estimate=cost(2 * size * size * k, 2 * size * size),
    )(own, low, two)


def lower_kernel(vec, low_one, low_two, one, far):
    across = vec[...].T.astype(BF16)
    half = one.shape[0]
    one[...] = jnp.dot(across, low_one[:, half:], preferred_element_type=F32).T
    far[...] = jnp.dot(across, low_two[:, half:], preferred_element_type=F32).T


def lower_coupling(vec, low_one, low_two):
    size, k = vec.shape
    return pl.pallas_call(
        lower_kernel,
        in_specs=[VMEM] * 3,
        out_specs=[VMEM] * 2,
        out_shape=[jax.ShapeDtypeStruct((size // 2, k), F32)] * 2,
        compiler_params=params(),
        cost_estimate=cost(2 * size * size * k, 2 * size * size),
    )(vec, low_one, low_two)


def own_kernel(v0, v1, v2, diag, after, moments):
    image = jnp.dot(diag[...], v2[...].astype(BF16), preferred_element_type=F32)
    pairs = [(v0, v0), (v0, v1), (v1, v1), (v1, v2), (v2, v2)]
    for row, (a, b) in enumerate(pairs):
        moments[row : row + 1] = jnp.sum(a[...] * b[...], axis=0, keepdims=True)
    moments[5:6] = jnp.sum(v2[...] * image, axis=0, keepdims=True)
    moments[6:8] = jnp.zeros_like(moments[6:8])


def own_moments(v0, v1, v2, diag, after):
    size, k = v0.shape
    return pl.pallas_call(
        own_kernel,
        in_specs=[VMEM] * 4 + [ANY],
        out_specs=VMEM,
        out_shape=jax.ShapeDtypeStruct((8, k), F32),
        compiler_params=params(),
        cost_estimate=cost(2 * size * size * k, 6 * size * size),
    )(v0, v1, v2, diag, after)


def last_kernel(odd, low_one, low_two, one_a, one_b, two, v2, up, pair, moments, out):
    quarter, half = one_a.shape[0], two.shape[0]
    below = jnp.dot(low_two[:, :half], two[...].astype(BF16), preferred_element_type=F32)
    below = below + jnp.dot(low_one[:, :quarter], one_a[...].astype(BF16), preferred_element_type=F32)
    below = below + jnp.dot(low_one[:, quarter:half], one_b[...].astype(BF16), preferred_element_type=F32)
    above = up[...] + jnp.where(odd[0] > 0, 0.0, pair[...])
    coupled = jnp.sum(v2[...] * below, axis=0, keepdims=True) + jnp.sum(v2[half:] * above, axis=0, keepdims=True)
    whole = moments[...]
    row = lax.broadcasted_iota(jnp.int32, whole.shape, 0)
    whole = jnp.where(row == 5, whole + 2.0 * coupled, whole)
    for place in range(out.shape[0]):
        out[place] = whole


def last(odd, low_one, low_two, one_a, one_b, two, v2, up, pair, moments):
    size, k = v2.shape
    return pl.pallas_call(
        last_kernel,
        in_specs=[SMEM] + [VMEM] * 9,
        out_specs=VMEM,
        out_shape=jax.ShapeDtypeStruct((lax.axis_size(AXES), 8, k), F32),
        compiler_params=params(),
        cost_estimate=cost(2 * size * size * k, 2 * size * size),
    )(odd, low_one, low_two, one_a, one_b, two, v2, up, pair, moments)


def group_rows(genotypes, groups, group):
    rows = genotypes.shape[0] // groups
    return genotypes[pl.ds(pl.multiple_of(group * rows, rows), rows)]


def send_kernel(groups, row, pieces, penalty, v0, v1, v2, genotypes, factors, rounded, send):
    sums = pieces[0]
    for piece in range(1, pieces.shape[0]):
        sums = sums + pieces[piece]
    moments = [sums[m : m + 1] for m in range(6)]
    c0, c1, c2 = coefficients(moments, penalty[...])
    value = c0 * v0[...] + c1 * v1[...] + c2 * v2[...]
    for place, factor in enumerate((c0, c1, c2)):
        factors[place : place + 1] = factor
    factors[3:8] = jnp.zeros_like(factors[3:8])
    narrow = value.astype(BF16)
    rounded[...] = narrow
    other = 1 - row[0] % 2
    for g in range(groups // 2):
        send[g] = jnp.dot(group_rows(genotypes, groups, 2 * g + other), narrow, preferred_element_type=F32)


def keep_kernel(groups, row, rounded, genotypes, keep):
    mine = row[0] % 2
    for g in range(groups // 2):
        keep[g] = jnp.dot(group_rows(genotypes, groups, 2 * g + mine), rounded[...], preferred_element_type=F32)


def partial_scores(row, groups, pieces, penalty, v0, v1, v2, genotypes):
    people, size = genotypes.shape
    k = v0.shape[1]
    half = jax.ShapeDtypeStruct((groups // 2, people // groups, k), F32)
    factors, rounded, send = pl.pallas_call(
        functools.partial(send_kernel, groups),
        in_specs=[SMEM] + [VMEM] * 6,
        out_specs=[VMEM] * 3,
        out_shape=[jax.ShapeDtypeStruct((8, k), F32), jax.ShapeDtypeStruct(v0.shape, BF16), half],
        compiler_params=params(),
        cost_estimate=cost(people * size * k, 2 * people * size),
    )(row, pieces, penalty, v0, v1, v2, genotypes)
    keep = pl.pallas_call(
        functools.partial(keep_kernel, groups),
        in_specs=[SMEM, VMEM, VMEM],
        out_specs=VMEM,
        out_shape=half,
        compiler_params=params(),
        cost_estimate=cost(people * size * k, 2 * people * size),
    )(row, rounded, genotypes)
    return factors, send, keep


def effects_kernel(factors, v0, v1, v2, after, effects):
    effects[...] = factors[0:1] * v0[...] + factors[1:2] * v1[...] + factors[2:3] * v2[...]


def combined(factors, v0, v1, v2, after):
    return pl.pallas_call(
        effects_kernel,
        in_specs=[VMEM] * 4 + [ANY],
        out_specs=VMEM,
        out_shape=jax.ShapeDtypeStruct(v0.shape, F32),
        compiler_params=params(),
        cost_estimate=cost(5 * v0.size, 16 * v0.size),
    )(factors, v0, v1, v2, after)


def pick_kernel(index, keep, received, mine, other):
    mine[...] = keep[index[0]] + received[index[0]]
    other[...] = keep[1 - index[0]] + received[1 - index[0]]


def pick(index, keep, received):
    half = jax.ShapeDtypeStruct(keep.shape[1:], F32)
    return pl.pallas_call(
        pick_kernel,
        in_specs=[SMEM, VMEM, VMEM],
        out_specs=[VMEM] * 2,
        out_shape=[half] * 2,
        compiler_params=params(),
        cost_estimate=cost(keep.size, 12 * keep.size),
    )(index, keep, received)


def scattered_over(values, axis):
    n = lax.axis_size(axis)
    pieces = values.reshape((n, values.shape[0] // n) + values.shape[1:])
    return jnp.sum(lax.all_to_all(pieces, axis, 0, 0, tiled=True), axis=0)


def routed(block, pairs):
    return lax.ppermute(block, AXES, pairs)


def coefficients(moments, penalty):
    def inner(u, v):
        return sum(a * b * moments[i + j] for i, a in enumerate(u) for j, b in enumerate(v))

    n0 = moments[0]
    a0 = n0 / (moments[1] + penalty * n0)
    r1 = [1.0 - a0 * penalty, -a0]
    n1 = inner(r1, r1)
    b0 = n1 / n0
    d1 = [r1[0] + b0, r1[1]]
    ad1 = [penalty * d1[0], d1[0] + penalty * d1[1], d1[1]]
    a1 = n1 / inner(d1, ad1)
    e1 = [a0 + a1 * d1[0], a1 * d1[1]]
    r2 = [r1[0] - a1 * ad1[0], r1[1] - a1 * ad1[1], -a1 * ad1[2]]
    n2 = inner(r2, r2)
    b1 = n2 / n1
    d2 = [r2[0] + b1 * d1[0], r2[1] + b1 * d1[1], r2[2]]
    ad2 = [penalty * d2[0], d2[0] + penalty * d2[1], d2[1] + penalty * d2[2], d2[2]]
    a2 = n2 / inner(d2, ad2)
    return e1[0] + a2 * d2[0], e1[1] + a2 * d2[1], a2 * d2[2]


def swapped(block, bit):
    return routed(block, [(i, i ^ bit) for i in range(lax.axis_size(AXES))])


def body(marginal, penalty, ld_diag, ld_low, band, genotypes):
    n = lax.axis_size(AXES)
    rows, cols = lax.axis_size("row"), lax.axis_size("col")
    position = lax.axis_index(AXES)
    row = lax.axis_index("row")
    site = position.astype(jnp.int32)[None]
    odd = (position % 2).astype(jnp.int32)[None]
    half = marginal.shape[0] // 2

    def halos(vec, two, first, second):
        one_a, one_b = first()
        pair_a, pair_b = swapped(one_a, 1), swapped(one_b, 1)
        far_a, far_b = second(one_b)
        sum_a = relay(odd, far_a, pair_a, far_b)
        up_a = shifted(sum_a, -2)
        [chosen] = choose(odd, vec, two, sum_a, 1)
        one = swapped(chosen, 1)
        sum_b = relay(odd, far_b, pair_b, chosen)
        return sum_b, (one, up_a, shifted(sum_b, -2), pair_a, pair_b)

    v0 = marginal
    two = shifted(v0, 2)

    lows = []

    def second_tile(after):
        vec, _ = lax.optimization_barrier((v0, after))
        *products, low_one, low_two = from_tiles(second_kernel, 2, 2, 46, band, site, vec, ld_low[0])
        lows.extend((low_one, low_two))
        return products

    last_sum, arrived = halos(
        v0, two, lambda: from_tiles(first_kernel, 1, 0, 58, band, site, v0, ld_low[0]), second_tile
    )
    low_one, low_two = lows
    diag, own = first_diag(v0, ld_diag[0], last_sum)
    [v1] = finish(odd, 0, add_two(own, low_two, two), low_one, *arrived)

    two = shifted(v1, 2)
    products = coupling(v1, low_one, low_two)
    last_sum, arrived = halos(v1, two, lambda: products[:2], lambda after: products[2:])
    own = diag_times(v1, diag, last_sum)
    v2, upper = finish(odd, 1, add_two(own, low_two, two), low_one, *arrived)

    two = shifted(upper, 2)
    one, far = lower_coupling(v2, low_one, low_two)
    pair = swapped(one, 1)
    above = relay(odd, far, pair, far)
    up = shifted(above, -2)
    chosen_a, chosen_b = choose(odd, upper, two, above, 2)
    moments = own_moments(v0, v1, v2, diag, chosen_b)
    one_a, one_b = swapped(chosen_a, 1), swapped(chosen_b, 1)
    moments = last(odd, low_one, low_two, one_a, one_b, two, v2, up, pair, moments)
    pieces = lax.all_to_all(moments, AXES, 0, 0, tiled=True)

    factors, send, keep = partial_scores(row.astype(jnp.int32)[None], rows, pieces, penalty[None], v0, v1, v2, genotypes)
    received = swapped(send, cols)
    bit = rows // 4
    while bit:
        mine = (row // (2 * bit)) % 2
        keep = keep.reshape((2, -1) + keep.shape[1:])
        received = received.reshape((2, -1) + received.shape[1:])

        keep, send = pick(mine.astype(jnp.int32)[None], keep, received)
        received = swapped(send, 2 * bit * cols)
        bit //= 2
    effects = combined(factors, v0, v1, v2, send)
    return effects, scattered_over((keep + received)[0], "col")


def solution(mesh):
    placed = (
        P(AXES, None),
        P(),
        P(AXES, None, None),
        P(AXES, None, None, None),
        P(AXES),
        P(None, AXES),
    )
    return jax.shard_map(
        body,
        mesh=mesh,
        in_specs=placed,
        out_specs=(P(AXES, None), P(AXES, None)),
        check_vma=False,
    )
```

```python
import functools

import jax
import jax.numpy as jnp
from jax import lax
from jax.experimental import pallas as pl
from jax.experimental.pallas import tpu as pltpu
from jax.sharding import PartitionSpec as P

AXES = ("row", "col")
F32 = jnp.float32
BF16 = jnp.bfloat16
MIB = 1024 * 1024
VMEM = pl.BlockSpec(memory_space=pltpu.VMEM)
SMEM = pl.BlockSpec(memory_space=pltpu.SMEM)
ANY = pl.BlockSpec(memory_space=pl.ANY)


def params(mib=20):
    return pltpu.CompilerParams(vmem_limit_bytes=mib * MIB)


def cost(flops, num_bytes):
    return pl.CostEstimate(flops=int(flops), bytes_accessed=int(num_bytes), transcendentals=0)


def shifted(block, distance):
    n = lax.axis_size(AXES)
    route = [(i - distance, i) for i in range(n) if 0 <= i - distance < n]
    return lax.ppermute(block, AXES, route)


def active(d, band, position):
    return jnp.logical_and(band[0] >= d + 1, position[0] >= d + 1)


def split_store(value, first, second):
    half = first.shape[0]
    first[...] = value[:half]
    second[...] = value[half:]


GROUP = 4


def fetched(low, tiles, arrived, order):
    count, rows = tiles.shape[0] // len(order), tiles.shape[1]
    copies = []
    for place in range(tiles.shape[0]):
        source = low.at[order[place // count], pl.ds(place % count * rows, rows)]
        copies.append(pltpu.make_async_copy(source, tiles.at[place], arrived.at[place]))
        copies[-1].start()
    return copies


def rounded_rows(copies, tiles, place, alive):
    for copy in copies[place : place + GROUP]:
        copy.wait()
    tile = tiles[place : place + GROUP].reshape(GROUP * tiles.shape[1], tiles.shape[2])
    return jnp.where(alive, tile, 0.0).astype(BF16)


def first_kernel(band, position, vec, low, one_a, one_b, own, tiles, arrived):
    fetch = pltpu.make_async_copy(vec, own, arrived.at[tiles.shape[0]])
    fetch.start()
    copies = fetched(low, tiles, arrived, (0,))
    fetch.wait()
    across = own[...].T.astype(BF16)
    rows = GROUP * tiles.shape[1]
    acc = None
    for place in range(0, tiles.shape[0], GROUP):
        tile = rounded_rows(copies, tiles, place, active(0, band, position))
        start = place * tiles.shape[1]
        term = jnp.dot(across[:, start : start + rows], tile, preferred_element_type=F32)
        acc = term if acc is None else acc + term
    split_store(acc.T, one_a, one_b)


def second_kernel(band, position, vec, low, far_a, far_b, low_one, low_two, own, tiles, arrived):
    fetch = pltpu.make_async_copy(vec, own, arrived.at[tiles.shape[0]])
    fetch.start()
    copies = fetched(low, tiles, arrived, (1, 0))
    fetch.wait()
    across = own[...].T.astype(BF16)
    rows = GROUP * tiles.shape[1]
    count = tiles.shape[0] // 2
    acc = None
    for place in range(0, count, GROUP):
        tile = rounded_rows(copies, tiles, place, active(1, band, position))
        start = place * tiles.shape[1]
        low_two[start : start + rows] = tile
        term = jnp.dot(across[:, start : start + rows], tile, preferred_element_type=F32)
        acc = term if acc is None else acc + term
    split_store(acc.T, far_a, far_b)
    for place in range(0, count, GROUP):
        start = place * tiles.shape[1]
        low_one[start : start + rows] = rounded_rows(copies, tiles, count + place, active(0, band, position))


def from_tiles(kernel, tiles, narrow, mib, band, position, vec, low):
    size, k = vec.shape
    count = 16
    return pl.pallas_call(
        kernel,
        in_specs=[SMEM] * 2 + [pl.BlockSpec(memory_space=pltpu.HBM)] * 2,
        out_specs=[VMEM] * (2 + narrow),
        out_shape=[jax.ShapeDtypeStruct((size // 2, k), F32)] * 2 + [jax.ShapeDtypeStruct((size, size), BF16)] * narrow,
        scratch_shapes=[
            pltpu.VMEM((size, k), F32),
            pltpu.VMEM((tiles * count, size // count, size), F32),
            pltpu.SemaphoreType.DMA((tiles * count + 1,)),
        ],
        compiler_params=params(mib),
        cost_estimate=cost(2 * size * size * k, 4 * tiles * size * size),
    )(band, position, vec, low)


def coupling_kernel(vec, low_one, low_two, one_a, one_b, far_a, far_b):
    across = vec[...].T.astype(BF16)
    split_store(jnp.dot(across, low_one[...], preferred_element_type=F32).T, one_a, one_b)
    split_store(jnp.dot(across, low_two[...], preferred_element_type=F32).T, far_a, far_b)


def coupling(vec, low_one, low_two):
    size, k = vec.shape
    return pl.pallas_call(
        coupling_kernel,
        in_specs=[VMEM] * 3,
        out_specs=[VMEM] * 4,
        out_shape=[jax.ShapeDtypeStruct((size // 2, k), F32)] * 4,
        compiler_params=params(),
        cost_estimate=cost(4 * size * size * k, 4 * size * size),
    )(vec, low_one, low_two)


def relay_kernel(odd, far, pair, after, out):
    out[...] = far[...] + jnp.where(odd[0] > 0, pair[...], 0.0)


def choose_kernel(odd, vec, two, after, *parts):
    rows = parts[0].shape[0]
    for place, part in enumerate(parts):
        here = slice(place * rows, (place + 1) * rows)
        part[...] = jnp.where(odd[0] > 0, two[here], vec[here])


def choose(odd, vec, two, after, parts):
    rows, k = vec.shape
    return pl.pallas_call(
        choose_kernel,
        in_specs=[SMEM, VMEM, VMEM, ANY],
        out_specs=[VMEM] * parts,
        out_shape=[jax.ShapeDtypeStruct((rows // parts, k), F32)] * parts,
        compiler_params=params(),
        cost_estimate=cost(vec.size, 12 * vec.size),
    )(odd, vec, two, after)


def relay(odd, far, pair, after):
    return pl.pallas_call(
        relay_kernel,
        in_specs=[SMEM, VMEM, VMEM, ANY],
        out_specs=VMEM,
        out_shape=jax.ShapeDtypeStruct(far.shape, F32),
        compiler_params=params(),
        cost_estimate=cost(far.size, 12 * far.size),
    )(odd, far, pair, after)


def first_diag_kernel(vec, diag, after, narrow, product):
    tile = diag[...].astype(BF16)
    rest = (diag[...] - tile.astype(F32)).astype(BF16)
    narrow[...] = tile
    value = vec[...]
    high = value.astype(BF16)
    low = (value - high.astype(F32)).astype(BF16)
    both = jnp.dot(tile, jnp.concatenate([high, low], axis=1), preferred_element_type=F32)
    k = value.shape[1]
    product[...] = both[:, :k] + both[:, k:] + jnp.dot(rest, high, preferred_element_type=F32)


def first_diag(vec, diag, after):
    size, k = vec.shape
    rows = size // 4
    return pl.pallas_call(
        first_diag_kernel,
        grid=(4,),
        in_specs=[pl.BlockSpec((size, k), lambda r: (0, 0)), pl.BlockSpec((rows, size), lambda r: (r, 0)), ANY],
        out_specs=[pl.BlockSpec((rows, size), lambda r: (r, 0)), pl.BlockSpec((rows, k), lambda r: (r, 0))],
        out_shape=[jax.ShapeDtypeStruct(diag.shape, BF16), jax.ShapeDtypeStruct(vec.shape, F32)],
        compiler_params=params(),
        cost_estimate=cost(2 * size * size * k, 6 * size * size),
    )(vec, diag, after)


def diag_kernel(vec, diag, after, product):
    product[...] = jnp.dot(diag[...], vec[...].astype(BF16), preferred_element_type=F32)


def diag_times(vec, diag, after):
    size, k = vec.shape
    return pl.pallas_call(
        diag_kernel,
        in_specs=[VMEM, VMEM, ANY],
        out_specs=VMEM,
        out_shape=jax.ShapeDtypeStruct(vec.shape, F32),
        compiler_params=params(),
        cost_estimate=cost(2 * size * size * k, 6 * size * size),
    )(vec, diag, after)


def finish_kernel(odd, part, low, one, ahead_a, ahead_b, pair_a, pair_b, out, *upper):
    acc = jnp.dot(low[...], one[...].astype(BF16), preferred_element_type=F32) + part[...]
    half = ahead_a.shape[0]
    for place, (straight, pair) in enumerate(((ahead_a, pair_a), (ahead_b, pair_b))):
        rows = slice(place * half, (place + 1) * half)
        out[rows] = acc[rows] + straight[...] + jnp.where(odd[0] > 0, 0.0, pair[...])
    for copy in upper:
        copy[...] = out[:half]


def finish(odd, uppers, part, low, *arrived):
    size, k = part.shape
    return pl.pallas_call(
        finish_kernel,
        in_specs=[SMEM] + [VMEM] * 7,
        out_specs=[VMEM] * (1 + uppers),
        out_shape=[jax.ShapeDtypeStruct(part.shape, F32)] + [jax.ShapeDtypeStruct((size // 2, k), F32)] * uppers,
        compiler_params=params(),
        cost_estimate=cost(2 * size * size * k, 2 * size * size),
    )(odd, part, low, *arrived)


def two_kernel(own, low, two, product):
    product[...] = own[...] + jnp.dot(low[...], two[...].astype(BF16), preferred_element_type=F32)


def add_two(own, low, two):
    size, k = two.shape
    return pl.pallas_call(
        two_kernel,
        in_specs=[VMEM] * 3,
        out_specs=VMEM,
        out_shape=jax.ShapeDtypeStruct(two.shape, F32),
        compiler_params=params(),
        cost_estimate=cost(2 * size * size * k, 2 * size * size),
    )(own, low, two)


def lower_kernel(vec, low_one, low_two, one, far):
    across = vec[...].T.astype(BF16)
    half = one.shape[0]
    one[...] = jnp.dot(across, low_one[:, half:], preferred_element_type=F32).T
    far[...] = jnp.dot(across, low_two[:, half:], preferred_element_type=F32).T


def lower_coupling(vec, low_one, low_two):
    size, k = vec.shape
    return pl.pallas_call(
        lower_kernel,
        in_specs=[VMEM] * 3,
        out_specs=[VMEM] * 2,
        out_shape=[jax.ShapeDtypeStruct((size // 2, k), F32)] * 2,
        compiler_params=params(),
        cost_estimate=cost(2 * size * size * k, 2 * size * size),
    )(vec, low_one, low_two)


def own_kernel(v0, v1, v2, diag, after, moments):
    image = jnp.dot(diag[...], v2[...].astype(BF16), preferred_element_type=F32)
    pairs = [(v0, v0), (v0, v1), (v1, v1), (v1, v2), (v2, v2)]
    for row, (a, b) in enumerate(pairs):
        moments[row : row + 1] = jnp.sum(a[...] * b[...], axis=0, keepdims=True)
    moments[5:6] = jnp.sum(v2[...] * image, axis=0, keepdims=True)
    moments[6:8] = jnp.zeros_like(moments[6:8])


def own_moments(v0, v1, v2, diag, after):
    size, k = v0.shape
    return pl.pallas_call(
        own_kernel,
        in_specs=[VMEM] * 4 + [ANY],
        out_specs=VMEM,
        out_shape=jax.ShapeDtypeStruct((8, k), F32),
        compiler_params=params(),
        cost_estimate=cost(2 * size * size * k, 6 * size * size),
    )(v0, v1, v2, diag, after)


def last_kernel(odd, low_one, low_two, one_a, one_b, two, v2, up, pair, moments, out):
    quarter, half = one_a.shape[0], two.shape[0]
    below = jnp.dot(low_two[:, :half], two[...].astype(BF16), preferred_element_type=F32)
    below = below + jnp.dot(low_one[:, :quarter], one_a[...].astype(BF16), preferred_element_type=F32)
    below = below + jnp.dot(low_one[:, quarter:half], one_b[...].astype(BF16), preferred_element_type=F32)
    above = up[...] + jnp.where(odd[0] > 0, 0.0, pair[...])
    coupled = jnp.sum(v2[...] * below, axis=0, keepdims=True) + jnp.sum(v2[half:] * above, axis=0, keepdims=True)
    whole = moments[...]
    row = lax.broadcasted_iota(jnp.int32, whole.shape, 0)
    whole = jnp.where(row == 5, whole + 2.0 * coupled, whole)
    for place in range(out.shape[0]):
        out[place] = whole


def last(odd, low_one, low_two, one_a, one_b, two, v2, up, pair, moments):
    size, k = v2.shape
    return pl.pallas_call(
        last_kernel,
        in_specs=[SMEM] + [VMEM] * 9,
        out_specs=VMEM,
        out_shape=jax.ShapeDtypeStruct((lax.axis_size(AXES), 8, k), F32),
        compiler_params=params(),
        cost_estimate=cost(2 * size * size * k, 2 * size * size),
    )(odd, low_one, low_two, one_a, one_b, two, v2, up, pair, moments)


def group_rows(genotypes, groups, group):
    rows = genotypes.shape[0] // groups
    return genotypes[pl.ds(pl.multiple_of(group * rows, rows), rows)]


def send_kernel(groups, row, pieces, penalty, v0, v1, v2, genotypes, factors, send, keep):
    sums = pieces[0]
    for piece in range(1, pieces.shape[0]):
        sums = sums + pieces[piece]
    moments = [sums[m : m + 1] for m in range(6)]
    c0, c1, c2 = coefficients(moments, penalty[...])
    value = c0 * v0[...] + c1 * v1[...] + c2 * v2[...]
    for place, factor in enumerate((c0, c1, c2)):
        factors[place : place + 1] = factor
    factors[3:8] = jnp.zeros_like(factors[3:8])
    narrow = value.astype(BF16)
    mine = row[0] % 2
    for g in range(groups // 2):
        send[g] = jnp.dot(group_rows(genotypes, groups, 2 * g + 1 - mine), narrow, preferred_element_type=F32)
        keep[g] = jnp.dot(group_rows(genotypes, groups, 2 * g + mine), narrow, preferred_element_type=F32)


def partial_scores(row, groups, pieces, penalty, v0, v1, v2, genotypes):
    people, size = genotypes.shape
    k = v0.shape[1]
    half = jax.ShapeDtypeStruct((groups // 2, people // groups, k), F32)
    return pl.pallas_call(
        functools.partial(send_kernel, groups),
        in_specs=[SMEM] + [VMEM] * 6,
        out_specs=[VMEM] * 3,
        out_shape=[jax.ShapeDtypeStruct((8, k), F32), half, half],
        compiler_params=params(),
        cost_estimate=cost(2 * people * size * k, 2 * people * size),
    )(row, pieces, penalty, v0, v1, v2, genotypes)


def effects_kernel(factors, v0, v1, v2, after, effects):
    effects[...] = factors[0:1] * v0[...] + factors[1:2] * v1[...] + factors[2:3] * v2[...]


def combined(factors, v0, v1, v2, after):
    return pl.pallas_call(
        effects_kernel,
        in_specs=[VMEM] * 4 + [ANY],
        out_specs=VMEM,
        out_shape=jax.ShapeDtypeStruct(v0.shape, F32),
        compiler_params=params(),
        cost_estimate=cost(5 * v0.size, 16 * v0.size),
    )(factors, v0, v1, v2, after)


def pick_kernel(index, keep, received, mine, other):
    mine[...] = keep[index[0]] + received[index[0]]
    other[...] = keep[1 - index[0]] + received[1 - index[0]]


def pick(index, keep, received):
    half = jax.ShapeDtypeStruct(keep.shape[1:], F32)
    return pl.pallas_call(
        pick_kernel,
        in_specs=[SMEM, VMEM, VMEM],
        out_specs=[VMEM] * 2,
        out_shape=[half] * 2,
        compiler_params=params(),
        cost_estimate=cost(keep.size, 12 * keep.size),
    )(index, keep, received)


def scattered_over(values, axis):
    n = lax.axis_size(axis)
    pieces = values.reshape((n, values.shape[0] // n) + values.shape[1:])
    return jnp.sum(lax.all_to_all(pieces, axis, 0, 0, tiled=True), axis=0)


def routed(block, pairs):
    return lax.ppermute(block, AXES, pairs)


def coefficients(moments, penalty):
    def inner(u, v):
        return sum(a * b * moments[i + j] for i, a in enumerate(u) for j, b in enumerate(v))

    n0 = moments[0]
    a0 = n0 / (moments[1] + penalty * n0)
    r1 = [1.0 - a0 * penalty, -a0]
    n1 = inner(r1, r1)
    b0 = n1 / n0
    d1 = [r1[0] + b0, r1[1]]
    ad1 = [penalty * d1[0], d1[0] + penalty * d1[1], d1[1]]
    a1 = n1 / inner(d1, ad1)
    e1 = [a0 + a1 * d1[0], a1 * d1[1]]
    r2 = [r1[0] - a1 * ad1[0], r1[1] - a1 * ad1[1], -a1 * ad1[2]]
    n2 = inner(r2, r2)
    b1 = n2 / n1
    d2 = [r2[0] + b1 * d1[0], r2[1] + b1 * d1[1], r2[2]]
    ad2 = [penalty * d2[0], d2[0] + penalty * d2[1], d2[1] + penalty * d2[2], d2[2]]
    a2 = n2 / inner(d2, ad2)
    return e1[0] + a2 * d2[0], e1[1] + a2 * d2[1], a2 * d2[2]


def swapped(block, bit):
    return routed(block, [(i, i ^ bit) for i in range(lax.axis_size(AXES))])


def body(marginal, penalty, ld_diag, ld_low, band, genotypes):
    n = lax.axis_size(AXES)
    rows, cols = lax.axis_size("row"), lax.axis_size("col")
    position = lax.axis_index(AXES)
    row = lax.axis_index("row")
    site = position.astype(jnp.int32)[None]
    odd = (position % 2).astype(jnp.int32)[None]
    half = marginal.shape[0] // 2

    def halos(vec, two, first, second):
        one_a, one_b = first()
        pair_a, pair_b = swapped(one_a, 1), swapped(one_b, 1)
        far_a, far_b = second(one_b)
        sum_a = relay(odd, far_a, pair_a, far_b)
        up_a = shifted(sum_a, -2)
        [chosen] = choose(odd, vec, two, sum_a, 1)
        one = swapped(chosen, 1)
        sum_b = relay(odd, far_b, pair_b, chosen)
        return sum_b, (one, up_a, shifted(sum_b, -2), pair_a, pair_b)

    v0 = marginal
    two = shifted(v0, 2)

    lows = []

    def second_tile(after):
        vec, _ = lax.optimization_barrier((v0, after))
        *products, low_one, low_two = from_tiles(second_kernel, 2, 2, 46, band, site, vec, ld_low[0])
        lows.extend((low_one, low_two))
        return products

    last_sum, arrived = halos(
        v0, two, lambda: from_tiles(first_kernel, 1, 0, 58, band, site, v0, ld_low[0]), second_tile
    )
    low_one, low_two = lows
    diag, own = first_diag(v0, ld_diag[0], last_sum)
    [v1] = finish(odd, 0, add_two(own, low_two, two), low_one, *arrived)

    two = shifted(v1, 2)
    products = coupling(v1, low_one, low_two)
    last_sum, arrived = halos(v1, two, lambda: products[:2], lambda after: products[2:])
    own = diag_times(v1, diag, last_sum)
    v2, upper = finish(odd, 1, add_two(own, low_two, two), low_one, *arrived)

    two = shifted(upper, 2)
    one, far = lower_coupling(v2, low_one, low_two)
    pair = swapped(one, 1)
    above = relay(odd, far, pair, far)
    up = shifted(above, -2)
    chosen_a, chosen_b = choose(odd, upper, two, above, 2)
    moments = own_moments(v0, v1, v2, diag, chosen_b)
    one_a, one_b = swapped(chosen_a, 1), swapped(chosen_b, 1)
    moments = last(odd, low_one, low_two, one_a, one_b, two, v2, up, pair, moments)
    pieces = lax.all_to_all(moments, AXES, 0, 0, tiled=True)

    factors, send, keep = partial_scores(row.astype(jnp.int32)[None], rows, pieces, penalty[None], v0, v1, v2, genotypes)
    received = swapped(send, cols)
    bit = rows // 4
    while bit:
        mine = (row // (2 * bit)) % 2
        keep = keep.reshape((2, -1) + keep.shape[1:])
        received = received.reshape((2, -1) + received.shape[1:])

        keep, send = pick(mine.astype(jnp.int32)[None], keep, received)
        received = swapped(send, 2 * bit * cols)
        bit //= 2
    effects = combined(factors, v0, v1, v2, send)
    keep, effects = lax.optimization_barrier((keep, effects))
    return effects, scattered_over((keep + received)[0], "col")


def solution(mesh):
    placed = (
        P(AXES, None),
        P(),
        P(AXES, None, None),
        P(AXES, None, None, None),
        P(AXES),
        P(None, AXES),
    )
    return jax.shard_map(
        body,
        mesh=mesh,
        in_specs=placed,
        out_specs=(P(AXES, None), P(AXES, None)),
        check_vma=False,
    )
```

```python
import functools

import jax
import jax.numpy as jnp
from jax import lax
from jax.experimental import pallas as pl
from jax.experimental.pallas import tpu as pltpu
from jax.sharding import PartitionSpec as P

AXES = ("row", "col")
F32 = jnp.float32
BF16 = jnp.bfloat16
MIB = 1024 * 1024
VMEM = pl.BlockSpec(memory_space=pltpu.VMEM)
SMEM = pl.BlockSpec(memory_space=pltpu.SMEM)
ANY = pl.BlockSpec(memory_space=pl.ANY)


def params(mib=20):
    return pltpu.CompilerParams(vmem_limit_bytes=mib * MIB)


def cost(flops, num_bytes):
    return pl.CostEstimate(flops=int(flops), bytes_accessed=int(num_bytes), transcendentals=0)


def shifted(block, distance):
    n = lax.axis_size(AXES)
    route = [(i - distance, i) for i in range(n) if 0 <= i - distance < n]
    return lax.ppermute(block, AXES, route)


def active(d, band, position):
    return jnp.logical_and(band[0] >= d + 1, position[0] >= d + 1)


def split_store(value, first, second):
    half = first.shape[0]
    first[...] = value[:half]
    second[...] = value[half:]


GROUP = 4


def fetched(low, tiles, arrived, order):
    count, rows = tiles.shape[0] // len(order), tiles.shape[1]
    copies = []
    for place in range(tiles.shape[0]):
        source = low.at[order[place // count], pl.ds(place % count * rows, rows)]
        copies.append(pltpu.make_async_copy(source, tiles.at[place], arrived.at[place]))
        copies[-1].start()
    return copies


def rounded_rows(copies, tiles, place, alive):
    for copy in copies[place : place + GROUP]:
        copy.wait()
    tile = tiles[place : place + GROUP].reshape(GROUP * tiles.shape[1], tiles.shape[2])
    return jnp.where(alive, tile, 0.0).astype(BF16)


def first_kernel(band, position, vec, low, one_a, one_b, own, tiles, arrived):
    fetch = pltpu.make_async_copy(vec, own, arrived.at[tiles.shape[0]])
    fetch.start()
    copies = fetched(low, tiles, arrived, (0,))
    fetch.wait()
    across = own[...].T.astype(BF16)
    rows = GROUP * tiles.shape[1]
    acc = None
    for place in range(0, tiles.shape[0], GROUP):
        tile = rounded_rows(copies, tiles, place, active(0, band, position))
        start = place * tiles.shape[1]
        term = jnp.dot(across[:, start : start + rows], tile, preferred_element_type=F32)
        acc = term if acc is None else acc + term
    split_store(acc.T, one_a, one_b)


def second_kernel(band, position, vec, low, far_a, far_b, low_one, low_two, own, tiles, arrived):
    fetch = pltpu.make_async_copy(vec, own, arrived.at[tiles.shape[0]])
    fetch.start()
    copies = fetched(low, tiles, arrived, (1, 0))
    fetch.wait()
    across = own[...].T.astype(BF16)
    rows = GROUP * tiles.shape[1]
    count = tiles.shape[0] // 2
    acc = None
    for place in range(0, count, GROUP):
        tile = rounded_rows(copies, tiles, place, active(1, band, position))
        start = place * tiles.shape[1]
        low_two[start : start + rows] = tile
        term = jnp.dot(across[:, start : start + rows], tile, preferred_element_type=F32)
        acc = term if acc is None else acc + term
    split_store(acc.T, far_a, far_b)
    for place in range(0, count, GROUP):
        start = place * tiles.shape[1]
        low_one[start : start + rows] = rounded_rows(copies, tiles, count + place, active(0, band, position))


def from_tiles(kernel, tiles, narrow, mib, band, position, vec, low):
    size, k = vec.shape
    count = 16
    return pl.pallas_call(
        kernel,
        in_specs=[SMEM] * 2 + [pl.BlockSpec(memory_space=pltpu.HBM)] * 2,
        out_specs=[VMEM] * (2 + narrow),
        out_shape=[jax.ShapeDtypeStruct((size // 2, k), F32)] * 2 + [jax.ShapeDtypeStruct((size, size), BF16)] * narrow,
        scratch_shapes=[
            pltpu.VMEM((size, k), F32),
            pltpu.VMEM((tiles * count, size // count, size), F32),
            pltpu.SemaphoreType.DMA((tiles * count + 1,)),
        ],
        compiler_params=params(mib),
        cost_estimate=cost(2 * size * size * k, 4 * tiles * size * size),
    )(band, position, vec, low)


def coupling_kernel(vec, low_one, low_two, one_a, one_b, far_a, far_b):
    across = vec[...].T.astype(BF16)
    split_store(jnp.dot(across, low_one[...], preferred_element_type=F32).T, one_a, one_b)
    split_store(jnp.dot(across, low_two[...], preferred_element_type=F32).T, far_a, far_b)


def coupling(vec, low_one, low_two):
    size, k = vec.shape
    return pl.pallas_call(
        coupling_kernel,
        in_specs=[VMEM] * 3,
        out_specs=[VMEM] * 4,
        out_shape=[jax.ShapeDtypeStruct((size // 2, k), F32)] * 4,
        compiler_params=params(),
        cost_estimate=cost(4 * size * size * k, 4 * size * size),
    )(vec, low_one, low_two)


def relay_kernel(odd, far, pair, after, out):
    out[...] = far[...] + jnp.where(odd[0] > 0, pair[...], 0.0)


def choose_kernel(odd, vec, two, after, *parts):
    rows = parts[0].shape[0]
    for place, part in enumerate(parts):
        here = slice(place * rows, (place + 1) * rows)
        part[...] = jnp.where(odd[0] > 0, two[here], vec[here])


def choose(odd, vec, two, after, parts):
    rows, k = vec.shape
    return pl.pallas_call(
        choose_kernel,
        in_specs=[SMEM, VMEM, VMEM, ANY],
        out_specs=[VMEM] * parts,
        out_shape=[jax.ShapeDtypeStruct((rows // parts, k), F32)] * parts,
        compiler_params=params(),
        cost_estimate=cost(vec.size, 12 * vec.size),
    )(odd, vec, two, after)


def relay(odd, far, pair, after):
    return pl.pallas_call(
        relay_kernel,
        in_specs=[SMEM, VMEM, VMEM, ANY],
        out_specs=VMEM,
        out_shape=jax.ShapeDtypeStruct(far.shape, F32),
        compiler_params=params(),
        cost_estimate=cost(far.size, 12 * far.size),
    )(odd, far, pair, after)


def first_diag_kernel(vec, diag, after, narrow, product):
    tile = diag[...].astype(BF16)
    rest = (diag[...] - tile.astype(F32)).astype(BF16)
    narrow[...] = tile
    value = vec[...]
    high = value.astype(BF16)
    low = (value - high.astype(F32)).astype(BF16)
    both = jnp.dot(tile, jnp.concatenate([high, low], axis=1), preferred_element_type=F32)
    k = value.shape[1]
    product[...] = both[:, :k] + both[:, k:] + jnp.dot(rest, high, preferred_element_type=F32)


def first_diag(vec, diag, after):
    size, k = vec.shape
    rows = size // 4
    return pl.pallas_call(
        first_diag_kernel,
        grid=(4,),
        in_specs=[pl.BlockSpec((size, k), lambda r: (0, 0)), pl.BlockSpec((rows, size), lambda r: (r, 0)), ANY],
        out_specs=[pl.BlockSpec((rows, size), lambda r: (r, 0)), pl.BlockSpec((rows, k), lambda r: (r, 0))],
        out_shape=[jax.ShapeDtypeStruct(diag.shape, BF16), jax.ShapeDtypeStruct(vec.shape, F32)],
        compiler_params=params(),
        cost_estimate=cost(2 * size * size * k, 6 * size * size),
    )(vec, diag, after)


def diag_kernel(vec, diag, after, product):
    product[...] = jnp.dot(diag[...], vec[...].astype(BF16), preferred_element_type=F32)


def diag_times(vec, diag, after):
    size, k = vec.shape
    return pl.pallas_call(
        diag_kernel,
        in_specs=[VMEM, VMEM, ANY],
        out_specs=VMEM,
        out_shape=jax.ShapeDtypeStruct(vec.shape, F32),
        compiler_params=params(),
        cost_estimate=cost(2 * size * size * k, 6 * size * size),
    )(vec, diag, after)


def finish_kernel(odd, part, low, one, ahead_a, ahead_b, pair_a, pair_b, out, *upper):
    acc = jnp.dot(low[...], one[...].astype(BF16), preferred_element_type=F32) + part[...]
    half = ahead_a.shape[0]
    for place, (straight, pair) in enumerate(((ahead_a, pair_a), (ahead_b, pair_b))):
        rows = slice(place * half, (place + 1) * half)
        out[rows] = acc[rows] + straight[...] + jnp.where(odd[0] > 0, 0.0, pair[...])
    for copy in upper:
        copy[...] = out[:half]


def finish(odd, uppers, part, low, *arrived):
    size, k = part.shape
    return pl.pallas_call(
        finish_kernel,
        in_specs=[SMEM] + [VMEM] * 7,
        out_specs=[VMEM] * (1 + uppers),
        out_shape=[jax.ShapeDtypeStruct(part.shape, F32)] + [jax.ShapeDtypeStruct((size // 2, k), F32)] * uppers,
        compiler_params=params(),
        cost_estimate=cost(2 * size * size * k, 2 * size * size),
    )(odd, part, low, *arrived)


def two_kernel(own, low, two, product):
    product[...] = own[...] + jnp.dot(low[...], two[...].astype(BF16), preferred_element_type=F32)


def add_two(own, low, two):
    size, k = two.shape
    return pl.pallas_call(
        two_kernel,
        in_specs=[VMEM] * 3,
        out_specs=VMEM,
        out_shape=jax.ShapeDtypeStruct(two.shape, F32),
        compiler_params=params(),
        cost_estimate=cost(2 * size * size * k, 2 * size * size),
    )(own, low, two)


def lower_kernel(vec, low_one, low_two, one, far):
    across = vec[...].T.astype(BF16)
    half = one.shape[0]
    one[...] = jnp.dot(across, low_one[:, half:], preferred_element_type=F32).T
    far[...] = jnp.dot(across, low_two[:, half:], preferred_element_type=F32).T


def lower_coupling(vec, low_one, low_two):
    size, k = vec.shape
    return pl.pallas_call(
        lower_kernel,
        in_specs=[VMEM] * 3,
        out_specs=[VMEM] * 2,
        out_shape=[jax.ShapeDtypeStruct((size // 2, k), F32)] * 2,
        compiler_params=params(),
        cost_estimate=cost(2 * size * size * k, 2 * size * size),
    )(vec, low_one, low_two)


def own_kernel(v0, v1, v2, diag, after, moments):
    image = jnp.dot(diag[...], v2[...].astype(BF16), preferred_element_type=F32)
    pairs = [(v0, v0), (v0, v1), (v1, v1), (v1, v2), (v2, v2)]
    for row, (a, b) in enumerate(pairs):
        moments[row : row + 1] = jnp.sum(a[...] * b[...], axis=0, keepdims=True)
    moments[5:6] = jnp.sum(v2[...] * image, axis=0, keepdims=True)
    moments[6:8] = jnp.zeros_like(moments[6:8])


def own_moments(v0, v1, v2, diag, after):
    size, k = v0.shape
    return pl.pallas_call(
        own_kernel,
        in_specs=[VMEM] * 4 + [ANY],
        out_specs=VMEM,
        out_shape=jax.ShapeDtypeStruct((8, k), F32),
        compiler_params=params(),
        cost_estimate=cost(2 * size * size * k, 6 * size * size),
    )(v0, v1, v2, diag, after)


def most_kernel(low_one, low_two, one_a, two, below):
    quarter, half = one_a.shape[0], two.shape[0]
    value = jnp.dot(low_two[:, :half], two[...].astype(BF16), preferred_element_type=F32)
    below[...] = value + jnp.dot(low_one[:, :quarter], one_a[...].astype(BF16), preferred_element_type=F32)


def most(low_one, low_two, one_a, two):
    size, k = low_one.shape[0], two.shape[1]
    return pl.pallas_call(
        most_kernel,
        in_specs=[VMEM] * 4,
        out_specs=VMEM,
        out_shape=jax.ShapeDtypeStruct((size, k), F32),
        compiler_params=params(),
        cost_estimate=cost(2 * size * size * k, 2 * size * size),
    )(low_one, low_two, one_a, two)


def last_kernel(odd, low_one, part, one_b, v2, up, pair, moments, out):
    quarter = one_b.shape[0]
    half = 2 * quarter
    below = part[...] + jnp.dot(low_one[:, quarter:half], one_b[...].astype(BF16), preferred_element_type=F32)
    above = up[...] + jnp.where(odd[0] > 0, 0.0, pair[...])
    coupled = jnp.sum(v2[...] * below, axis=0, keepdims=True) + jnp.sum(v2[half:] * above, axis=0, keepdims=True)
    whole = moments[...]
    row = lax.broadcasted_iota(jnp.int32, whole.shape, 0)
    whole = jnp.where(row == 5, whole + 2.0 * coupled, whole)
    for place in range(out.shape[0]):
        out[place] = whole


def last(odd, low_one, part, one_b, v2, up, pair, moments):
    size, k = v2.shape
    return pl.pallas_call(
        last_kernel,
        in_specs=[SMEM] + [VMEM] * 7,
        out_specs=VMEM,
        out_shape=jax.ShapeDtypeStruct((lax.axis_size(AXES), 8, k), F32),
        compiler_params=params(),
        cost_estimate=cost(2 * size * size * k, 2 * size * size),
    )(odd, low_one, part, one_b, v2, up, pair, moments)


def group_rows(genotypes, groups, group):
    rows = genotypes.shape[0] // groups
    return genotypes[pl.ds(pl.multiple_of(group * rows, rows), rows)]


def send_kernel(groups, row, pieces, penalty, v0, v1, v2, genotypes, factors, send, keep):
    sums = pieces[0]
    for piece in range(1, pieces.shape[0]):
        sums = sums + pieces[piece]
    moments = [sums[m : m + 1] for m in range(6)]
    c0, c1, c2 = coefficients(moments, penalty[...])
    value = c0 * v0[...] + c1 * v1[...] + c2 * v2[...]
    for place, factor in enumerate((c0, c1, c2)):
        factors[place : place + 1] = factor
    factors[3:8] = jnp.zeros_like(factors[3:8])
    narrow = value.astype(BF16)
    mine = row[0] % 2
    for g in range(groups // 2):
        send[g] = jnp.dot(group_rows(genotypes, groups, 2 * g + 1 - mine), narrow, preferred_element_type=F32)
        keep[g] = jnp.dot(group_rows(genotypes, groups, 2 * g + mine), narrow, preferred_element_type=F32)


def partial_scores(row, groups, pieces, penalty, v0, v1, v2, genotypes):
    people, size = genotypes.shape
    k = v0.shape[1]
    half = jax.ShapeDtypeStruct((groups // 2, people // groups, k), F32)
    return pl.pallas_call(
        functools.partial(send_kernel, groups),
        in_specs=[SMEM] + [VMEM] * 6,
        out_specs=[VMEM] * 3,
        out_shape=[jax.ShapeDtypeStruct((8, k), F32), half, half],
        compiler_params=params(),
        cost_estimate=cost(2 * people * size * k, 2 * people * size),
    )(row, pieces, penalty, v0, v1, v2, genotypes)


def effects_kernel(factors, v0, v1, v2, after, effects):
    effects[...] = factors[0:1] * v0[...] + factors[1:2] * v1[...] + factors[2:3] * v2[...]


def combined(factors, v0, v1, v2, after):
    return pl.pallas_call(
        effects_kernel,
        in_specs=[VMEM] * 4 + [ANY],
        out_specs=VMEM,
        out_shape=jax.ShapeDtypeStruct(v0.shape, F32),
        compiler_params=params(),
        cost_estimate=cost(5 * v0.size, 16 * v0.size),
    )(factors, v0, v1, v2, after)


def pick_kernel(index, keep, received, mine, other):
    mine[...] = keep[index[0]] + received[index[0]]
    other[...] = keep[1 - index[0]] + received[1 - index[0]]


def pick(index, keep, received):
    half = jax.ShapeDtypeStruct(keep.shape[1:], F32)
    return pl.pallas_call(
        pick_kernel,
        in_specs=[SMEM, VMEM, VMEM],
        out_specs=[VMEM] * 2,
        out_shape=[half] * 2,
        compiler_params=params(),
        cost_estimate=cost(keep.size, 12 * keep.size),
    )(index, keep, received)


def scattered_over(values, axis):
    n = lax.axis_size(axis)
    pieces = values.reshape((n, values.shape[0] // n) + values.shape[1:])
    return jnp.sum(lax.all_to_all(pieces, axis, 0, 0, tiled=True), axis=0)


def routed(block, pairs):
    return lax.ppermute(block, AXES, pairs)


def coefficients(moments, penalty):
    def inner(u, v):
        return sum(a * b * moments[i + j] for i, a in enumerate(u) for j, b in enumerate(v))

    n0 = moments[0]
    a0 = n0 / (moments[1] + penalty * n0)
    r1 = [1.0 - a0 * penalty, -a0]
    n1 = inner(r1, r1)
    b0 = n1 / n0
    d1 = [r1[0] + b0, r1[1]]
    ad1 = [penalty * d1[0], d1[0] + penalty * d1[1], d1[1]]
    a1 = n1 / inner(d1, ad1)
    e1 = [a0 + a1 * d1[0], a1 * d1[1]]
    r2 = [r1[0] - a1 * ad1[0], r1[1] - a1 * ad1[1], -a1 * ad1[2]]
    n2 = inner(r2, r2)
    b1 = n2 / n1
    d2 = [r2[0] + b1 * d1[0], r2[1] + b1 * d1[1], r2[2]]
    ad2 = [penalty * d2[0], d2[0] + penalty * d2[1], d2[1] + penalty * d2[2], d2[2]]
    a2 = n2 / inner(d2, ad2)
    return e1[0] + a2 * d2[0], e1[1] + a2 * d2[1], a2 * d2[2]


def swapped(block, bit):
    return routed(block, [(i, i ^ bit) for i in range(lax.axis_size(AXES))])


def body(marginal, penalty, ld_diag, ld_low, band, genotypes):
    n = lax.axis_size(AXES)
    rows, cols = lax.axis_size("row"), lax.axis_size("col")
    position = lax.axis_index(AXES)
    row = lax.axis_index("row")
    site = position.astype(jnp.int32)[None]
    odd = (position % 2).astype(jnp.int32)[None]
    half = marginal.shape[0] // 2

    def halos(vec, two, first, second):
        one_a, one_b = first()
        pair_a, pair_b = swapped(one_a, 1), swapped(one_b, 1)
        far_a, far_b = second(one_b)
        sum_a = relay(odd, far_a, pair_a, far_b)
        up_a = shifted(sum_a, -2)
        [chosen] = choose(odd, vec, two, sum_a, 1)
        one = swapped(chosen, 1)
        sum_b = relay(odd, far_b, pair_b, chosen)
        return sum_b, (one, up_a, shifted(sum_b, -2), pair_a, pair_b)

    v0 = marginal
    two = shifted(v0, 2)

    lows = []

    def second_tile(after):
        vec, _ = lax.optimization_barrier((v0, after))
        *products, low_one, low_two = from_tiles(second_kernel, 2, 2, 46, band, site, vec, ld_low[0])
        lows.extend((low_one, low_two))
        return products

    last_sum, arrived = halos(
        v0, two, lambda: from_tiles(first_kernel, 1, 0, 58, band, site, v0, ld_low[0]), second_tile
    )
    low_one, low_two = lows
    diag, own = first_diag(v0, ld_diag[0], last_sum)
    [v1] = finish(odd, 0, add_two(own, low_two, two), low_one, *arrived)

    two = shifted(v1, 2)
    products = coupling(v1, low_one, low_two)
    last_sum, arrived = halos(v1, two, lambda: products[:2], lambda after: products[2:])
    own = diag_times(v1, diag, last_sum)
    v2, upper = finish(odd, 1, add_two(own, low_two, two), low_one, *arrived)

    two = shifted(upper, 2)
    one, far = lower_coupling(v2, low_one, low_two)
    pair = swapped(one, 1)
    above = relay(odd, far, pair, far)
    up = shifted(above, -2)
    chosen_a, chosen_b = choose(odd, upper, two, above, 2)
    moments = own_moments(v0, v1, v2, diag, chosen_b)
    one_a, one_b = swapped(chosen_a, 1), swapped(chosen_b, 1)
    part = most(low_one, low_two, one_a, two)
    moments = last(odd, low_one, part, one_b, v2, up, pair, moments)
    pieces = lax.all_to_all(moments, AXES, 0, 0, tiled=True)

    factors, send, keep = partial_scores(row.astype(jnp.int32)[None], rows, pieces, penalty[None], v0, v1, v2, genotypes)
    received = swapped(send, cols)
    bit = rows // 4
    while bit:
        mine = (row // (2 * bit)) % 2
        keep = keep.reshape((2, -1) + keep.shape[1:])
        received = received.reshape((2, -1) + received.shape[1:])

        keep, send = pick(mine.astype(jnp.int32)[None], keep, received)
        received = swapped(send, 2 * bit * cols)
        bit //= 2
    effects = combined(factors, v0, v1, v2, send)
    keep, effects = lax.optimization_barrier((keep, effects))
    return effects, scattered_over((keep + received)[0], "col")


def solution(mesh):
    placed = (
        P(AXES, None),
        P(),
        P(AXES, None, None),
        P(AXES, None, None, None),
        P(AXES),
        P(None, AXES),
    )
    return jax.shard_map(
        body,
        mesh=mesh,
        in_specs=placed,
        out_specs=(P(AXES, None), P(AXES, None)),
        check_vma=False,
    )
```

```python
import functools

import jax
import jax.numpy as jnp
from jax import lax
from jax.experimental import pallas as pl
from jax.experimental.pallas import tpu as pltpu
from jax.sharding import PartitionSpec as P

AXES = ("row", "col")
F32 = jnp.float32
BF16 = jnp.bfloat16
MIB = 1024 * 1024
VMEM = pl.BlockSpec(memory_space=pltpu.VMEM)
SMEM = pl.BlockSpec(memory_space=pltpu.SMEM)
ANY = pl.BlockSpec(memory_space=pl.ANY)


def params(mib=20):
    return pltpu.CompilerParams(vmem_limit_bytes=mib * MIB)


def cost(flops, num_bytes):
    return pl.CostEstimate(flops=int(flops), bytes_accessed=int(num_bytes), transcendentals=0)


def shifted(block, distance):
    n = lax.axis_size(AXES)
    route = [(i - distance, i) for i in range(n) if 0 <= i - distance < n]
    return lax.ppermute(block, AXES, route)


def active(d, band, position):
    return jnp.logical_and(band[0] >= d + 1, position[0] >= d + 1)


def split_store(value, first, second):
    half = first.shape[0]
    first[...] = value[:half]
    second[...] = value[half:]


GROUP = 4


def fetched(low, tiles, arrived, order):
    count, rows = tiles.shape[0] // len(order), tiles.shape[1]
    copies = []
    for place in range(tiles.shape[0]):
        source = low.at[order[place // count], pl.ds(place % count * rows, rows)]
        copies.append(pltpu.make_async_copy(source, tiles.at[place], arrived.at[place]))
        copies[-1].start()
    return copies


def rounded_rows(copies, tiles, place, alive):
    for copy in copies[place : place + GROUP]:
        copy.wait()
    tile = tiles[place : place + GROUP].reshape(GROUP * tiles.shape[1], tiles.shape[2])
    return jnp.where(alive, tile, 0.0).astype(BF16)


def first_kernel(band, position, vec, low, one_a, one_b, own, tiles, arrived):
    fetch = pltpu.make_async_copy(vec, own, arrived.at[tiles.shape[0]])
    fetch.start()
    copies = fetched(low, tiles, arrived, (0,))
    fetch.wait()
    across = own[...].T.astype(BF16)
    rows = GROUP * tiles.shape[1]
    acc = None
    for place in range(0, tiles.shape[0], GROUP):
        tile = rounded_rows(copies, tiles, place, active(0, band, position))
        start = place * tiles.shape[1]
        term = jnp.dot(across[:, start : start + rows], tile, preferred_element_type=F32)
        acc = term if acc is None else acc + term
    split_store(acc.T, one_a, one_b)


def second_kernel(band, position, vec, low, far_a, far_b, low_one, low_two, own, tiles, arrived):
    fetch = pltpu.make_async_copy(vec, own, arrived.at[tiles.shape[0]])
    fetch.start()
    copies = fetched(low, tiles, arrived, (1, 0))
    fetch.wait()
    across = own[...].T.astype(BF16)
    rows = GROUP * tiles.shape[1]
    count = tiles.shape[0] // 2
    acc = None
    for place in range(0, count, GROUP):
        tile = rounded_rows(copies, tiles, place, active(1, band, position))
        start = place * tiles.shape[1]
        low_two[start : start + rows] = tile
        term = jnp.dot(across[:, start : start + rows], tile, preferred_element_type=F32)
        acc = term if acc is None else acc + term
    split_store(acc.T, far_a, far_b)
    for place in range(0, count, GROUP):
        start = place * tiles.shape[1]
        low_one[start : start + rows] = rounded_rows(copies, tiles, count + place, active(0, band, position))


def from_tiles(kernel, tiles, narrow, mib, band, position, vec, low):
    size, k = vec.shape
    count = 16
    return pl.pallas_call(
        kernel,
        in_specs=[SMEM] * 2 + [pl.BlockSpec(memory_space=pltpu.HBM)] * 2,
        out_specs=[VMEM] * (2 + narrow),
        out_shape=[jax.ShapeDtypeStruct((size // 2, k), F32)] * 2 + [jax.ShapeDtypeStruct((size, size), BF16)] * narrow,
        scratch_shapes=[
            pltpu.VMEM((size, k), F32),
            pltpu.VMEM((tiles * count, size // count, size), F32),
            pltpu.SemaphoreType.DMA((tiles * count + 1,)),
        ],
        compiler_params=params(mib),
        cost_estimate=cost(2 * size * size * k, 4 * tiles * size * size),
    )(band, position, vec, low)


def coupling_kernel(vec, low_one, low_two, one_a, one_b, far_a, far_b):
    across = vec[...].T.astype(BF16)
    split_store(jnp.dot(across, low_one[...], preferred_element_type=F32).T, one_a, one_b)
    split_store(jnp.dot(across, low_two[...], preferred_element_type=F32).T, far_a, far_b)


def coupling(vec, low_one, low_two):
    size, k = vec.shape
    return pl.pallas_call(
        coupling_kernel,
        in_specs=[VMEM] * 3,
        out_specs=[VMEM] * 4,
        out_shape=[jax.ShapeDtypeStruct((size // 2, k), F32)] * 4,
        compiler_params=params(),
        cost_estimate=cost(4 * size * size * k, 4 * size * size),
    )(vec, low_one, low_two)


def relay_kernel(odd, far, pair, after, out):
    out[...] = far[...] + jnp.where(odd[0] > 0, pair[...], 0.0)


def choose_kernel(odd, vec, two, after, *parts):
    rows = parts[0].shape[0]
    for place, part in enumerate(parts):
        here = slice(place * rows, (place + 1) * rows)
        part[...] = jnp.where(odd[0] > 0, two[here], vec[here])


def choose(odd, vec, two, after, parts):
    rows, k = vec.shape
    return pl.pallas_call(
        choose_kernel,
        in_specs=[SMEM, VMEM, VMEM, ANY],
        out_specs=[VMEM] * parts,
        out_shape=[jax.ShapeDtypeStruct((rows // parts, k), F32)] * parts,
        compiler_params=params(),
        cost_estimate=cost(vec.size, 12 * vec.size),
    )(odd, vec, two, after)


def relay(odd, far, pair, after):
    return pl.pallas_call(
        relay_kernel,
        in_specs=[SMEM, VMEM, VMEM, ANY],
        out_specs=VMEM,
        out_shape=jax.ShapeDtypeStruct(far.shape, F32),
        compiler_params=params(),
        cost_estimate=cost(far.size, 12 * far.size),
    )(odd, far, pair, after)


def first_diag_kernel(vec, diag, after, narrow, product):
    tile = diag[...].astype(BF16)
    rest = (diag[...] - tile.astype(F32)).astype(BF16)
    narrow[...] = tile
    value = vec[...]
    high = value.astype(BF16)
    low = (value - high.astype(F32)).astype(BF16)
    both = jnp.dot(tile, jnp.concatenate([high, low], axis=1), preferred_element_type=F32)
    k = value.shape[1]
    product[...] = both[:, :k] + both[:, k:] + jnp.dot(rest, high, preferred_element_type=F32)


def first_diag(vec, diag, after):
    size, k = vec.shape
    rows = size // 4
    return pl.pallas_call(
        first_diag_kernel,
        grid=(4,),
        in_specs=[pl.BlockSpec((size, k), lambda r: (0, 0)), pl.BlockSpec((rows, size), lambda r: (r, 0)), ANY],
        out_specs=[pl.BlockSpec((rows, size), lambda r: (r, 0)), pl.BlockSpec((rows, k), lambda r: (r, 0))],
        out_shape=[jax.ShapeDtypeStruct(diag.shape, BF16), jax.ShapeDtypeStruct(vec.shape, F32)],
        compiler_params=params(),
        cost_estimate=cost(2 * size * size * k, 6 * size * size),
    )(vec, diag, after)


def diag_kernel(vec, diag, after, product):
    product[...] = jnp.dot(diag[...], vec[...].astype(BF16), preferred_element_type=F32)


def diag_times(vec, diag, after):
    size, k = vec.shape
    return pl.pallas_call(
        diag_kernel,
        in_specs=[VMEM, VMEM, ANY],
        out_specs=VMEM,
        out_shape=jax.ShapeDtypeStruct(vec.shape, F32),
        compiler_params=params(),
        cost_estimate=cost(2 * size * size * k, 6 * size * size),
    )(vec, diag, after)


def finish_kernel(odd, part, ahead_a, ahead_b, pair_a, pair_b, out, *upper):
    half = ahead_a.shape[0]
    for place, (straight, pair) in enumerate(((ahead_a, pair_a), (ahead_b, pair_b))):
        rows = slice(place * half, (place + 1) * half)
        out[rows] = part[rows] + straight[...] + jnp.where(odd[0] > 0, 0.0, pair[...])
    for copy in upper:
        copy[...] = out[:half]


def finish(odd, uppers, part, *arrived):
    size, k = part.shape
    return pl.pallas_call(
        finish_kernel,
        in_specs=[SMEM] + [VMEM] * 5,
        out_specs=[VMEM] * (1 + uppers),
        out_shape=[jax.ShapeDtypeStruct(part.shape, F32)] + [jax.ShapeDtypeStruct((size // 2, k), F32)] * uppers,
        compiler_params=params(),
        cost_estimate=cost(4 * size * k, 16 * size * k),
    )(odd, part, *arrived)


def two_kernel(own, low, two, product):
    product[...] = own[...] + jnp.dot(low[...], two[...].astype(BF16), preferred_element_type=F32)


def add_two(own, low, two):
    size, k = two.shape
    return pl.pallas_call(
        two_kernel,
        in_specs=[VMEM] * 3,
        out_specs=VMEM,
        out_shape=jax.ShapeDtypeStruct(two.shape, F32),
        compiler_params=params(),
        cost_estimate=cost(2 * size * size * k, 2 * size * size),
    )(own, low, two)


def lower_kernel(vec, low_one, low_two, one, far):
    across = vec[...].T.astype(BF16)
    half = one.shape[0]
    one[...] = jnp.dot(across, low_one[:, half:], preferred_element_type=F32).T
    far[...] = jnp.dot(across, low_two[:, half:], preferred_element_type=F32).T


def lower_coupling(vec, low_one, low_two):
    size, k = vec.shape
    return pl.pallas_call(
        lower_kernel,
        in_specs=[VMEM] * 3,
        out_specs=[VMEM] * 2,
        out_shape=[jax.ShapeDtypeStruct((size // 2, k), F32)] * 2,
        compiler_params=params(),
        cost_estimate=cost(2 * size * size * k, 2 * size * size),
    )(vec, low_one, low_two)


def own_kernel(v0, v1, v2, diag, after, moments):
    image = jnp.dot(diag[...], v2[...].astype(BF16), preferred_element_type=F32)
    pairs = [(v0, v0), (v0, v1), (v1, v1), (v1, v2), (v2, v2)]
    for row, (a, b) in enumerate(pairs):
        moments[row : row + 1] = jnp.sum(a[...] * b[...], axis=0, keepdims=True)
    moments[5:6] = jnp.sum(v2[...] * image, axis=0, keepdims=True)
    moments[6:8] = jnp.zeros_like(moments[6:8])


def own_moments(v0, v1, v2, diag, after):
    size, k = v0.shape
    return pl.pallas_call(
        own_kernel,
        in_specs=[VMEM] * 4 + [ANY],
        out_specs=VMEM,
        out_shape=jax.ShapeDtypeStruct((8, k), F32),
        compiler_params=params(),
        cost_estimate=cost(2 * size * size * k, 6 * size * size),
    )(v0, v1, v2, diag, after)


def most_kernel(low_one, low_two, one_a, two, below):
    quarter, half = one_a.shape[0], two.shape[0]
    value = jnp.dot(low_two[:, :half], two[...].astype(BF16), preferred_element_type=F32)
    below[...] = value + jnp.dot(low_one[:, :quarter], one_a[...].astype(BF16), preferred_element_type=F32)


def most(low_one, low_two, one_a, two):
    size, k = low_one.shape[0], two.shape[1]
    return pl.pallas_call(
        most_kernel,
        in_specs=[VMEM] * 4,
        out_specs=VMEM,
        out_shape=jax.ShapeDtypeStruct((size, k), F32),
        compiler_params=params(),
        cost_estimate=cost(2 * size * size * k, 2 * size * size),
    )(low_one, low_two, one_a, two)


def last_kernel(odd, low_one, part, one_b, v2, up, pair, moments, out):
    quarter = one_b.shape[0]
    half = 2 * quarter
    below = part[...] + jnp.dot(low_one[:, quarter:half], one_b[...].astype(BF16), preferred_element_type=F32)
    above = up[...] + jnp.where(odd[0] > 0, 0.0, pair[...])
    coupled = jnp.sum(v2[...] * below, axis=0, keepdims=True) + jnp.sum(v2[half:] * above, axis=0, keepdims=True)
    whole = moments[...]
    row = lax.broadcasted_iota(jnp.int32, whole.shape, 0)
    whole = jnp.where(row == 5, whole + 2.0 * coupled, whole)
    for place in range(out.shape[0]):
        out[place] = whole


def last(odd, low_one, part, one_b, v2, up, pair, moments):
    size, k = v2.shape
    return pl.pallas_call(
        last_kernel,
        in_specs=[SMEM] + [VMEM] * 7,
        out_specs=VMEM,
        out_shape=jax.ShapeDtypeStruct((lax.axis_size(AXES), 8, k), F32),
        compiler_params=params(),
        cost_estimate=cost(2 * size * size * k, 2 * size * size),
    )(odd, low_one, part, one_b, v2, up, pair, moments)


def group_rows(genotypes, groups, group):
    rows = genotypes.shape[0] // groups
    return genotypes[pl.ds(pl.multiple_of(group * rows, rows), rows)]


def send_kernel(groups, row, pieces, penalty, v0, v1, v2, genotypes, factors, send, keep):
    sums = pieces[0]
    for piece in range(1, pieces.shape[0]):
        sums = sums + pieces[piece]
    moments = [sums[m : m + 1] for m in range(6)]
    c0, c1, c2 = coefficients(moments, penalty[...])
    value = c0 * v0[...] + c1 * v1[...] + c2 * v2[...]
    for place, factor in enumerate((c0, c1, c2)):
        factors[place : place + 1] = factor
    factors[3:8] = jnp.zeros_like(factors[3:8])
    narrow = value.astype(BF16)
    mine = row[0] % 2
    for g in range(groups // 2):
        send[g] = jnp.dot(group_rows(genotypes, groups, 2 * g + 1 - mine), narrow, preferred_element_type=F32)
        keep[g] = jnp.dot(group_rows(genotypes, groups, 2 * g + mine), narrow, preferred_element_type=F32)


def partial_scores(row, groups, pieces, penalty, v0, v1, v2, genotypes):
    people, size = genotypes.shape
    k = v0.shape[1]
    half = jax.ShapeDtypeStruct((groups // 2, people // groups, k), F32)
    return pl.pallas_call(
        functools.partial(send_kernel, groups),
        in_specs=[SMEM] + [VMEM] * 6,
        out_specs=[VMEM] * 3,
        out_shape=[jax.ShapeDtypeStruct((8, k), F32), half, half],
        compiler_params=params(),
        cost_estimate=cost(2 * people * size * k, 2 * people * size),
    )(row, pieces, penalty, v0, v1, v2, genotypes)


def effects_kernel(factors, v0, v1, v2, after, effects):
    effects[...] = factors[0:1] * v0[...] + factors[1:2] * v1[...] + factors[2:3] * v2[...]


def combined(factors, v0, v1, v2, after):
    return pl.pallas_call(
        effects_kernel,
        in_specs=[VMEM] * 4 + [ANY],
        out_specs=VMEM,
        out_shape=jax.ShapeDtypeStruct(v0.shape, F32),
        compiler_params=params(),
        cost_estimate=cost(5 * v0.size, 16 * v0.size),
    )(factors, v0, v1, v2, after)


def pick_kernel(index, keep, received, mine, other):
    mine[...] = keep[index[0]] + received[index[0]]
    other[...] = keep[1 - index[0]] + received[1 - index[0]]


def pick(index, keep, received):
    half = jax.ShapeDtypeStruct(keep.shape[1:], F32)
    return pl.pallas_call(
        pick_kernel,
        in_specs=[SMEM, VMEM, VMEM],
        out_specs=[VMEM] * 2,
        out_shape=[half] * 2,
        compiler_params=params(),
        cost_estimate=cost(keep.size, 12 * keep.size),
    )(index, keep, received)


def scattered_over(values, axis):
    n = lax.axis_size(axis)
    pieces = values.reshape((n, values.shape[0] // n) + values.shape[1:])
    return jnp.sum(lax.all_to_all(pieces, axis, 0, 0, tiled=True), axis=0)


def routed(block, pairs):
    return lax.ppermute(block, AXES, pairs)


def coefficients(moments, penalty):
    def inner(u, v):
        return sum(a * b * moments[i + j] for i, a in enumerate(u) for j, b in enumerate(v))

    n0 = moments[0]
    a0 = n0 / (moments[1] + penalty * n0)
    r1 = [1.0 - a0 * penalty, -a0]
    n1 = inner(r1, r1)
    b0 = n1 / n0
    d1 = [r1[0] + b0, r1[1]]
    ad1 = [penalty * d1[0], d1[0] + penalty * d1[1], d1[1]]
    a1 = n1 / inner(d1, ad1)
    e1 = [a0 + a1 * d1[0], a1 * d1[1]]
    r2 = [r1[0] - a1 * ad1[0], r1[1] - a1 * ad1[1], -a1 * ad1[2]]
    n2 = inner(r2, r2)
    b1 = n2 / n1
    d2 = [r2[0] + b1 * d1[0], r2[1] + b1 * d1[1], r2[2]]
    ad2 = [penalty * d2[0], d2[0] + penalty * d2[1], d2[1] + penalty * d2[2], d2[2]]
    a2 = n2 / inner(d2, ad2)
    return e1[0] + a2 * d2[0], e1[1] + a2 * d2[1], a2 * d2[2]


def swapped(block, bit):
    return routed(block, [(i, i ^ bit) for i in range(lax.axis_size(AXES))])


def body(marginal, penalty, ld_diag, ld_low, band, genotypes):
    n = lax.axis_size(AXES)
    rows, cols = lax.axis_size("row"), lax.axis_size("col")
    position = lax.axis_index(AXES)
    row = lax.axis_index("row")
    site = position.astype(jnp.int32)[None]
    odd = (position % 2).astype(jnp.int32)[None]
    half = marginal.shape[0] // 2

    def halos(vec, two, first, second):
        one_a, one_b = first()
        pair_a, pair_b = swapped(one_a, 1), swapped(one_b, 1)
        far_a, far_b = second(one_b)
        sum_a = relay(odd, far_a, pair_a, far_b)
        up_a = shifted(sum_a, -2)
        [chosen] = choose(odd, vec, two, sum_a, 1)
        one = swapped(chosen, 1)
        sum_b = relay(odd, far_b, pair_b, chosen)
        return sum_b, (one, up_a, shifted(sum_b, -2), pair_a, pair_b)

    v0 = marginal
    two = shifted(v0, 2)

    lows = []

    def second_tile(after):
        vec, _ = lax.optimization_barrier((v0, after))
        *products, low_one, low_two = from_tiles(second_kernel, 2, 2, 46, band, site, vec, ld_low[0])
        lows.extend((low_one, low_two))
        return products

    last_sum, arrived = halos(
        v0, two, lambda: from_tiles(first_kernel, 1, 0, 58, band, site, v0, ld_low[0]), second_tile
    )
    low_one, low_two = lows
    diag, own = first_diag(v0, ld_diag[0], last_sum)
    [v1] = finish(odd, 0, add_two(add_two(own, low_two, two), low_one, arrived[0]), *arrived[1:])

    two = shifted(v1, 2)
    products = coupling(v1, low_one, low_two)
    last_sum, arrived = halos(v1, two, lambda: products[:2], lambda after: products[2:])
    own = diag_times(v1, diag, last_sum)
    v2, upper = finish(odd, 1, add_two(add_two(own, low_two, two), low_one, arrived[0]), *arrived[1:])

    two = shifted(upper, 2)
    one, far = lower_coupling(v2, low_one, low_two)
    pair = swapped(one, 1)
    above = relay(odd, far, pair, far)
    up = shifted(above, -2)
    chosen_a, chosen_b = choose(odd, upper, two, above, 2)
    moments = own_moments(v0, v1, v2, diag, chosen_b)
    one_a, one_b = swapped(chosen_a, 1), swapped(chosen_b, 1)
    part = most(low_one, low_two, one_a, two)
    moments = last(odd, low_one, part, one_b, v2, up, pair, moments)
    pieces = lax.all_to_all(moments, AXES, 0, 0, tiled=True)

    factors, send, keep = partial_scores(row.astype(jnp.int32)[None], rows, pieces, penalty[None], v0, v1, v2, genotypes)
    received = swapped(send, cols)
    bit = rows // 4
    while bit:
        mine = (row // (2 * bit)) % 2
        keep = keep.reshape((2, -1) + keep.shape[1:])
        received = received.reshape((2, -1) + received.shape[1:])

        keep, send = pick(mine.astype(jnp.int32)[None], keep, received)
        received = swapped(send, 2 * bit * cols)
        bit //= 2
    effects = combined(factors, v0, v1, v2, send)
    keep, effects = lax.optimization_barrier((keep, effects))
    return effects, scattered_over((keep + received)[0], "col")


def solution(mesh):
    placed = (
        P(AXES, None),
        P(),
        P(AXES, None, None),
        P(AXES, None, None, None),
        P(AXES),
        P(None, AXES),
    )
    return jax.shard_map(
        body,
        mesh=mesh,
        in_specs=placed,
        out_specs=(P(AXES, None), P(AXES, None)),
        check_vma=False,
    )
```
